32 devices in a mesh: seq: 8 (over y, x, core), tm: 4 (over z).
Axes of the slice: x: 2, y: 2, z: 4, core: 2. Of those that a mesh axis runs over, the one named last changes fastest.
Arguments:
- phonemes: bfloat16 [32768, 512], P('seq'), may hold values from -6 to 6
- send_order: int32 [8, 4096], P('seq'), may hold values from 0 to 4095, each once within a row
- phoneme_counts: int32 [8, 4], P('seq'), may hold values from 1 to 3584, as said below
- frame_lengths: int32 [8, 4], P('seq'), may hold values from 512 to 14336, as said below
- tile_offsets: int32 [1024], P(('seq', 'tm')), may hold values from 0 to 3968, as said below
- alignment: bfloat16 [131072, 128], P(('seq', 'tm')), may hold values from 0 to 0.19921875
- style_vec: bfloat16 [32, 128], P('seq'), may hold values from -6 to 6
- first_affine_weight: bfloat16 [128, 1024], replicated, may hold values from -0.25 to 0.25
- first_affine_bias: bfloat16 [1024], replicated, may hold values from -2 to 2
- first_conv_weight: bfloat16 [1536, 512], replicated, may hold values from -0.15625 to 0.15625
- second_affine_weight: bfloat16 [128, 1024], replicated, may hold values from -0.25 to 0.25
- second_affine_bias: bfloat16 [1024], replicated, may hold values from -2 to 2
- second_conv_weight: bfloat16 [1536, 512], replicated, may hold values from -0.15625 to 0.15625
- second_conv_bias: bfloat16 [512], replicated, may hold values from -2 to 2
- cotangent: bfloat16 [131072, 512], P(('seq', 'tm')), may hold values from -6 to 6
Outputs:
- frames_out: bfloat16 [131072, 512], P(('seq', 'tm'))
- phonemes_grad: float32 [32768, 512], P('seq')
- style_grad: float32 [32, 128], P('seq')
- first_affine_weight_grad: float32 [128, 1024], replicated
- first_affine_bias_grad: float32 [1024], replicated
- first_conv_weight_grad: float32 [1536, 512], replicated
- second_affine_weight_grad: float32 [128, 1024], replicated
- second_affine_bias_grad: float32 [1024], replicated
- second_conv_weight_grad: float32 [1536, 512], replicated
- second_conv_bias_grad: float32 [512], replicated
The draws below stay inside these ranges and needn't reach their ends.
Inputs may be any that keep to these rules, and one draw needn't show every extreme that they name: `frame_lengths`: utterances of a group in order; their sum is at most 16384, frames past it are padding; the second utterance of each group starts on the group's first 4096 frames and ends on its last 4096. `phoneme_counts`: each is a quarter of its utterance's frames, rounded down, or one less; a group's counts sum to at most 4096. `send_order`: each row is a permutation. `tile_offsets`: window start of a block within its group's 4096 slots; a block among frames t * 4096 to (t + 1) * 4096 - 1 of its group starts at slot max(0, t * 1024 - 128 / 2) or later and at slot min(3968, (t + 1) * 1024 - 128 / 2) or earlier, and both ends are taken in every group.
All inputs are finite; a program needn't handle non-finite values.
Results may differ from the reference program's by a relative error of at most 0.007.
Values may be sent and summed in bfloat16 or wider, within the bound.
No kernel may reach another device: no remote copies, remote signals or barrier semaphores. Data moves between devices by JAX's collectives and lax.ppermute only.
A program may use at most 256 MiB of HBM per device.

```python
import jax
import jax.numpy as jnp
from jax import lax

C = 512
S = 128
F_DEV = 4096
TILE = 128
KW = 128
GROUPS = 8
GROUP_FR = 16384
PH_G = 4096
FRAMES = 131072
PHON = 32768
STYLES = 32
TILES = 1024
N_TM = 4


def lengths_table(key):
    lead_group = jnp.arange(GROUPS) == 0
    opening = jax.random.randint(jax.random.fold_in(key, 11), (GROUPS,), F_DEV // 4, 3 * F_DEV // 4 + 1)
    tail_one = jax.random.randint(jax.random.fold_in(key, 12), (GROUPS,), F_DEV // 8, 3 * F_DEV // 8 + 1)
    tail_two = jax.random.randint(jax.random.fold_in(key, 13), (GROUPS,), F_DEV // 8, 3 * F_DEV // 8 + 1)
    padding = jax.random.randint(jax.random.fold_in(key, 14), (GROUPS,), 0, F_DEV // 8 + 1)
    opening = jnp.where(lead_group, F_DEV // 4, opening)
    tail_one = jnp.where(lead_group, F_DEV // 8, tail_one)
    tail_two = jnp.where(lead_group, F_DEV // 8, tail_two)
    padding = jnp.where(lead_group, 0, padding)
    longest = GROUP_FR - opening - tail_one - tail_two - padding
    return jnp.stack([opening, longest, tail_one, tail_two], axis=1).astype(jnp.int32)


def draw_frame_lengths(key, part):
    return lengths_table(key)


def draw_phoneme_counts(key, part):
    table = lengths_table(key)
    shortfall = jax.random.randint(jax.random.fold_in(key, 23), table.shape, 0, 2)
    lead_group = (jnp.arange(GROUPS) == 0)[:, None]
    shortfall = jnp.where(lead_group, 0, shortfall)
    return (table // 4 - shortfall).astype(jnp.int32)


def draw_tile_offsets(key, part):
    tiles_group = GROUP_FR // TILE
    tiles_shard = F_DEV // TILE
    shard_count = GROUP_FR // F_DEV
    shard_slots = PH_G // shard_count
    tile_pos = jnp.arange(TILES, dtype=jnp.int32) % tiles_group
    shard = tile_pos // tiles_shard
    within = tile_pos % tiles_shard
    jitter = jax.random.randint(jax.random.fold_in(key, 31), (TILES,), -(KW // 8), KW // 8 + 1)
    drawn = tile_pos * TILE * PH_G // GROUP_FR - KW // 4 + jitter
    lowest = shard * shard_slots - KW // 2
    highest = (shard + 1) * shard_slots - KW // 2
    drawn = jnp.clip(drawn, lowest, highest)
    drawn = jnp.where(within == 0, lowest, drawn)
    drawn = jnp.where(within == tiles_shard - 1, highest, drawn)
    return jnp.clip(drawn, 0, PH_G - KW).astype(jnp.int32)


def block_scale(key, extent, split, low, high):
    factor_of, own = 1.0, jax.random.fold_in(key, 6)
    for dim, blocks in split:
        steps = jnp.exp(jax.random.uniform(jax.random.fold_in(own, dim), (blocks,), jnp.float32, low / len(split), high / len(split)))
        factor_of = factor_of * jnp.repeat(steps, extent[dim] // blocks).reshape([-1 if axis == dim else 1 for axis in range(len(extent))])
    return factor_of


def bell_draw(own_key, shape, deviation, bound, pieces=(), kind=jnp.bfloat16):
    entries = deviation * jax.random.normal(own_key, shape, jnp.float32)
    if pieces:
        entries = entries * block_scale(own_key, shape, pieces, -0.22, 0.18)
    return jnp.clip(entries, -bound, bound).astype(kind)


def setup_inputs(seed: int = 0) -> dict:
    splits = jax.random.split(jax.random.key(seed), 16)
    return {
        "phonemes": bell_draw(splits[0], (PHON, C), 1.0, 6.0, ((0, 8),)),
        "send_order": jax.vmap(lambda own: jax.random.permutation(own, PH_G))(jax.random.split(splits[1], GROUPS)).reshape((GROUPS, PH_G)).astype(jnp.int32),
        "phoneme_counts": draw_phoneme_counts(jax.random.fold_in(splits[15], 71), 0),
        "frame_lengths": draw_frame_lengths(jax.random.fold_in(splits[15], 71), 0),
        "tile_offsets": draw_tile_offsets(jax.random.fold_in(splits[15], 71), 0),
        "alignment": jnp.clip(0.19921875 * jax.random.uniform(splits[5], (FRAMES, KW), jnp.float32) ** block_scale(splits[5], (FRAMES, KW), ((0, 32),), -0.2, 0.2), 0.0, 0.19921875).astype(jnp.bfloat16),
        "style_vec": bell_draw(splits[6], (STYLES, S), 1.0, 6.0, ((0, 8),)),
        "first_affine_weight": bell_draw(splits[7], (S, 2 * C), (4 * S) ** -0.5, 0.25),
        "first_affine_bias": bell_draw(splits[8], (2 * C,), 0.3, 2.0),
        "first_conv_weight": bell_draw(splits[9], (3 * C, C), (3 * C) ** -0.5, 0.15625),
        "second_affine_weight": bell_draw(splits[10], (S, 2 * C), (4 * S) ** -0.5, 0.25),
        "second_affine_bias": bell_draw(splits[11], (2 * C,), 0.3, 2.0),
        "second_conv_weight": bell_draw(splits[12], (3 * C, C), (3 * C) ** -0.5, 0.15625),
        "second_conv_bias": bell_draw(splits[13], (C,), 0.3, 2.0),
        "cotangent": bell_draw(splits[14], (FRAMES, C), 1.0, 6.0, ((0, 32),)),
    }


@jax.custom_vjp
def low(v):
    return lax.optimization_barrier(v.astype(jnp.bfloat16)).astype(jnp.float32)

@jax.custom_vjp
def low_back(v):
    return v

def low_keep(v):
    return (low(v), None)

def low_pass(kept, grad):
    return (grad,)

def back_keep(v):
    return (v, None)

def back_low(kept, grad):
    return (low(grad),)
low.defvjp(low_keep, low_pass)
low_back.defvjp(back_keep, back_low)
PRECISE = lax.Precision.HIGHEST
EPSILON = 1e-05
ROOT_HALF = 0.7071067811865476

def smooth_act(values):
    return values * jax.nn.sigmoid(values)

def owner_of(lengths, positions):
    ends_at = jnp.cumsum(lengths).astype(jnp.int32)
    starts = (ends_at - lengths).astype(jnp.int32)
    inside = (positions[:, None] >= starts[None, :]) & (positions[:, None] < ends_at[None, :])
    labels = jnp.arange(1, lengths.shape[0] + 1, dtype=jnp.int32)
    return lax.optimization_barrier(jnp.sum(jnp.where(inside, labels[None, :], 0), axis=1)).astype(jnp.int32)

def adaptive_norm(values, member, inv_count, style_rows, affine_weight, affine_bias):
    totals = jnp.dot(member.T, values, precision=PRECISE)
    square = jnp.dot(member.T, values * values, precision=PRECISE)
    average = totals * inv_count[:, None]
    inv_std = lax.rsqrt(square * inv_count[:, None] - average * average + EPSILON)
    params = jnp.dot(style_rows, affine_weight, precision=PRECISE) + affine_bias
    channels = values.shape[1]
    scale_rows = jnp.dot(member, 1.0 + params[:, :channels], precision=PRECISE)
    shift_rows = jnp.dot(member, params[:, channels:], precision=PRECISE)
    normed = (values - jnp.dot(member, average, precision=PRECISE)) * jnp.dot(member, inv_std, precision=PRECISE)
    return scale_rows * normed + shift_rows

def convolve(values, weight, left_mask, right_mask, valid_rows):
    zero_row = jnp.zeros_like(values[:1])
    before = jnp.concatenate([zero_row, values[:-1]], axis=0) * left_mask[:, None]
    after = jnp.concatenate([values[1:], zero_row], axis=0) * right_mask[:, None]
    stacked = jnp.concatenate([before, values, after], axis=1)
    return valid_rows[:, None] * jnp.dot(stacked, weight, precision=PRECISE)

def group_layer(group_pack, weights):
    buffer, aligned, offsets, lengths, counts, style_rows = group_pack
    first_affine_weight, first_affine_bias, first_conv_weight, second_affine_weight, second_affine_bias, second_conv_weight, second_conv_bias = weights
    frame_total = aligned.shape[0]
    window = aligned.shape[1]
    positions = jnp.arange(frame_total, dtype=jnp.int32)
    labels = jnp.arange(1, lengths.shape[0] + 1, dtype=jnp.int32)
    frame_owner = owner_of(lengths, positions)
    member = (frame_owner[:, None] == labels[None, :]).astype(jnp.float32)
    valid_rows = (frame_owner > 0).astype(jnp.float32)
    left_mask = ((owner_of(lengths, positions - 1) == frame_owner) & (frame_owner > 0)).astype(jnp.float32)
    right_mask = ((owner_of(lengths, positions + 1) == frame_owner) & (frame_owner > 0)).astype(jnp.float32)
    inv_count = 1.0 / lengths.astype(jnp.float32)
    slot_owner = owner_of(counts, jnp.arange(buffer.shape[0], dtype=jnp.int32))
    tile_count = offsets.shape[0]
    tile_rows = frame_total // tile_count
    window_rows = (offsets[:, None] + jnp.arange(window, dtype=jnp.int32)[None, :]).astype(jnp.int32)
    gathered = jnp.take(buffer, window_rows, axis=0)
    tile_owner = frame_owner.reshape(tile_count, tile_rows)
    matches = (tile_owner[:, :, None] == jnp.take(slot_owner, window_rows, axis=0)[:, None, :]) & (tile_owner[:, :, None] > 0)
    masked = jnp.where(matches, aligned.reshape(tile_count, tile_rows, window), 0.0)
    upsampled = jnp.einsum('tfw,twc->tfc', masked, gathered, precision=PRECISE).reshape(frame_total, -1)
    upsampled = low_back(upsampled)
    act_one = low(smooth_act(adaptive_norm(upsampled, member, inv_count, style_rows, first_affine_weight, first_affine_bias)))
    middle = low_back(convolve(act_one, first_conv_weight, left_mask, right_mask, valid_rows))
    act_two = low(smooth_act(adaptive_norm(middle, member, inv_count, style_rows, second_affine_weight, second_affine_bias)))
    branch = low_back(convolve(act_two, second_conv_weight, left_mask, right_mask, valid_rows) + valid_rows[:, None] * second_conv_bias)
    return low(valid_rows[:, None] * (upsampled + branch) * ROOT_HALF)

def reference(phonemes, send_order, phoneme_counts, frame_lengths, tile_offsets, alignment, style_vec, first_affine_weight, first_affine_bias, first_conv_weight, second_affine_weight, second_affine_bias, second_conv_weight, second_conv_bias, cotangent):
    groups = send_order.shape[0]
    slot_count = send_order.shape[1]
    shards = N_TM
    piece_rows = slot_count // (groups * shards)
    channels = phonemes.shape[1]
    source = jnp.arange(groups, dtype=jnp.int32)[:, None, None, None] * slot_count
    routes = (send_order.astype(jnp.int32).reshape(groups, groups, shards, piece_rows) + source).transpose(1, 2, 0, 3).reshape(groups, slot_count).astype(jnp.int32)
    aligned = alignment.astype(jnp.float32).reshape(groups, -1, alignment.shape[1])
    offsets = tile_offsets.astype(jnp.int32).reshape(groups, -1)
    lengths_all = frame_lengths.astype(jnp.int32)
    counts_all = phoneme_counts.astype(jnp.int32)

    def forward(phoneme_rows, style_rows, fa_weight, fa_bias, fc_weight, sa_weight, sa_bias, sc_weight, sc_bias):
        weights = (fa_weight, fa_bias, fc_weight, sa_weight, sa_bias, sc_weight, sc_bias)
        buffers = jnp.take(phoneme_rows, routes, axis=0)
        styles = style_rows.reshape(groups, -1, style_rows.shape[1])
        layer = jax.checkpoint(lambda group_pack: group_layer(group_pack, weights))
        result = lax.map(layer, (buffers, aligned, offsets, lengths_all, counts_all, styles))
        return result.reshape(-1, channels)
    frames_out, pull = jax.vjp(forward, phonemes.astype(jnp.float32), style_vec.astype(jnp.float32), first_affine_weight.astype(jnp.float32), first_affine_bias.astype(jnp.float32), first_conv_weight.astype(jnp.float32), second_affine_weight.astype(jnp.float32), second_affine_bias.astype(jnp.float32), second_conv_weight.astype(jnp.float32), second_conv_bias.astype(jnp.float32))
    phon_g, style_g, faw_g, fab_g, fcw_g, saw_g, sab_g, scw_g, scb_g = pull(cotangent.astype(jnp.float32))
    return (frames_out.astype(jnp.bfloat16), phon_g, style_g, faw_g, fab_g, fcw_g, saw_g, sab_g, scw_g, scb_g)
```

```python
import functools

import jax
import jax.numpy as jnp
from jax import lax
from jax.experimental import pallas as pl
from jax.experimental.pallas import tpu as pltpu
from jax.sharding import PartitionSpec as P

EPSILON = 1e-05
ROOT_HALF = 0.7071067811865476
PRECISE = lax.Precision.HIGHEST
F32, BF16, I32 = jnp.float32, jnp.bfloat16, jnp.int32
UTTS = 4
PAD = 16
ROWS = 512
WIDE = 256
MIB = 2**20

STAT_ROWS = 24
FIRST_ROW, LAST_ROW, EXTRA_ROW = 16, 17, 18


def owner_at(ends, position):
    return sum((position >= end).astype(I32) for end in ends)


def rows_of(start, shape):
    return start + lax.broadcasted_iota(I32, shape, 0)


def fold_rows(values):
    return jnp.sum(values.reshape(values.shape[0] // 8, 8, values.shape[1]), axis=0)


def by_utterance(ends, start, count, uniform_body, mixed_body):
    low, high = owner_at(ends, start), owner_at(ends, start + count - 1)

    @pl.when(low == high)
    def _():
        uniform_body(low)

    @pl.when(low != high)
    def _():
        def step(u, carry):
            lower = jnp.int32(-1)
            upper = jnp.int32(2**30)
            for k in range(UTTS):
                lower = jnp.where(u == k + 1, ends[k], lower)
                upper = jnp.where(u == k, ends[k], upper)

            def mask(shape):
                rows = rows_of(start, shape)
                return (rows >= lower) & (rows < upper)

            mixed_body(u, mask)
            return carry

        lax.fori_loop(low, high + 1, step, 0)


def row(ref, index):
    return ref[pl.ds(index, 1), :]


def logistic(values):
    return 0.5 * jnp.tanh(0.5 * values) + 0.5


def build_taps(padded_ref, taps_ref, ends, tile_start, base, mirrored):
    rows, channels = taps_ref.shape[0], taps_ref.shape[1] // 3
    start = pl.multiple_of(tile_start, PAD)
    block = padded_ref[pl.ds(start, rows + 2 * PAD), :].astype(F32)
    before = block[PAD - 1 : PAD - 1 + rows]
    after = block[PAD + 1 : PAD + 1 + rows]
    left, right = (2, 0) if mirrored else (0, 2)
    taps_ref[:, channels : 2 * channels] = padded_ref[pl.ds(start + PAD, rows), :]
    first = base + tile_start
    same = owner_at(ends, first - 1) == owner_at(ends, first + rows)

    @pl.when(same)
    def _():
        taps_ref[:, left * channels : (left + 1) * channels] = before.astype(BF16)
        taps_ref[:, right * channels : (right + 1) * channels] = after.astype(BF16)

    @pl.when(jnp.logical_not(same))
    def _():
        positions = rows_of(first, (rows, channels))
        cut_left = positions == ends[0]
        cut_right = positions + 1 == ends[0]
        for end in ends[1:]:
            cut_left = cut_left | (positions == end)
            cut_right = cut_right | (positions + 1 == end)
        taps_ref[:, left * channels : (left + 1) * channels] = jnp.where(
            cut_left, 0.0, before
        ).astype(BF16)
        taps_ref[:, right * channels : (right + 1) * channels] = jnp.where(
            cut_right, 0.0, after
        ).astype(BF16)


def sum_over_tm(own_ref, other_refs, first, count):
    one, two, three = other_refs
    part = pl.ds(first, count)
    return (own_ref[part, :] + two[part, :]) + (one[part, :] + three[part, :])


def finish_stats(acc_ref, stat_ref):
    for kind in range(2):
        for u in range(8):
            at = kind * 8 + u
            if u < UTTS:
                first = (kind * (UTTS + 1) + u) * 8
                stat_ref[at : at + 1, :] = jnp.sum(
                    acc_ref[first : first + 8, :], axis=0, keepdims=True
                )
            else:
                stat_ref[at : at + 1, :] = jnp.zeros_like(stat_ref[at : at + 1, :])
    stat_ref[16:24, :] = jnp.zeros_like(stat_ref[16:24, :])


ACC_ROWS = 2 * (UTTS + 1) * 8


def add_stats(acc_ref, u, first, second):
    for kind, term in enumerate((first, second)):
        at = pl.ds(pl.multiple_of((kind * (UTTS + 1) + u) * 8, 8), 8)
        acc_ref[at, :] += fold_rows(term)


def read_ends(info_ref):
    return [info_ref[k] for k in range(UTTS)]


def halo_owner(info_ref, ends, base, frames):
    before = jnp.where(base == 0, UTTS, owner_at(ends, base - 1))
    return before, owner_at(ends, base + frames)


def gradient_kernel(
    info_ref, cot_ref, before_ref, after_ref, weight_ref, out_ref, padded_ref, bias_ref, taps_ref
):
    frames, channels = cot_ref.shape
    ends = read_ends(info_ref)
    base = info_ref[8]
    owner_before, owner_after = halo_owner(info_ref, ends, base, frames)
    zeros = jnp.zeros((PAD, channels), BF16)
    padded_ref[0:PAD, :] = zeros
    padded_ref[PAD + frames :, :] = zeros
    tile = jnp.broadcast_to(before_ref[...].astype(F32) * ROOT_HALF, (PAD, channels))
    padded_ref[0:PAD, :] = jnp.where(owner_before < UTTS, tile, 0.0).astype(BF16)
    tile = jnp.broadcast_to(after_ref[...].astype(F32) * ROOT_HALF, (PAD, channels))
    padded_ref[PAD + frames :, :] = jnp.where(owner_after < UTTS, tile, 0.0).astype(BF16)
    bias_ref[...] = jnp.zeros_like(bias_ref)

    def scale(i, carry):
        start = pl.multiple_of(i * ROWS, ROWS)
        here = cot_ref[pl.ds(start, ROWS), :].astype(F32) * ROOT_HALF
        here = jnp.where(rows_of(base + start, (ROWS, channels)) < ends[UTTS - 1], here, 0.0)
        rounded = here.astype(BF16)
        padded_ref[pl.ds(start + PAD, ROWS), :] = rounded
        bias_ref[...] += fold_rows(rounded.astype(F32))
        return carry

    lax.fori_loop(0, frames // ROWS, scale, 0)

    def step(i, carry):
        start = pl.multiple_of(i * ROWS, ROWS)
        build_taps(padded_ref, taps_ref, ends, start, base, True)
        out_ref[pl.ds(start, ROWS), :] = jnp.dot(
            taps_ref[...], weight_ref[...], preferred_element_type=F32
        )
        return carry

    lax.fori_loop(0, frames // ROWS, step, 0)


def upsample_kernel(
    info_ref,
    offset_ref,
    before_ref,
    own_ref,
    after_ref,
    align_ref,
    bias_ref,
    out_ref,
    wide_ref,
    stat_ref,
    buffer_ref,
    acc_ref,
):
    frames, channels = out_ref.shape
    window = align_ref.shape[1]
    tiles = offset_ref.shape[0]
    rows = frames // tiles
    halo, own = before_ref.shape[0], own_ref.shape[0]
    ends = read_ends(info_ref)
    slot_ends = [info_ref[UTTS + k] for k in range(UTTS)]
    base, slot_base = info_ref[8], info_ref[9]
    buffer_ref[0:halo, :] = before_ref[...]
    buffer_ref[halo : halo + own, :] = own_ref[...]
    buffer_ref[halo + own : 2 * halo + own, :] = after_ref[...]
    buffer_ref[2 * halo + own :, :] = jnp.zeros_like(buffer_ref[2 * halo + own :, :])
    acc_ref[...] = jnp.zeros_like(acc_ref)

    def step(i, carry):
        start = pl.multiple_of(i * rows, rows)
        shift = offset_ref[i] - slot_base
        aligned = pl.multiple_of((shift // PAD) * PAD, PAD)
        block = align_ref[pl.ds(start, rows), :].astype(F32)
        block = jnp.concatenate([block, jnp.zeros((rows, WIDE - window), F32)], axis=1)
        block = pltpu.roll(block, shift - aligned, 1)
        slots = slot_base + aligned + lax.broadcasted_iota(I32, (rows, WIDE), 1)
        slot_owner = owner_at(slot_ends, slots)
        frame_owner = owner_at(ends, rows_of(base + start, (rows, WIDE)))
        match = (slot_owner == frame_owner) & (frame_owner < UTTS)
        block = jnp.where(match, block, 0.0).astype(BF16)
        wide_ref[pl.ds(start, rows), :] = block
        out_ref[pl.ds(start, rows), :] = jnp.dot(
            block, buffer_ref[pl.ds(aligned, WIDE), :], preferred_element_type=F32
        )
        return carry

    lax.fori_loop(0, tiles, step, 0)

    def sums(i, carry):
        start = pl.multiple_of(i * ROWS, ROWS)

        def uniform(u):
            here = out_ref[pl.ds(start, ROWS), :]
            add_stats(acc_ref, u, here, here * here)

        def mixed(u, mask):
            here = jnp.where(mask((ROWS, channels)), out_ref[pl.ds(start, ROWS), :], 0.0)
            add_stats(acc_ref, u, here, here * here)

        by_utterance(ends, base + start, ROWS, uniform, mixed)
        return carry

    lax.fori_loop(0, frames // ROWS, sums, 0)
    finish_stats(acc_ref, stat_ref)
    stat_ref[FIRST_ROW : FIRST_ROW + 1, :] = out_ref[0:1, :]
    stat_ref[LAST_ROW : LAST_ROW + 1, :] = out_ref[frames - 1 : frames, :]
    stat_ref[EXTRA_ROW : EXTRA_ROW + 1, :] = jnp.sum(bias_ref[...], axis=0, keepdims=True)


def write_coefficients(own_ref, other_refs, inverse_ref, params_ref, coef_ref):
    channels = inverse_ref.shape[1]
    inverse = inverse_ref[...]
    total = sum_over_tm(own_ref, other_refs, 0, 8)
    square = sum_over_tm(own_ref, other_refs, 8, 8)
    mean = total * inverse
    rstd = lax.rsqrt(square * inverse - mean * mean + EPSILON)
    real = inverse > 0.0
    scale = jnp.where(real, (1.0 + params_ref[:, 0:channels]) * rstd, 0.0)
    shift = jnp.where(real, params_ref[:, channels : 2 * channels] - mean * scale, 0.0)
    coef_ref[0:8, :] = mean
    coef_ref[8:16, :] = jnp.where(real, rstd, 0.0)
    coef_ref[16:24, :] = scale
    coef_ref[24:32, :] = shift


def activation(values, coef_ref, u):
    normed = values * row(coef_ref, 16 + u) + row(coef_ref, 24 + u)
    return normed * logistic(normed)


def first_conv_kernel(
    info_ref,
    values_ref,
    own_ref,
    one_ref,
    two_ref,
    three_ref,
    inverse_ref,
    params_ref,
    weight_ref,
    act_ref,
    out_ref,
    coef_ref,
    stat_ref,
    taps_ref,
    acc_ref,
):
    frames, channels = values_ref.shape
    ends = read_ends(info_ref)
    base = info_ref[8]
    write_coefficients(own_ref, (one_ref, two_ref, three_ref), inverse_ref, params_ref, coef_ref)
    acc_ref[...] = jnp.zeros_like(acc_ref)
    owner_before, owner_after = halo_owner(info_ref, ends, base, frames)
    edge = activation(row(one_ref, LAST_ROW), coef_ref, owner_before)
    act_ref[0:PAD, :] = jnp.broadcast_to(edge, (PAD, channels)).astype(BF16)
    edge = activation(row(three_ref, FIRST_ROW), coef_ref, owner_after)
    act_ref[PAD + frames :, :] = jnp.broadcast_to(edge, (PAD, channels)).astype(BF16)

    def act_step(i, carry):
        start = pl.multiple_of(i * ROWS, ROWS)

        def uniform(u):
            here = activation(values_ref[pl.ds(start, ROWS), :], coef_ref, u)
            act_ref[pl.ds(start + PAD, ROWS), :] = here.astype(BF16)

        def mixed(u, mask):
            here = activation(values_ref[pl.ds(start, ROWS), :], coef_ref, u)
            old = act_ref[pl.ds(start + PAD, ROWS), :].astype(F32)
            here = jnp.where(mask((ROWS, channels)), here, old)
            act_ref[pl.ds(start + PAD, ROWS), :] = here.astype(BF16)

        by_utterance(ends, base + start, ROWS, uniform, mixed)
        return carry

    lax.fori_loop(0, frames // ROWS, act_step, 0)

    def step(i, carry):
        start = pl.multiple_of(i * ROWS, ROWS)
        build_taps(act_ref, taps_ref, ends, start, base, False)
        out_ref[pl.ds(start, ROWS), :] = jnp.dot(
            taps_ref[...], weight_ref[...], preferred_element_type=F32
        )

        def uniform(u):
            here = out_ref[pl.ds(start, ROWS), :]
            add_stats(acc_ref, u, here, here * here)

        def mixed(u, mask):
            here = jnp.where(mask((ROWS, channels)), out_ref[pl.ds(start, ROWS), :], 0.0)
            add_stats(acc_ref, u, here, here * here)

        by_utterance(ends, base + start, ROWS, uniform, mixed)
        return carry

    lax.fori_loop(0, frames // ROWS, step, 0)
    finish_stats(acc_ref, stat_ref)
    stat_ref[FIRST_ROW : FIRST_ROW + 1, :] = out_ref[0:1, :]
    stat_ref[LAST_ROW : LAST_ROW + 1, :] = out_ref[frames - 1 : frames, :]


def slope_and_sums(gradient, values, coef_ref, u):
    normed = values * row(coef_ref, 16 + u) + row(coef_ref, 24 + u)
    gate = logistic(normed)
    act = normed * gate
    inner = gradient * (gate + act * (1.0 - gate))
    unit = (values - row(coef_ref, u)) * row(coef_ref, 8 + u)
    return act, inner, inner * unit


def second_norm_kernel(
    info_ref,
    gradient_ref,
    values_ref,
    own_ref,
    one_ref,
    two_ref,
    three_ref,
    inverse_ref,
    params_ref,
    act_ref,
    inner_ref,
    coef_ref,
    stat_ref,
    acc_ref,
):
    frames, channels = values_ref.shape
    ends = read_ends(info_ref)
    base = info_ref[8]
    write_coefficients(own_ref, (one_ref, two_ref, three_ref), inverse_ref, params_ref, coef_ref)
    acc_ref[...] = jnp.zeros_like(acc_ref)
    owner_before, owner_after = halo_owner(info_ref, ends, base, frames)
    edge = activation(row(one_ref, LAST_ROW), coef_ref, owner_before)
    act_ref[0:PAD, :] = jnp.broadcast_to(edge, (PAD, channels)).astype(BF16)
    edge = activation(row(three_ref, FIRST_ROW), coef_ref, owner_after)
    act_ref[PAD + frames :, :] = jnp.broadcast_to(edge, (PAD, channels)).astype(BF16)

    def step(i, carry):
        start = pl.multiple_of(i * ROWS, ROWS)
        here = pl.ds(start, ROWS)

        def uniform(u):
            act, inner, cross = slope_and_sums(
                gradient_ref[here, :], values_ref[here, :], coef_ref, u
            )
            act_ref[pl.ds(start + PAD, ROWS), :] = act.astype(BF16)
            inner_ref[here, :] = inner
            add_stats(acc_ref, u, inner, cross)

        def mixed(u, mask):
            keep = mask((ROWS, channels))
            act, inner, cross = slope_and_sums(
                gradient_ref[here, :], values_ref[here, :], coef_ref, u
            )
            old = act_ref[pl.ds(start + PAD, ROWS), :].astype(F32)
            act_ref[pl.ds(start + PAD, ROWS), :] = jnp.where(keep, act, old).astype(BF16)
            inner_ref[here, :] = jnp.where(keep, inner, inner_ref[here, :])
            add_stats(acc_ref, u, jnp.where(keep, inner, 0.0), jnp.where(keep, cross, 0.0))

        by_utterance(ends, base + start, ROWS, uniform, mixed)
        return carry

    lax.fori_loop(0, frames // ROWS, step, 0)
    finish_stats(acc_ref, stat_ref)
    stat_ref[FIRST_ROW : FIRST_ROW + 1, :] = inner_ref[0:1, :]
    stat_ref[LAST_ROW : LAST_ROW + 1, :] = inner_ref[frames - 1 : frames, :]


def second_conv_kernel(
    info_ref, act_ref, values_ref, weight_ref, bias_ref, out_ref, taps_ref
):
    frames, channels = values_ref.shape
    ends = read_ends(info_ref)
    base = info_ref[8]
    bias = bias_ref[...].astype(F32)

    def step(i, carry):
        start = pl.multiple_of(i * ROWS, ROWS)
        here = pl.ds(start, ROWS)
        build_taps(act_ref, taps_ref, ends, start, base, False)
        branch = jnp.dot(taps_ref[...], weight_ref[...], preferred_element_type=F32) + bias
        valid = rows_of(base + start, (ROWS, channels)) < ends[UTTS - 1]
        total = jnp.where(valid, (values_ref[here, :] + branch) * ROOT_HALF, 0.0)
        out_ref[here, :] = total.astype(BF16)
        return carry

    lax.fori_loop(0, frames // ROWS, step, 0)


def weight_gradient_kernel(info_ref, act_ref, gradient_ref, out_ref, taps_ref, total_ref):
    frames = act_ref.shape[0] - 2 * PAD
    channels = act_ref.shape[1]
    ends = read_ends(info_ref)
    base = info_ref[8]
    total_ref[...] = jnp.zeros_like(total_ref)

    def step(i, carry):
        start = pl.multiple_of(i * ROWS, ROWS)
        build_taps(gradient_ref, taps_ref, ends, start, base, True)
        total_ref[...] += lax.dot_general(
            act_ref[pl.ds(start + PAD, ROWS), :],
            taps_ref[...],
            (((0,), (0,)), ((), ())),
            preferred_element_type=F32,
        )
        return carry

    lax.fori_loop(0, frames // ROWS, step, 0)
    for k in range(3):
        out_ref[k * channels : (k + 1) * channels, :] = total_ref[
            :, k * channels : (k + 1) * channels
        ]


def back_coefficients(own_ref, other_refs, inverse_ref, coef_ref, back_ref):
    inverse = inverse_ref[...]
    total = sum_over_tm(own_ref, other_refs, 0, 8)
    cross = sum_over_tm(own_ref, other_refs, 8, 8)
    mean, rstd, scale = coef_ref[0:8, :], coef_ref[8:16, :], coef_ref[16:24, :]
    back_ref[0:8, :] = total
    back_ref[8:16, :] = cross
    slant = scale * rstd * cross * inverse
    back_ref[16:24, :] = scale * total * inverse - mean * slant
    back_ref[24:32, :] = slant


def inward(inner, values, coef_ref, back_ref, u):
    return (
        inner * row(coef_ref, 16 + u) - row(back_ref, 16 + u) - values * row(back_ref, 24 + u)
    )


def first_back_kernel(
    info_ref,
    inner_ref,
    middle_ref,
    own_ref,
    one_ref,
    two_ref,
    three_ref,
    middle_one_ref,
    middle_three_ref,
    inverse_ref,
    coef_two_ref,
    coef_one_ref,
    values_ref,
    weight_ref,
    gradient_ref,
    out_ref,
    back_ref,
    stat_ref,
    taps_ref,
    acc_ref,
):
    frames, channels = values_ref.shape
    ends = read_ends(info_ref)
    base = info_ref[8]
    back_coefficients(own_ref, (one_ref, two_ref, three_ref), inverse_ref, coef_two_ref, back_ref)
    acc_ref[...] = jnp.zeros_like(acc_ref)
    owner_before, owner_after = halo_owner(info_ref, ends, base, frames)
    edge = inward(
        row(one_ref, LAST_ROW), row(middle_one_ref, LAST_ROW), coef_two_ref, back_ref, owner_before
    )
    gradient_ref[0:PAD, :] = jnp.broadcast_to(edge, (PAD, channels)).astype(BF16)
    edge = inward(
        row(three_ref, FIRST_ROW),
        row(middle_three_ref, FIRST_ROW),
        coef_two_ref,
        back_ref,
        owner_after,
    )
    gradient_ref[PAD + frames :, :] = jnp.broadcast_to(edge, (PAD, channels)).astype(BF16)

    def back_step(i, carry):
        start = pl.multiple_of(i * ROWS, ROWS)
        here = pl.ds(start, ROWS)

        def uniform(u):
            now = inward(inner_ref[here, :], middle_ref[here, :], coef_two_ref, back_ref, u)
            gradient_ref[pl.ds(start + PAD, ROWS), :] = now.astype(BF16)

        def mixed(u, mask):
            now = inward(inner_ref[here, :], middle_ref[here, :], coef_two_ref, back_ref, u)
            old = gradient_ref[pl.ds(start + PAD, ROWS), :].astype(F32)
            now = jnp.where(mask((ROWS, channels)), now, old)
            gradient_ref[pl.ds(start + PAD, ROWS), :] = now.astype(BF16)

        by_utterance(ends, base + start, ROWS, uniform, mixed)
        return carry

    lax.fori_loop(0, frames // ROWS, back_step, 0)

    def step(i, carry):
        start = pl.multiple_of(i * ROWS, ROWS)
        here = pl.ds(start, ROWS)
        build_taps(gradient_ref, taps_ref, ends, start, base, True)
        out_ref[here, :] = jnp.dot(taps_ref[...], weight_ref[...], preferred_element_type=F32)

        def uniform(u):
            _, inner, cross = slope_and_sums(
                out_ref[here, :], values_ref[here, :], coef_one_ref, u
            )
            out_ref[here, :] = inner
            add_stats(acc_ref, u, inner, cross)

        def mixed(u, mask):
            keep = mask((ROWS, channels))
            before = out_ref[here, :]
            _, inner, cross = slope_and_sums(before, values_ref[here, :], coef_one_ref, u)
            out_ref[here, :] = jnp.where(keep, inner, before)
            add_stats(acc_ref, u, jnp.where(keep, inner, 0.0), jnp.where(keep, cross, 0.0))

        by_utterance(ends, base + start, ROWS, uniform, mixed)
        return carry

    lax.fori_loop(0, frames // ROWS, step, 0)
    finish_stats(acc_ref, stat_ref)


def buffer_gradient_kernel(
    info_ref,
    offset_ref,
    inner_ref,
    values_ref,
    cot_ref,
    wide_ref,
    own_ref,
    one_ref,
    two_ref,
    three_ref,
    inverse_ref,
    coef_ref,
    before_ref,
    out_ref,
    after_ref,
    back_ref,
    up_ref,
    total_ref,
):
    frames, channels = values_ref.shape
    tiles = offset_ref.shape[0]
    rows = frames // tiles
    halo, own = before_ref.shape[0], out_ref.shape[0]
    ends = read_ends(info_ref)
    base, slot_base = info_ref[8], info_ref[9]
    back_coefficients(own_ref, (one_ref, two_ref, three_ref), inverse_ref, coef_ref, back_ref)
    total_ref[...] = jnp.zeros_like(total_ref)
    span = rows + PAD

    def step(i, carry):
        start = pl.multiple_of(i * rows, rows)
        here = pl.ds(start, rows)

        def upward(u):
            lead = cot_ref[here, :].astype(F32) * ROOT_HALF
            return lead + inward(inner_ref[here, :], values_ref[here, :], coef_ref, back_ref, u)

        def uniform(u):
            up_ref[...] = upward(u).astype(BF16)

        def mixed(u, mask):
            old = up_ref[...].astype(F32)
            up_ref[...] = jnp.where(mask((rows, channels)), upward(u), old).astype(BF16)

        by_utterance(ends, base + start, rows, uniform, mixed)
        shift = offset_ref[i] - slot_base
        aligned = pl.multiple_of((shift // PAD) * PAD, PAD)
        part = lax.dot_general(
            wide_ref[here, :], up_ref[...], (((0,), (0,)), ((), ())), preferred_element_type=F32
        )
        total_ref[pl.ds(aligned, span), :] += part[0:span]
        return carry

    lax.fori_loop(0, tiles, step, 0)
    before_ref[...] = total_ref[0:halo, :]
    out_ref[...] = total_ref[halo : halo + own, :]
    after_ref[...] = total_ref[halo + own : 2 * halo + own, :]


VM = pl.BlockSpec(memory_space=pltpu.VMEM)
SM = pl.BlockSpec(memory_space=pltpu.SMEM)


def call(kernel, inputs, outputs, scratch, scalars, flops, limit):
    return pl.pallas_call(
        kernel,
        in_specs=[SM] * scalars + [VM] * (len(inputs) - scalars),
        out_specs=tuple(VM for _ in outputs),
        out_shape=tuple(jax.ShapeDtypeStruct(shape, dtype) for shape, dtype in outputs),
        scratch_shapes=[pltpu.VMEM(shape, dtype) for shape, dtype in scratch],
        compiler_params=pltpu.CompilerParams(vmem_limit_bytes=limit * MIB),
        cost_estimate=pl.CostEstimate(flops=flops, bytes_accessed=flops // 200, transcendentals=0),
    )(*inputs)


def shifted(values, axis, step):
    devices = lax.axis_size(axis)
    return lax.ppermute(values, axis, [(i, (i + step) % devices) for i in range(devices)])


def others_over_tm(values):
    return [shifted(values, "tm", d) for d in (1, 2, 3)]


def from_neighbours(first_rows, last_rows):
    devices = lax.axis_size("tm")
    up = [(i, i + 1) for i in range(devices - 1)]
    down = [(i + 1, i) for i in range(devices - 1)]
    return lax.ppermute(last_rows, "tm", up), lax.ppermute(first_rows, "tm", down)


def swapped(values, bit):
    devices = lax.axis_size("seq")
    return lax.ppermute(values, "seq", [(i, i ^ (1 << bit)) for i in range(devices)])


def bit_of(index, bit):
    return (index >> bit) & 1


def sum_everywhere(values, bits):
    copies = lax.axis_size("tm")
    seq_index, tm_index = lax.axis_index("seq"), lax.axis_index("tm")
    part = values
    for bit in bits:
        half = part.shape[0] // 2
        mine = bit_of(seq_index, bit)
        keep = lax.dynamic_slice_in_dim(part, mine * half, half)
        give = lax.dynamic_slice_in_dim(part, (1 - mine) * half, half)
        part = keep + swapped(give.astype(BF16), bit).astype(F32)
    piece = part.shape[0] // copies
    pieces = part.reshape(copies, piece, part.shape[1])
    part = lax.dynamic_index_in_dim(pieces, tm_index, 0, False)
    for step in range(1, copies):
        give = lax.dynamic_index_in_dim(pieces, (tm_index + step) % copies, 0, False)
        part = part + shifted(give.astype(BF16), "tm", step).astype(F32)
    part = part.astype(BF16)
    every = jnp.zeros((copies,) + part.shape, BF16)
    every = lax.dynamic_update_index_in_dim(every, part, tm_index, 0)
    for step in range(1, copies):
        every = lax.dynamic_update_index_in_dim(
            every, shifted(part, "tm", step), (tm_index - step) % copies, 0
        )
    part = every.reshape(copies * piece, part.shape[1])
    for bit in reversed(bits):
        other = swapped(part, bit)
        mine = bit_of(seq_index, bit)
        part = jnp.concatenate(
            [jnp.where(mine == 0, part, other), jnp.where(mine == 0, other, part)]
        )
    return part


def gathered_over_seq(values):
    seq_index = lax.axis_index("seq")
    part = values
    bit = 0
    while (1 << bit) < lax.axis_size("seq"):
        other = swapped(part, bit)
        mine = bit_of(seq_index, bit)
        part = jnp.concatenate(
            [jnp.where(mine == 0, part, other), jnp.where(mine == 0, other, part)]
        )
        bit += 1
    return part


def on_device(
    phonemes,
    send_order,
    phoneme_counts,
    frame_lengths,
    tile_offsets,
    alignment,
    style_vec,
    first_affine_weight,
    first_affine_bias,
    first_conv_weight,
    second_affine_weight,
    second_affine_bias,
    second_conv_weight,
    second_conv_bias,
    cotangent,
):
    frames, channels = cotangent.shape
    slot_count = phonemes.shape[0]
    groups = lax.axis_size("seq")
    copies = lax.axis_size("tm")
    tm_index = lax.axis_index("tm")
    piece_rows = slot_count // groups // copies
    local_rows = slot_count // copies
    tiles = tile_offsets.shape[0]
    window = alignment.shape[1]
    halo = window // 2
    lengths = frame_lengths[0]
    conv_flops = 2 * frames * 3 * channels * channels

    info = jnp.concatenate(
        [
            jnp.cumsum(lengths),
            jnp.cumsum(phoneme_counts[0]),
            (tm_index * frames)[None],
            (tm_index * local_rows - halo)[None],
            jnp.zeros((6,), I32),
        ]
    ).astype(I32)
    inverse = jnp.zeros((8, channels), F32).at[0:UTTS].set(
        jnp.broadcast_to(1.0 / lengths.astype(F32)[:, None], (UTTS, channels))
    )
    style_rows = jnp.zeros((8, style_vec.shape[1]), BF16).at[0:UTTS].set(style_vec)
    params_one = jnp.dot(style_rows, first_affine_weight, preferred_element_type=F32) + (
        first_affine_bias.astype(F32)
    )
    params_two = jnp.dot(style_rows, second_affine_weight, preferred_element_type=F32) + (
        second_affine_bias.astype(F32)
    )

    def turned(weight):
        return (
            weight.reshape(3, channels, channels).transpose(0, 2, 1).reshape(3 * channels, channels)
        )

    order = send_order[0].reshape(groups, copies, piece_rows)
    mine = lax.dynamic_index_in_dim(order, tm_index, 1, False)
    outgoing = jnp.take(phonemes, mine.reshape(-1), axis=0, mode="clip")
    received = lax.all_to_all(
        outgoing.reshape(groups, piece_rows, channels), "seq", 0, 0, tiled=True
    ).reshape(local_rows, channels)
    slots_before, slots_after = from_neighbours(received[:halo], received[-halo:])

    cot_before, cot_after = from_neighbours(cotangent[:1], cotangent[-1:])
    grad_act_two, grad_branch, bias_part = call(
        gradient_kernel,
        (info, cotangent, cot_before, cot_after, turned(second_conv_weight)),
        (
            ((frames, channels), F32),
            ((frames + 2 * PAD, channels), BF16),
            ((8, channels), F32),
        ),
        [((ROWS, 3 * channels), BF16)],
        1,
        conv_flops,
        24,
    )

    upsampled, wide, stat = call(
        upsample_kernel,
        (info, tile_offsets, slots_before, received, slots_after, alignment, bias_part),
        (
            ((frames, channels), F32),
            ((frames, WIDE), BF16),
            ((STAT_ROWS, channels), F32),
        ),
        [((local_rows + WIDE, channels), BF16), ((ACC_ROWS, channels), F32)],
        2,
        2 * frames * WIDE * channels,
        24,
    )
    others = others_over_tm(stat)
    bias_total = (stat[EXTRA_ROW] + others[1][EXTRA_ROW]) + (
        others[0][EXTRA_ROW] + others[2][EXTRA_ROW]
    )

    act_one, middle, coef_one, stat_two = call(
        first_conv_kernel,
        (info, upsampled, stat, *others, inverse, params_one, first_conv_weight),
        (
            ((frames + 2 * PAD, channels), BF16),
            ((frames, channels), F32),
            ((32, channels), F32),
            ((STAT_ROWS, channels), F32),
        ),
        [((ROWS, 3 * channels), BF16), ((ACC_ROWS, channels), F32)],
        1,
        conv_flops,
        24,
    )
    others_two = others_over_tm(stat_two)

    act_two, inner_two, coef_two, stat_three = call(
        second_norm_kernel,
        (info, grad_act_two, middle, stat_two, *others_two, inverse, params_two),
        (
            ((frames + 2 * PAD, channels), BF16),
            ((frames, channels), F32),
            ((32, channels), F32),
            ((STAT_ROWS, channels), F32),
        ),
        [((ACC_ROWS, channels), F32)],
        1,
        2 * frames * channels * 100,
        24,
    )
    others_three = others_over_tm(stat_three)

    (frames_out,) = call(
        second_conv_kernel,
        (info, act_two, upsampled, second_conv_weight, second_conv_bias[None]),
        (((frames, channels), BF16),),
        [((ROWS, 3 * channels), BF16)],
        1,
        conv_flops,
        24,
    )
    (second_grad,) = call(
        weight_gradient_kernel,
        (info, act_two, grad_branch),
        (((3 * channels, channels), F32),),
        [((ROWS, 3 * channels), BF16), ((channels, 3 * channels), F32)],
        1,
        conv_flops,
        24,
    )

    grad_middle, inner_one, back_two, stat_four = call(
        first_back_kernel,
        (
            info,
            inner_two,
            middle,
            stat_three,
            *others_three,
            others_two[0],
            others_two[2],
            inverse,
            coef_two,
            coef_one,
            upsampled,
            turned(first_conv_weight),
        ),
        (
            ((frames + 2 * PAD, channels), BF16),
            ((frames, channels), F32),
            ((32, channels), F32),
            ((STAT_ROWS, channels), F32),
        ),
        [((ROWS, 3 * channels), BF16), ((ACC_ROWS, channels), F32)],
        1,
        conv_flops,
        24,
    )
    others_four = others_over_tm(stat_four)
    (first_grad,) = call(
        weight_gradient_kernel,
        (info, act_one, grad_middle),
        (((3 * channels, channels), F32),),
        [((ROWS, 3 * channels), BF16), ((channels, 3 * channels), F32)],
        1,
        conv_flops,
        24,
    )

    grad_before, grad_own, grad_after, back_one = call(
        buffer_gradient_kernel,
        (
            info,
            tile_offsets,
            inner_one,
            upsampled,
            cotangent,
            wide,
            stat_four,
            *others_four,
            inverse,
            coef_one,
        ),
        (
            ((halo, channels), F32),
            ((local_rows, channels), F32),
            ((halo, channels), F32),
            ((32, channels), F32),
        ),
        [((frames // tiles, channels), BF16), ((local_rows + WIDE, channels), F32)],
        2,
        2 * frames * WIDE * channels,
        24,
    )

    from_before, from_after = from_neighbours(grad_before, grad_after)
    return_rows = jnp.concatenate(
        [
            grad_own[:halo] + from_before,
            grad_own[halo:-halo],
            grad_own[-halo:] + from_after,
        ]
    ).astype(BF16)
    returned = lax.all_to_all(
        return_rows.reshape(groups, piece_rows, channels), "seq", 0, 0, tiled=True
    )
    parts = [returned] + others_over_tm(returned)
    slots_back = jnp.zeros((groups, copies, piece_rows, channels), BF16)
    for step, part in enumerate(parts):
        slots_back = lax.dynamic_update_index_in_dim(
            slots_back, part, (tm_index - step) % copies, 1
        )
    place = (
        jnp.zeros((slot_count,), I32)
        .at[send_order[0]]
        .set(jnp.arange(slot_count, dtype=I32), unique_indices=True)
    )
    phonemes_grad = jnp.take(
        slots_back.reshape(slot_count, channels), place, axis=0, mode="clip"
    ).astype(F32)

    bits = [b for b in range(16) if (1 << b) < groups]
    second_conv_grad = sum_everywhere(second_grad, bits).astype(F32)
    first_conv_grad = sum_everywhere(first_grad, bits[:1] + bits[1:][::-1]).astype(F32)
    params_grad = [
        jnp.concatenate([back[8 : 8 + UTTS], back[0:UTTS]], axis=1) for back in (back_one, back_two)
    ]
    style_grad = jnp.dot(
        params_grad[0], first_affine_weight.astype(F32).T, precision=PRECISE
    ) + jnp.dot(params_grad[1], second_affine_weight.astype(F32).T, precision=PRECISE)
    small = jnp.concatenate(
        [
            params_grad[0].reshape(2 * UTTS, channels),
            params_grad[1].reshape(2 * UTTS, channels),
            style_vec.astype(F32).reshape(-1, channels),
            bias_total[None],
            jnp.zeros((6, channels), F32),
        ]
    )
    every = gathered_over_seq(small[None])
    styles = every[:, 4 * UTTS].reshape(groups * UTTS, -1)
    grads = [
        every[:, 2 * UTTS * k : 2 * UTTS * (k + 1)].reshape(groups * UTTS, 2 * channels)
        for k in range(2)
    ]
    affine_grads = [
        lax.dot_general(styles, g, (((0,), (0,)), ((), ())), precision=PRECISE) for g in grads
    ]
    shift_grads = [jnp.sum(g, axis=0) for g in grads]
    second_bias_grad = jnp.sum(every[:, 4 * UTTS + 1], axis=0)
    return (
        frames_out,
        phonemes_grad,
        style_grad,
        affine_grads[0],
        shift_grads[0],
        first_conv_grad,
        affine_grads[1],
        shift_grads[1],
        second_conv_grad,
        second_bias_grad,
    )


def solution(mesh):
    split, whole = ("seq", "tm"), P()
    in_specs = (
        P("seq", None),
        P("seq", None),
        P("seq", None),
        P("seq", None),
        P(split),
        P(split, None),
        P("seq", None),
        *([whole] * 7),
        P(split, None),
    )
    out_specs = (P(split, None), P("seq", None), P("seq", None), *([whole] * 7))
    return jax.shard_map(
        on_device, mesh=mesh, in_specs=in_specs, out_specs=out_specs, check_vma=False
    )
```

```python
import functools

import jax
import jax.numpy as jnp
from jax import lax
from jax.experimental import pallas as pl
from jax.experimental.pallas import tpu as pltpu
from jax.sharding import PartitionSpec as P

EPSILON = 1e-05
ROOT_HALF = 0.7071067811865476
PRECISE = lax.Precision.HIGHEST
F32, BF16, I32 = jnp.float32, jnp.bfloat16, jnp.int32
UTTS = 4
PAD = 16
ROWS = 1024
BLOCK = 128
WIDE = 256
MIB = 2**20

STAT_ROWS = 24
FIRST_ROW, LAST_ROW, EXTRA_ROW = 16, 17, 18
SMALL_ROWS = 48
BITS_AT = 12


def owner_at(ends, position):
    return sum((position >= end).astype(I32) for end in ends)


def tile_of(ref, index, offset=0):
    return ref.at[pl.ds(pl.multiple_of(offset + index * ROWS, PAD), ROWS), :]


class Stream:
    def __init__(self, source, target, sems, source_offset=0, target_offset=0):
        self.ends = (source, source_offset, target, target_offset)
        self.sems = sems
        self.tiles = sems.shape[0]

    def tile(self, index):
        source, source_offset, target, target_offset = self.ends
        return pltpu.make_async_copy(
            tile_of(source, index, source_offset),
            tile_of(target, index, target_offset),
            self.sems.at[index],
        )

    def start(self):
        for index in range(self.tiles):
            self.tile(index).start()

    def finish(self):
        for index in range(self.tiles):
            self.tile(index).wait()


def edge_copies(source, target, sems):
    last = source.shape[0] - PAD
    return [
        pltpu.make_async_copy(
            source.at[pl.ds(at, PAD), :], target.at[pl.ds(at, PAD), :], sems.at[k]
        )
        for k, at in enumerate((0, last))
    ]


def rows_of(start, shape):
    return start + lax.broadcasted_iota(I32, shape, 0)


def fold_rows(values):
    return jnp.sum(values.reshape(values.shape[0] // 8, 8, values.shape[1]), axis=0)


def by_utterance(ends, start, count, uniform_body, mixed_body):
    low, high = owner_at(ends, start), owner_at(ends, start + count - 1)

    @pl.when(low == high)
    def _():
        uniform_body(low)

    @pl.when(low != high)
    def _():
        def step(u, carry):
            lower = jnp.int32(-1)
            upper = jnp.int32(2**30)
            for k in range(UTTS):
                lower = jnp.where(u == k + 1, ends[k], lower)
                upper = jnp.where(u == k, ends[k], upper)

            def mask(shape):
                rows = rows_of(start, shape)
                return (rows >= lower) & (rows < upper)

            mixed_body(u, mask)
            return carry

        lax.fori_loop(low, high + 1, step, 0)


def row(ref, index):
    return ref[pl.ds(index, 1), :]


def logistic(values):
    return 0.5 * jnp.tanh(0.5 * values) + 0.5


def taps_of(padded_ref, ends, start, base):
    channels = padded_ref.shape[1]
    block = padded_ref[pl.ds(start, ROWS + 2 * PAD), :].astype(F32)
    positions = rows_of(base + start, (ROWS, channels))
    cut_left = positions == ends[0]
    cut_right = positions + 1 == ends[0]
    for end in ends[1:]:
        cut_left = cut_left | (positions == end)
        cut_right = cut_right | (positions + 1 == end)
    before = jnp.where(cut_left, 0.0, block[PAD - 1 : PAD - 1 + ROWS]).astype(BF16)
    after = jnp.where(cut_right, 0.0, block[PAD + 1 : PAD + 1 + ROWS]).astype(BF16)
    return before, padded_ref[pl.ds(start + PAD, ROWS), :], after


def convolved(taps, weight_ref):
    channels = weight_ref.shape[1]
    return sum(
        jnp.dot(tap, weight_ref[k * channels : (k + 1) * channels, :], preferred_element_type=F32)
        for k, tap in enumerate(taps)
    )


def for_blocks(first, count, size, body, unroll=1):
    def step(i, carry):
        body(pl.multiple_of(first + i * size, size))
        return carry

    lax.fori_loop(0, count // size, step, 0, unroll=unroll)


def for_tiles(count, body):
    def step(i, carry):
        body(i, pl.multiple_of(i * ROWS, ROWS))
        return carry

    lax.fori_loop(0, count // ROWS, step, 0)


def wait_next(streams, i, count):
    @pl.when(i + 1 < count // ROWS)
    def _():
        for stream in streams:
            stream.tile(i + 1).wait()


def sum_over_tm(own_ref, other_refs, first, count):
    one, two, three = other_refs
    part = pl.ds(first, count)
    return (own_ref[part, :] + two[part, :]) + (one[part, :] + three[part, :])


def finish_stats(acc_ref, stat_ref):
    for kind in range(2):
        for u in range(8):
            at = kind * 8 + u
            if u < UTTS:
                first = (kind * (UTTS + 1) + u) * 8
                stat_ref[at : at + 1, :] = jnp.sum(
                    acc_ref[first : first + 8, :], axis=0, keepdims=True
                )
            else:
                stat_ref[at : at + 1, :] = jnp.zeros_like(stat_ref[at : at + 1, :])
    stat_ref[16:24, :] = jnp.zeros_like(stat_ref[16:24, :])


ACC_ROWS = 2 * (UTTS + 1) * 8


def add_stats(acc_ref, u, first, second):
    for kind, term in enumerate((first, second)):
        at = pl.ds(pl.multiple_of((kind * (UTTS + 1) + u) * 8, 8), 8)
        acc_ref[at, :] += fold_rows(term)


def read_ends(info_ref):
    return [info_ref[k] for k in range(UTTS)]


def halo_owner(info_ref, ends, base, frames):
    before = jnp.where(base == 0, UTTS, owner_at(ends, base - 1))
    return before, owner_at(ends, base + frames)


def gradient_kernel(
    info_ref,
    cot_hbm,
    before_ref,
    after_ref,
    weight_ref,
    out_hbm,
    padded_hbm,
    bias_ref,
    cot_ref,
    padded_ref,
    out_ref,
    cot_sems,
    padded_sems,
    edge_sems,
    out_sems,
):
    frames, channels = cot_ref.shape
    ends = read_ends(info_ref)
    base = info_ref[8]
    cot_in = Stream(cot_hbm, cot_ref, cot_sems)
    padded_out = Stream(padded_ref, padded_hbm, padded_sems, PAD, PAD)
    outward = Stream(out_ref, out_hbm, out_sems)
    cot_in.start()
    owner_before, owner_after = halo_owner(info_ref, ends, base, frames)
    tile = jnp.broadcast_to(before_ref[...].astype(F32) * ROOT_HALF, (PAD, channels))
    padded_ref[0:PAD, :] = jnp.where(owner_before < UTTS, tile, 0.0).astype(BF16)
    tile = jnp.broadcast_to(after_ref[...].astype(F32) * ROOT_HALF, (PAD, channels))
    padded_ref[PAD + frames :, :] = jnp.where(owner_after < UTTS, tile, 0.0).astype(BF16)
    edges = edge_copies(padded_ref, padded_hbm, edge_sems)
    for edge in edges:
        edge.start()
    bias_ref[...] = jnp.zeros_like(bias_ref)

    def scale(start):
        here = cot_ref[pl.ds(start, BLOCK), :].astype(F32) * ROOT_HALF
        here = jnp.where(rows_of(base + start, (BLOCK, channels)) < ends[UTTS - 1], here, 0.0)
        rounded = here.astype(BF16)
        padded_ref[pl.ds(start + PAD, BLOCK), :] = rounded
        bias_ref[...] += fold_rows(rounded.astype(F32))

    def scale_tile(i, start):
        cot_in.tile(i).wait()
        for_blocks(start, ROWS, BLOCK, scale)
        padded_out.tile(i).start()

    for_tiles(frames, scale_tile)

    def conv(i, start):
        before, here, after = taps_of(padded_ref, ends, start, base)
        total = convolved((after, here, before), weight_ref)
        out_ref[pl.ds(start, ROWS), :] = total.astype(BF16)
        outward.tile(i).start()

    for_tiles(frames, conv)
    padded_out.finish()
    outward.finish()
    for edge in edges:
        edge.wait()


def upsample_kernel(
    info_ref,
    offset_ref,
    before_ref,
    own_ref,
    after_ref,
    align_hbm,
    bias_ref,
    out_ref,
    out_hbm,
    wide_hbm,
    stat_ref,
    buffer_ref,
    acc_ref,
    align_ref,
    wide_ref,
    align_sems,
    out_sems,
    wide_sems,
):
    frames, channels = out_ref.shape
    align_in = Stream(align_hbm, align_ref, align_sems)
    outward = Stream(out_ref, out_hbm, out_sems)
    wide_out = Stream(wide_ref, wide_hbm, wide_sems)
    align_in.start()
    window = align_ref.shape[1]
    tiles = offset_ref.shape[0]
    rows = frames // tiles
    halo, own = before_ref.shape[0], own_ref.shape[0]
    ends = read_ends(info_ref)
    slot_ends = [info_ref[UTTS + k] for k in range(UTTS)]
    base, slot_base = info_ref[8], info_ref[9]
    buffer_ref[0:halo, :] = before_ref[...]
    buffer_ref[halo : halo + own, :] = own_ref[...]
    buffer_ref[halo + own : 2 * halo + own, :] = after_ref[...]
    buffer_ref[2 * halo + own :, :] = jnp.zeros_like(buffer_ref[2 * halo + own :, :])
    acc_ref[...] = jnp.zeros_like(acc_ref)

    def step(i):
        start = pl.multiple_of(i * rows, rows)
        shift = offset_ref[i] - slot_base
        aligned = pl.multiple_of((shift // PAD) * PAD, PAD)
        block = align_ref[pl.ds(start, rows), :].astype(F32)
        block = jnp.concatenate([block, jnp.zeros((rows, WIDE - window), F32)], axis=1)
        block = pltpu.roll(block, shift - aligned, 1)
        slots = slot_base + aligned + lax.broadcasted_iota(I32, (rows, WIDE), 1)
        slot_owner = owner_at(slot_ends, slots)
        frame_owner = owner_at(ends, rows_of(base + start, (rows, WIDE)))
        match = (slot_owner == frame_owner) & (frame_owner < UTTS)
        block = jnp.where(match, block, 0.0).astype(BF16)
        wide_ref[pl.ds(start, rows), :] = block
        out_ref[pl.ds(start, rows), :] = jnp.dot(
            block, buffer_ref[pl.ds(aligned, WIDE), :], preferred_element_type=F32
        )

    def blocks(i, start):
        align_in.tile(i).wait()
        each = ROWS // rows

        def four(k, carry):
            for n in range(4):
                step(i * each + k * 4 + n)
            return carry

        lax.fori_loop(0, each // 4, four, 0)
        outward.tile(i).start()
        wide_out.tile(i).start()
        for_blocks(
            start, ROWS, BLOCK, lambda at: value_sums(out_ref, acc_ref, ends, base, at)
        )

    for_tiles(frames, blocks)
    finish_stats(acc_ref, stat_ref)
    stat_ref[FIRST_ROW : FIRST_ROW + 1, :] = out_ref[0:1, :]
    stat_ref[LAST_ROW : LAST_ROW + 1, :] = out_ref[frames - 1 : frames, :]
    stat_ref[EXTRA_ROW : EXTRA_ROW + 1, :] = jnp.sum(bias_ref[...], axis=0, keepdims=True)
    outward.finish()
    wide_out.finish()


def value_sums(out_ref, acc_ref, ends, base, start):
    channels = out_ref.shape[1]

    def uniform(u):
        here = out_ref[pl.ds(start, BLOCK), :]
        add_stats(acc_ref, u, here, here * here)

    def mixed(u, mask):
        here = jnp.where(mask((BLOCK, channels)), out_ref[pl.ds(start, BLOCK), :], 0.0)
        add_stats(acc_ref, u, here, here * here)

    by_utterance(ends, base + start, BLOCK, uniform, mixed)


def write_coefficients(own_ref, other_refs, inverse_ref, params_ref, coef_ref):
    channels = inverse_ref.shape[1]
    inverse = inverse_ref[...]
    total = sum_over_tm(own_ref, other_refs, 0, 8)
    square = sum_over_tm(own_ref, other_refs, 8, 8)
    mean = total * inverse
    real = inverse > 0.0
    rstd = jnp.where(real, lax.rsqrt(square * inverse - mean * mean + EPSILON), 0.0)
    coef_ref[0:8, :] = rstd
    coef_ref[8:16, :] = mean * rstd
    coef_ref[16:24, :] = jnp.where(real, 1.0 + params_ref[:, 0:channels], 0.0)
    coef_ref[24:32, :] = jnp.where(real, params_ref[:, channels : 2 * channels], 0.0)


def unit_of(values, coef_ref, u):
    return values * row(coef_ref, u) - row(coef_ref, 8 + u)


def normed_of(unit, coef_ref, u):
    return unit * row(coef_ref, 16 + u) + row(coef_ref, 24 + u)


def activation(values, coef_ref, u):
    normed = normed_of(unit_of(values, coef_ref, u), coef_ref, u)
    return normed * logistic(normed)


def edge_rows(padded_ref, before, after):
    channels = padded_ref.shape[1]
    padded_ref[0:PAD, :] = jnp.broadcast_to(before, (PAD, channels)).astype(BF16)
    last = padded_ref.shape[0] - PAD
    padded_ref[last:, :] = jnp.broadcast_to(after, (PAD, channels)).astype(BF16)


def first_conv_kernel(
    info_ref,
    values_ref,
    own_ref,
    one_ref,
    two_ref,
    three_ref,
    inverse_ref,
    params_ref,
    weight_ref,
    act_hbm,
    out_ref,
    unit_hbm,
    coef_ref,
    stat_ref,
    acc_ref,
    act_ref,
    unit_ref,
    act_sems,
    edge_sems,
    unit_sems,
):
    frames, channels = values_ref.shape
    act_out = Stream(act_ref, act_hbm, act_sems, PAD, PAD)
    unit_out = Stream(unit_ref, unit_hbm, unit_sems)
    ends = read_ends(info_ref)
    base = info_ref[8]
    write_coefficients(own_ref, (one_ref, two_ref, three_ref), inverse_ref, params_ref, coef_ref)
    acc_ref[...] = jnp.zeros_like(acc_ref)
    owner_before, owner_after = halo_owner(info_ref, ends, base, frames)
    edge_rows(
        act_ref,
        activation(row(one_ref, LAST_ROW), coef_ref, owner_before),
        activation(row(three_ref, FIRST_ROW), coef_ref, owner_after),
    )

    edges = edge_copies(act_ref, act_hbm, edge_sems)
    for edge in edges:
        edge.start()

    def act_step(start):
        here = pl.ds(start, BLOCK)
        there = pl.ds(start + PAD, BLOCK)

        def parts(u):
            unit = unit_of(values_ref[here, :], coef_ref, u)
            normed = normed_of(unit, coef_ref, u)
            return unit, normed * logistic(normed)

        def uniform(u):
            unit, act = parts(u)
            unit_ref[here, :] = unit.astype(BF16)
            act_ref[there, :] = act.astype(BF16)

        def mixed(u, mask):
            keep = mask((BLOCK, channels))
            unit, act = parts(u)
            unit_ref[here, :] = jnp.where(keep, unit, unit_ref[here, :].astype(F32)).astype(BF16)
            act_ref[there, :] = jnp.where(keep, act, act_ref[there, :].astype(F32)).astype(BF16)

        by_utterance(ends, base + start, BLOCK, uniform, mixed)

    def act_tile(i, start):
        for_blocks(start, ROWS, BLOCK, act_step)
        act_out.tile(i).start()
        unit_out.tile(i).start()

    for_tiles(frames, act_tile)

    def conv(start):
        out_ref[pl.ds(start, ROWS), :] = convolved(
            taps_of(act_ref, ends, start, base), weight_ref
        )

    for_blocks(0, frames, ROWS, conv)
    for_blocks(0, frames, BLOCK, lambda start: value_sums(out_ref, acc_ref, ends, base, start))
    finish_stats(acc_ref, stat_ref)
    stat_ref[FIRST_ROW : FIRST_ROW + 1, :] = out_ref[0:1, :]
    stat_ref[LAST_ROW : LAST_ROW + 1, :] = out_ref[frames - 1 : frames, :]
    act_out.finish()
    unit_out.finish()
    for edge in edges:
        edge.wait()


def slope_and_sums(gradient, unit, coef_ref, u):
    normed = normed_of(unit, coef_ref, u)
    gate = logistic(normed)
    act = normed * gate
    inner = gradient * (gate + act * (1.0 - gate))
    return act, inner, inner * unit


def second_norm_kernel(
    info_ref,
    gradient_hbm,
    values_ref,
    own_ref,
    one_ref,
    two_ref,
    three_ref,
    inverse_ref,
    params_ref,
    act_ref,
    act_hbm,
    inner_hbm,
    unit_hbm,
    coef_ref,
    stat_ref,
    acc_ref,
    gradient_ref,
    inner_ref,
    unit_ref,
    gradient_sems,
    act_sems,
    edge_sems,
    inner_sems,
    unit_sems,
):
    frames, channels = values_ref.shape
    gradient_in = Stream(gradient_hbm, gradient_ref, gradient_sems)
    outward = [
        Stream(act_ref, act_hbm, act_sems, PAD, PAD),
        Stream(inner_ref, inner_hbm, inner_sems),
        Stream(unit_ref, unit_hbm, unit_sems),
    ]
    gradient_in.start()
    ends = read_ends(info_ref)
    base = info_ref[8]
    write_coefficients(own_ref, (one_ref, two_ref, three_ref), inverse_ref, params_ref, coef_ref)
    acc_ref[...] = jnp.zeros_like(acc_ref)
    owner_before, owner_after = halo_owner(info_ref, ends, base, frames)
    edge_rows(
        act_ref,
        activation(row(one_ref, LAST_ROW), coef_ref, owner_before),
        activation(row(three_ref, FIRST_ROW), coef_ref, owner_after),
    )

    edges = edge_copies(act_ref, act_hbm, edge_sems)
    for edge in edges:
        edge.start()

    def step(start):
        here = pl.ds(start, BLOCK)
        there = pl.ds(start + PAD, BLOCK)

        def parts(u):
            unit = unit_of(values_ref[here, :], coef_ref, u)
            return unit, *slope_and_sums(gradient_ref[here, :].astype(F32), unit, coef_ref, u)

        def uniform(u):
            unit, act, inner, cross = parts(u)
            act_ref[there, :] = act.astype(BF16)
            unit_ref[here, :] = unit.astype(BF16)
            inner_ref[here, :] = inner.astype(BF16)
            add_stats(acc_ref, u, inner, cross)

        def mixed(u, mask):
            keep = mask((BLOCK, channels))
            unit, act, inner, cross = parts(u)
            act_ref[there, :] = jnp.where(keep, act, act_ref[there, :].astype(F32)).astype(BF16)
            unit_ref[here, :] = jnp.where(keep, unit, unit_ref[here, :].astype(F32)).astype(BF16)
            old = inner_ref[here, :].astype(F32)
            inner_ref[here, :] = jnp.where(keep, inner, old).astype(BF16)
            add_stats(acc_ref, u, jnp.where(keep, inner, 0.0), jnp.where(keep, cross, 0.0))

        by_utterance(ends, base + start, BLOCK, uniform, mixed)

    def tile(i, start):
        gradient_in.tile(i).wait()
        for_blocks(start, ROWS, BLOCK, step)
        for stream in outward:
            stream.tile(i).start()

    for_tiles(frames, tile)
    finish_stats(acc_ref, stat_ref)
    stat_ref[FIRST_ROW : FIRST_ROW + 1, :] = inner_ref[0:PAD, :].astype(F32)[0:1]
    stat_ref[LAST_ROW : LAST_ROW + 1, :] = inner_ref[frames - PAD :, :].astype(F32)[PAD - 1 :]
    for stream in outward:
        stream.finish()
    for edge in edges:
        edge.wait()


def second_conv_kernel(
    info_ref,
    act_hbm,
    values_hbm,
    weight_ref,
    bias_ref,
    out_hbm,
    act_ref,
    values_ref,
    out_ref,
    act_sems,
    edge_sems,
    values_sems,
    out_sems,
):
    frames, channels = values_ref.shape
    ends = read_ends(info_ref)
    base = info_ref[8]
    bias = bias_ref[...].astype(F32)
    act_in = Stream(act_hbm, act_ref, act_sems, PAD, PAD)
    values_in = Stream(values_hbm, values_ref, values_sems)
    outward = Stream(out_ref, out_hbm, out_sems)
    edges = edge_copies(act_hbm, act_ref, edge_sems)
    for edge in edges:
        edge.start()
    act_in.start()
    values_in.start()
    for edge in edges:
        edge.wait()
    act_in.tile(0).wait()

    def step(i, start):
        here = pl.ds(start, ROWS)
        wait_next([act_in], i, frames)
        values_in.tile(i).wait()
        branch = convolved(taps_of(act_ref, ends, start, base), weight_ref) + bias
        valid = rows_of(base + start, (ROWS, channels)) < ends[UTTS - 1]
        total = jnp.where(valid, (values_ref[here, :] + branch) * ROOT_HALF, 0.0)
        out_ref[here, :] = total.astype(BF16)
        outward.tile(i).start()

    for_tiles(frames, step)
    outward.finish()


def weight_gradient_kernel(
    stream_act,
    info_ref,
    act_any,
    gradient_any,
    keep_ref,
    give_ref,
    out_ref,
    held_ref,
    held_sems,
    edge_sems,
):
    frames = held_ref.shape[0] - 2 * PAD
    channels = held_ref.shape[1]
    ends = read_ends(info_ref)
    base = info_ref[8]
    source = act_any if stream_act else gradient_any
    act_ref, gradient_ref = (held_ref, gradient_any) if stream_act else (act_any, held_ref)
    inward_stream = Stream(source, held_ref, held_sems, PAD, PAD)
    edges = edge_copies(source, held_ref, edge_sems)
    for edge in edges:
        edge.start()
    inward_stream.start()
    out_ref[...] = jnp.zeros_like(out_ref)
    for edge in edges:
        edge.wait()
    inward_stream.tile(0).wait()

    def step(i, start):
        wait_next([inward_stream], i, frames)
        before, here, after = taps_of(gradient_ref, ends, start, base)
        act = act_ref[pl.ds(start + PAD, ROWS), :]
        for k, tap in enumerate((after, here, before)):
            out_ref[k * channels : (k + 1) * channels, :] += lax.dot_general(
                act, tap, (((0,), (0,)), ((), ())), preferred_element_type=F32
            )

    for_tiles(frames, step)
    write_halves(info_ref, 0, out_ref, keep_ref, give_ref)


def write_halves(info_ref, bit, total_ref, keep_ref, give_ref):
    half = keep_ref.shape[0]
    mine = info_ref[BITS_AT + bit]
    keep_ref[...] = total_ref[pl.ds(pl.multiple_of(mine * half, PAD), half), :]
    give_ref[...] = total_ref[pl.ds(pl.multiple_of((1 - mine) * half, PAD), half), :].astype(BF16)


def halves_kernel(bits, info_ref, *refs):
    count = len(bits)
    inputs, outputs, totals = refs[: 2 * count], refs[2 * count : 4 * count], refs[4 * count :]
    for k, bit in enumerate(bits):
        totals[k][...] = inputs[2 * k][...] + inputs[2 * k + 1][...].astype(F32)
        write_halves(info_ref, bit, totals[k], outputs[2 * k], outputs[2 * k + 1])


def join_kernel(bits, info_ref, *refs):
    count = len(bits)
    for k, bit in enumerate(bits):
        part_ref, other_ref, out_ref = refs[2 * k], refs[2 * k + 1], refs[2 * count + k]
        half = part_ref.shape[0]
        mine = info_ref[BITS_AT + bit]
        out_ref[pl.ds(pl.multiple_of(mine * half, PAD), half), :] = part_ref[...]
        out_ref[pl.ds(pl.multiple_of((1 - mine) * half, PAD), half), :] = other_ref[...]


def block_order(order):
    places = []
    for index in range(1 << (len(order) + 1)):
        source, joined = index & 1, 0
        for at, bit in enumerate(order):
            source = 2 * source + ((index >> bit) & 1)
            joined += ((index >> bit) & 1) << at
        places.append((index & 1, source, joined))
    return places


def final_kernel(
    orders,
    rows,
    info_ref,
    second_ref,
    second_other_ref,
    first_ref,
    first_other_ref,
    second_out_ref,
    first_out_ref,
    first_affine_ref,
    first_shift_ref,
    second_affine_ref,
    second_shift_ref,
    bias_ref,
):
    channels = second_ref.shape[1]
    mine = info_ref[BITS_AT]
    gathered = []
    pairs = (
        (second_ref, second_other_ref, second_out_ref, rows + SMALL_ROWS),
        (first_ref, first_other_ref, first_out_ref, rows),
    )
    for k, (part_ref, other_ref, out_ref, step) in enumerate(pairs):
        for core, source, joined in block_order(orders[k]):
            here = pl.ds(joined * step, step)
            block = jnp.where(
                mine == core, part_ref[here, :].astype(F32), other_ref[here, :].astype(F32)
            )
            out_ref[source * rows : (source + 1) * rows, :] = block[:rows]
            if k == 0:
                gathered.append(block[rows:])
    styles = jnp.concatenate([block[32:40, 0:128] for block in gathered], axis=0)
    for at, (affine_ref, shift_ref) in enumerate(
        ((first_affine_ref, first_shift_ref), (second_affine_ref, second_shift_ref))
    ):
        for side in range(2):
            first = 16 * at + 8 * side
            sums = jnp.concatenate([block[first : first + 8] for block in gathered], axis=0)
            lanes = slice(side * channels, (side + 1) * channels)
            affine_ref[:, lanes] = lax.dot_general(
                styles, sums, (((0,), (0,)), ((), ())), precision=PRECISE
            )
            shift_ref[:, lanes] = jnp.sum(sums, axis=0, keepdims=True)
    biases = jnp.concatenate([block[40:48] for block in gathered], axis=0)
    bias_ref[...] = jnp.sum(biases, axis=0, keepdims=True)


def back_coefficients(own_ref, other_refs, inverse_ref, coef_ref, back_ref):
    inverse = inverse_ref[...]
    total = sum_over_tm(own_ref, other_refs, 0, 8)
    cross = sum_over_tm(own_ref, other_refs, 8, 8)
    scale = coef_ref[0:8, :] * coef_ref[16:24, :]
    back_ref[0:8, :] = total
    back_ref[8:16, :] = cross
    back_ref[16:24, :] = scale * total * inverse
    back_ref[24:32, :] = scale * cross * inverse
    back_ref[32:40, :] = scale


def inward(inner, unit, back_ref, u):
    return inner * row(back_ref, 32 + u) - row(back_ref, 16 + u) - unit * row(back_ref, 24 + u)


def first_back_kernel(
    info_ref,
    inner_hbm,
    unit_two_hbm,
    own_ref,
    one_ref,
    two_ref,
    three_ref,
    middle_one_ref,
    middle_three_ref,
    inverse_ref,
    coef_two_ref,
    coef_one_ref,
    unit_one_hbm,
    weight_ref,
    gradient_ref,
    out_hbm,
    back_ref,
    stat_ref,
    acc_ref,
    full_ref,
    inner_ref,
    unit_two_ref,
    unit_one_ref,
    out_ref,
    inner_sems,
    two_sems,
    one_sems,
    out_sems,
):
    frames, channels = unit_one_ref.shape
    early = [
        Stream(inner_hbm, inner_ref, inner_sems),
        Stream(unit_two_hbm, unit_two_ref, two_sems),
    ]
    late = Stream(unit_one_hbm, unit_one_ref, one_sems)
    outward = Stream(out_ref, out_hbm, out_sems)
    for stream in (*early, late):
        stream.start()
    ends = read_ends(info_ref)
    base = info_ref[8]
    back_coefficients(own_ref, (one_ref, two_ref, three_ref), inverse_ref, coef_two_ref, back_ref)
    acc_ref[...] = jnp.zeros_like(acc_ref)
    owner_before, owner_after = halo_owner(info_ref, ends, base, frames)
    edge_rows(
        gradient_ref,
        inward(
            row(one_ref, LAST_ROW),
            unit_of(row(middle_one_ref, LAST_ROW), coef_two_ref, owner_before),
            back_ref,
            owner_before,
        ),
        inward(
            row(three_ref, FIRST_ROW),
            unit_of(row(middle_three_ref, FIRST_ROW), coef_two_ref, owner_after),
            back_ref,
            owner_after,
        ),
    )

    def back_step(start):
        here = pl.ds(start, BLOCK)
        there = pl.ds(start + PAD, BLOCK)

        def now(u):
            return inward(
                inner_ref[here, :].astype(F32), unit_two_ref[here, :].astype(F32), back_ref, u
            )

        def uniform(u):
            gradient_ref[there, :] = now(u).astype(BF16)

        def mixed(u, mask):
            old = gradient_ref[there, :].astype(F32)
            gradient_ref[there, :] = jnp.where(mask((BLOCK, channels)), now(u), old).astype(BF16)

        by_utterance(ends, base + start, BLOCK, uniform, mixed)

    def back_tile(i, start):
        for stream in early:
            stream.tile(i).wait()
        for_blocks(start, ROWS, BLOCK, back_step)

    for_tiles(frames, back_tile)

    def slope_step(start, row_start):
        here = pl.ds(start, BLOCK)

        def parts(u):
            unit = unit_one_ref[here, :].astype(F32)
            _, inner, cross = slope_and_sums(
                full_ref[pl.ds(row_start, BLOCK), :], unit, coef_one_ref, u
            )
            return inner, cross

        def uniform(u):
            inner, cross = parts(u)
            out_ref[here, :] = inner.astype(BF16)
            add_stats(acc_ref, u, inner, cross)

        def mixed(u, mask):
            keep = mask((BLOCK, channels))
            inner, cross = parts(u)
            old = out_ref[here, :].astype(F32)
            out_ref[here, :] = jnp.where(keep, inner, old).astype(BF16)
            add_stats(acc_ref, u, jnp.where(keep, inner, 0.0), jnp.where(keep, cross, 0.0))

        by_utterance(ends, base + start, BLOCK, uniform, mixed)

    def conv(i, start):
        late.tile(i).wait()
        before, here, after = taps_of(gradient_ref, ends, start, base)
        full_ref[...] = convolved((after, here, before), weight_ref)
        for_blocks(0, ROWS, BLOCK, lambda inside: slope_step(start + inside, inside))
        outward.tile(i).start()

    for_tiles(frames, conv)
    finish_stats(acc_ref, stat_ref)
    outward.finish()


def buffer_gradient_kernel(
    info_ref,
    offset_ref,
    inner_hbm,
    unit_hbm,
    cot_hbm,
    wide_hbm,
    own_ref,
    one_ref,
    two_ref,
    three_ref,
    inverse_ref,
    coef_ref,
    before_ref,
    out_ref,
    after_ref,
    back_ref,
    free_ref,
    up_ref,
    total_ref,
    inner_ref,
    unit_ref,
    cot_ref,
    wide_ref,
    inner_sems,
    unit_sems,
    cot_sems,
    wide_sems,
):
    frames, channels = unit_ref.shape
    streams = [
        Stream(inner_hbm, inner_ref, inner_sems),
        Stream(unit_hbm, unit_ref, unit_sems),
        Stream(cot_hbm, cot_ref, cot_sems),
        Stream(wide_hbm, wide_ref, wide_sems),
    ]
    for index in range(frames // ROWS):
        for stream in streams:
            stream.tile(index).start()
    tiles = offset_ref.shape[0]
    rows = frames // tiles
    halo, own = before_ref.shape[0], out_ref.shape[0]
    ends = read_ends(info_ref)
    base, slot_base = info_ref[8], info_ref[9]
    back_coefficients(own_ref, (one_ref, two_ref, three_ref), inverse_ref, coef_ref, back_ref)
    total_ref[...] = jnp.zeros_like(total_ref)
    span = rows + PAD

    def up_step(start):
        here = pl.ds(start, BLOCK)

        def upward(u):
            lead = cot_ref[here, :].astype(F32) * ROOT_HALF
            return lead + inward(
                inner_ref[here, :].astype(F32), unit_ref[here, :].astype(F32), back_ref, u
            )

        def uniform(u):
            up_ref[here, :] = upward(u).astype(BF16)

        def mixed(u, mask):
            old = up_ref[here, :].astype(F32)
            up_ref[here, :] = jnp.where(mask((BLOCK, channels)), upward(u), old).astype(BF16)

        by_utterance(ends, base + start, BLOCK, uniform, mixed)

    def step(i):
        start = pl.multiple_of(i * rows, rows)
        here = pl.ds(start, rows)
        shift = offset_ref[i] - slot_base
        aligned = pl.multiple_of((shift // PAD) * PAD, PAD)
        part = lax.dot_general(
            wide_ref[here, :], up_ref[here, :], (((0,), (0,)), ((), ())), preferred_element_type=F32
        )
        total_ref[pl.ds(aligned, span), :] += part[0:span]

    def blocks(i, start):
        for stream in streams:
            stream.tile(i).wait()
        for_blocks(start, ROWS, BLOCK, up_step)
        each = ROWS // rows

        def four(k, carry):
            for n in range(4):
                step(i * each + k * 4 + n)
            return carry

        lax.fori_loop(0, each // 4, four, 0)

    for_tiles(frames, blocks)
    before_ref[...] = total_ref[0:halo, :]
    out_ref[...] = total_ref[halo : halo + own, :]
    after_ref[...] = total_ref[halo + own : 2 * halo + own, :]
    groups, copies, half = free_ref.shape[:3]
    for s in range(groups):
        first = halo + (2 * s + (1 if s < groups // 2 else 0)) * half
        rows_out = total_ref[first : first + half, :].astype(BF16)
        for t in range(copies):
            free_ref[s, t] = rows_out


def scatter_kernel(late, info_ref, order_ref, part_ref, *refs):
    out_ref, tmp_ref = refs[-2], refs[-1]
    blocks, half, channels = part_ref.shape
    lanes = channels // 128
    offset = jnp.where(info_ref[11] == 1 - late, half, 0)
    for old_ref in refs[:-2]:

        def copy(start, old_ref=old_ref):
            out_ref[pl.ds(start, ROWS), :] = old_ref[pl.ds(start, ROWS), :]

        for_blocks(0, out_ref.shape[0], ROWS, copy)

    def body(block, carry):
        for b in range(half // 16):
            both = part_ref[block, b * 16 : b * 16 + 16, :].astype(F32)
            for h in range(2):
                for q in range(lanes):
                    tmp_ref[pl.ds(((2 * b + h) * lanes + q) * 8, 8), :] = both[
                        8 * h : 8 * h + 8, q * 128 : (q + 1) * 128
                    ]
        first = block * 2 * half + offset
        for r in range(half):
            to = order_ref[first + r]
            out_ref[pl.ds((to >> 3) * (8 * lanes) + (to & 7), lanes, stride=8), :] = tmp_ref[
                pl.ds((r // 8) * 8 * lanes + r % 8, lanes, stride=8), :
            ]
        return carry

    lax.fori_loop(0, blocks, body, 0)


VM = pl.BlockSpec(memory_space=pltpu.VMEM)
SM = pl.BlockSpec(memory_space=pltpu.SMEM)


HB = pl.BlockSpec(memory_space=pltpu.HBM)


def call(kernel, inputs, outputs, scratch, flops, limit):
    return pl.pallas_call(
        kernel,
        in_specs=[spec for _, spec in inputs],
        out_specs=tuple(spec for _, _, spec in outputs),
        out_shape=tuple(
            pltpu.HBM(shape, dtype) if spec is HB else jax.ShapeDtypeStruct(shape, dtype)
            for shape, dtype, spec in outputs
        ),
        scratch_shapes=[
            pltpu.SemaphoreType.DMA((one,)) if isinstance(one, int) else pltpu.VMEM(*one)
            for one in scratch
        ],
        compiler_params=pltpu.CompilerParams(vmem_limit_bytes=limit * MIB),
        cost_estimate=pl.CostEstimate(flops=flops, bytes_accessed=flops // 200, transcendentals=0),
    )(
        *(
            pltpu.with_memory_space_constraint(array, pltpu.HBM) if spec is HB else array
            for array, spec in inputs
        )
    )


def scattered(old, part, late, info, order):
    half, channels = part.shape[1:]
    lanes = channels // 128
    kept = [] if old is None else [old]
    return pl.pallas_call(
        functools.partial(scatter_kernel, late),
        in_specs=[SM, SM] + [VM] * (1 + len(kept)),
        out_specs=VM,
        out_shape=jax.ShapeDtypeStruct((order.shape[0] * lanes, 128), F32),
        scratch_shapes=[pltpu.VMEM((half * lanes, 128), F32)],
        input_output_aliases={3: 0} if kept else {},
        compiler_params=pltpu.CompilerParams(vmem_limit_bytes=22 * MIB),
        cost_estimate=pl.CostEstimate(flops=10**6, bytes_accessed=10**4, transcendentals=0),
    )(info, order, part, *kept)


def shifted(values, axis, step):
    devices = lax.axis_size(axis)
    return lax.ppermute(values, axis, [(i, (i + step) % devices) for i in range(devices)])


def others_over_tm(values):
    return [shifted(values, "tm", d) for d in (1, 2, 3)]


def from_neighbours(first_rows, last_rows):
    devices = lax.axis_size("tm")
    up = [(i, i + 1) for i in range(devices - 1)]
    down = [(i + 1, i) for i in range(devices - 1)]
    return lax.ppermute(last_rows, "tm", up), lax.ppermute(first_rows, "tm", down)


def swapped(values, bit):
    devices = lax.axis_size("seq")
    return lax.ppermute(values, "seq", [(i, i ^ (1 << bit)) for i in range(devices)])


def after(values, *others):
    return lax.optimization_barrier((values, others))[0]


def summed_over_tm(parts):
    copies, tm_index = lax.axis_size("tm"), lax.axis_index("tm")
    rows, channels = parts[0].shape
    pieces = jnp.stack(parts).reshape(len(parts), copies, rows // copies, channels)
    part = lax.dynamic_index_in_dim(pieces, tm_index, 1, False)
    sent = pieces.astype(BF16)
    for step in (1, 3, 2):
        give = lax.dynamic_index_in_dim(sent, (tm_index + step) % copies, 1, False)
        part = part + shifted(give, "tm", step).astype(F32)
    return part.astype(BF16)


def gathered_over_tm(part):
    copies, tm_index = lax.axis_size("tm"), lax.axis_index("tm")
    count, rows, channels = part.shape
    every = jnp.zeros((count, copies, rows, channels), BF16)
    every = lax.dynamic_update_index_in_dim(every, part, tm_index, 1)
    for step in (1, 3, 2):
        every = lax.dynamic_update_index_in_dim(
            every, shifted(part, "tm", step), (tm_index - step) % copies, 1
        )
    return every.reshape(count, copies * rows, channels)


def on_device(
    phonemes,
    send_order,
    phoneme_counts,
    frame_lengths,
    tile_offsets,
    alignment,
    style_vec,
    first_affine_weight,
    first_affine_bias,
    first_conv_weight,
    second_affine_weight,
    second_affine_bias,
    second_conv_weight,
    second_conv_bias,
    cotangent,
):
    frames, channels = cotangent.shape
    slot_count = phonemes.shape[0]
    groups = lax.axis_size("seq")
    copies = lax.axis_size("tm")
    seq_index, tm_index = lax.axis_index("seq"), lax.axis_index("tm")
    piece_rows = slot_count // groups // copies
    local_rows = slot_count // copies
    tiles = tile_offsets.shape[0]
    window = alignment.shape[1]
    halo = window // 2
    lengths = frame_lengths[0]
    conv_flops = 2 * frames * 3 * channels * channels

    info = jnp.concatenate(
        [
            jnp.cumsum(lengths),
            jnp.cumsum(phoneme_counts[0]),
            (tm_index * frames)[None],
            (tm_index * local_rows - halo)[None],
            tm_index[None],
            (seq_index < groups // 2)[None].astype(I32),
            (seq_index[None] >> jnp.arange(12, dtype=I32)) & 1,
        ]
    ).astype(I32)
    inverse = jnp.zeros((8, channels), F32).at[0:UTTS].set(
        jnp.broadcast_to(1.0 / lengths.astype(F32)[:, None], (UTTS, channels))
    )
    style_rows = jnp.zeros((8, style_vec.shape[1]), BF16).at[0:UTTS].set(style_vec)
    params_one = jnp.dot(style_rows, first_affine_weight, preferred_element_type=F32) + (
        first_affine_bias.astype(F32)
    )
    params_two = jnp.dot(style_rows, second_affine_weight, preferred_element_type=F32) + (
        second_affine_bias.astype(F32)
    )

    def turned(weight):
        return (
            weight.reshape(3, channels, channels).transpose(0, 2, 1).reshape(3 * channels, channels)
        )

    tiles_of = frames // ROWS
    full, padded = (frames, channels), (frames + 2 * PAD, channels)
    stats_shape, coef_shape = (STAT_ROWS, channels), (32, channels)
    small_acc = ((ACC_ROWS, channels), F32)

    cot_before, cot_after = from_neighbours(cotangent[:1], cotangent[-1:])
    order = send_order[0].reshape(groups, copies, piece_rows)
    mine = lax.dynamic_index_in_dim(order, tm_index, 1, False)
    outgoing = jnp.take(phonemes, mine.reshape(-1), axis=0, mode="clip")
    outgoing = after(outgoing, cot_before, cot_after)
    received = lax.all_to_all(
        outgoing.reshape(groups, piece_rows, channels), "seq", 0, 0, tiled=True
    ).reshape(local_rows, channels)

    grad_act_two, grad_branch, bias_part = call(
        gradient_kernel,
        (
            (info, SM),
            (cotangent, HB),
            (cot_before, VM),
            (cot_after, VM),
            (turned(second_conv_weight), VM),
        ),
        ((full, BF16, HB), (padded, BF16, HB), ((8, channels), F32, VM)),
        [(full, BF16), (padded, BF16), (full, BF16), tiles_of, tiles_of, 2, tiles_of],
        conv_flops,
        24,
    )

    received, bias_part = lax.optimization_barrier((received, bias_part))
    slots_before, slots_after = from_neighbours(received[:halo], received[-halo:])
    upsampled, upsampled_far, wide, stat = call(
        upsample_kernel,
        (
            (info, SM),
            (tile_offsets, SM),
            (slots_before, VM),
            (received, VM),
            (slots_after, VM),
            (alignment, HB),
            (bias_part, VM),
        ),
        (
            (full, F32, VM),
            (full, F32, HB),
            ((frames, WIDE), BF16, HB),
            (stats_shape, F32, VM),
        ),
        [
            ((local_rows + WIDE, channels), BF16),
            small_acc,
            ((frames, window), BF16),
            ((frames, WIDE), BF16),
            tiles_of,
            tiles_of,
            tiles_of,
        ],
        2 * frames * WIDE * channels,
        12,
    )
    others = others_over_tm(stat)
    bias_total = (stat[EXTRA_ROW] + others[1][EXTRA_ROW]) + (
        others[0][EXTRA_ROW] + others[2][EXTRA_ROW]
    )

    act_one, middle, unit_one, coef_one, stat_two = call(
        first_conv_kernel,
        (
            (info, SM),
            (upsampled, VM),
            *((one, VM) for one in (stat, *others)),
            (inverse, VM),
            (params_one, VM),
            (first_conv_weight, VM),
        ),
        (
            (padded, BF16, HB),
            (full, F32, VM),
            (full, BF16, HB),
            (coef_shape, F32, VM),
            (stats_shape, F32, VM),
        ),
        [small_acc, (padded, BF16), (full, BF16), tiles_of, 2, tiles_of],
        conv_flops,
        20,
    )
    others_two = others_over_tm(stat_two)

    act_two, act_two_far, inner_two, unit_two, coef_two, stat_three = call(
        second_norm_kernel,
        (
            (info, SM),
            (grad_act_two, HB),
            (middle, VM),
            *((one, VM) for one in (stat_two, *others_two)),
            (inverse, VM),
            (params_two, VM),
        ),
        (
            (padded, BF16, VM),
            (padded, BF16, HB),
            (full, BF16, HB),
            (full, BF16, HB),
            (coef_shape, F32, VM),
            (stats_shape, F32, VM),
        ),
        [
            small_acc,
            (full, BF16),
            (full, BF16),
            (full, BF16),
            tiles_of,
            tiles_of,
            2,
            tiles_of,
            tiles_of,
        ],
        2 * frames * channels * 100,
        20,
    )
    others_three = others_over_tm(stat_three)
    second_keep, second_give = call(
        functools.partial(weight_gradient_kernel, False),
        ((info, SM), (after(act_two, others_three[0]), VM), (grad_branch, HB)),
        (((3 * channels // 2, channels), F32, VM), ((3 * channels // 2, channels), BF16, VM)),
        [((3 * channels, channels), F32), (padded, BF16), tiles_of, 2],
        conv_flops,
        16,
    )

    grad_middle, inner_one, back_two, stat_four = call(
        first_back_kernel,
        (
            (info, SM),
            (inner_two, HB),
            (unit_two, HB),
            *((one, VM) for one in (stat_three, *others_three)),
            (others_two[0], VM),
            (others_two[2], VM),
            (inverse, VM),
            (coef_two, VM),
            (coef_one, VM),
            (unit_one, HB),
            (turned(first_conv_weight), VM),
        ),
        (
            (padded, BF16, VM),
            (full, BF16, HB),
            ((40, channels), F32, VM),
            (stats_shape, F32, VM),
        ),
        [
            small_acc,
            ((ROWS, channels), F32),
            *([(full, BF16)] * 4),
            *([tiles_of] * 4),
        ],
        conv_flops,
        28,
    )
    others_four = others_over_tm(stat_four)
    first_keep, first_give = call(
        functools.partial(weight_gradient_kernel, True),
        ((info, SM), (act_one, HB), (after(grad_middle, others_four[0]), VM)),
        (((3 * channels // 2, channels), F32, VM), ((3 * channels // 2, channels), BF16, VM)),
        [((3 * channels, channels), F32), (padded, BF16), tiles_of, 2],
        conv_flops,
        16,
    )

    grad_before, grad_own, grad_after, back_one, free_rows = call(
        buffer_gradient_kernel,
        (
            (info, SM),
            (tile_offsets, SM),
            (inner_one, HB),
            (unit_one, HB),
            (cotangent, HB),
            (wide, HB),
            *((one, VM) for one in (stat_four, *others_four)),
            (inverse, VM),
            (coef_one, VM),
        ),
        (
            ((halo, channels), F32, VM),
            ((local_rows, channels), F32, VM),
            ((halo, channels), F32, VM),
            ((40, channels), F32, VM),
            ((groups, copies, piece_rows // 2, channels), BF16, VM),
        ),
        [
            (full, BF16),
            ((local_rows + WIDE, channels), F32),
            *([(full, BF16)] * 3),
            ((frames, WIDE), BF16),
            *([tiles_of] * 4),
        ],
        2 * frames * WIDE * channels,
        28,
    )

    def sent_back(rows):
        rows = rows.reshape(groups * copies, half, channels)
        return lax.all_to_all(rows, ("seq", "tm"), 0, 0, tiled=True)

    half = piece_rows // 2
    from_before, from_after = from_neighbours(grad_before, grad_after)
    if half >= halo:
        split = grad_own.reshape(groups, 2, half, channels)
        late_rows = jnp.concatenate([split[: groups // 2, 0], split[groups // 2 :, 1]], axis=0)
        late_rows = (
            late_rows.at[0, :halo].add(from_before).at[groups - 1, half - halo :].add(from_after)
        ).astype(BF16)
    else:
        own = grad_own.at[:halo].add(from_before).at[local_rows - halo :].add(from_after)
        split = own.astype(BF16).reshape(groups, 2, half, channels)
        free_rows = jnp.concatenate([split[: groups // 2, 1], split[groups // 2 :, 0]], axis=0)
        free_rows = jnp.broadcast_to(free_rows[:, None], (groups, copies, half, channels))
        late_rows = jnp.concatenate([split[: groups // 2, 0], split[groups // 2 :, 1]], axis=0)
    late_rows = jnp.broadcast_to(late_rows[:, None], (groups, copies, half, channels))
    first_chunk = sent_back(free_rows)

    bits = [b for b in range(12) if (1 << b) < groups]
    orders = (bits[1:], bits[1:][::-1])
    keeps = [second_keep, first_keep]
    gives = after([second_give, first_give], back_one)
    gots = [swapped(give, bits[0]) for give in gives]
    for pair in zip(*orders):
        count = keeps[0].shape[0] // 2
        out = call(
            functools.partial(halves_kernel, pair),
            ((info, SM), *((one, VM) for both in zip(keeps, gots) for one in both)),
            (((count, channels), F32, VM), ((count, channels), BF16, VM)) * 2,
            [((2 * count, channels), F32)] * 2,
            10**6,
            8,
        )
        keeps, gives = [out[0], out[2]], [out[1], out[3]]
        gots = [swapped(give, bit) for give, bit in zip(gives, pair)]
    row_sums = [keep + got.astype(F32) for keep, got in zip(keeps, gots)]
    act_two_far, _ = lax.optimization_barrier((act_two_far, back_one))
    (frames_out,) = call(
        second_conv_kernel,
        (
            (info, SM),
            (act_two_far, HB),
            (upsampled_far, HB),
            (second_conv_weight, VM),
            (second_conv_bias[None], VM),
        ),
        ((full, BF16, HB),),
        [(padded, BF16), (full, F32), (full, BF16), tiles_of, 2, tiles_of, tiles_of],
        10**6,
        28,
    )

    row_sums, first_chunk, frames_out = lax.optimization_barrier((row_sums, first_chunk, frames_out))
    sums = gathered_over_tm(summed_over_tm(row_sums))
    late_rows, sums, first_chunk = lax.optimization_barrier((late_rows, sums, first_chunk))
    second_chunk = sent_back(late_rows)
    placed = scattered(None, first_chunk, 0, info, send_order[0])

    params_grad = [
        jnp.concatenate([back[8 : 8 + UTTS], back[0:UTTS]], axis=1) for back in (back_one, back_two)
    ]
    style_grad = jnp.dot(
        params_grad[0], first_affine_weight.astype(F32).T, precision=PRECISE
    ) + jnp.dot(params_grad[1], second_affine_weight.astype(F32).T, precision=PRECISE)
    style_block = jnp.zeros((8, channels), BF16).at[:, : style_rows.shape[1]].set(style_rows)
    small = jnp.concatenate(
        [
            back_one[8:16].astype(BF16),
            back_one[0:8].astype(BF16),
            back_two[8:16].astype(BF16),
            back_two[0:8].astype(BF16),
            style_block,
            jnp.zeros((8, channels), BF16).at[0].set(bias_total.astype(BF16)),
        ]
    )
    rows = sums.shape[1]
    held = [jnp.concatenate([sums[0], small]), sums[1]]
    for pair in zip(*orders):
        others = [swapped(one, bit) for one, bit in zip(held, pair)]
        held = call(
            functools.partial(join_kernel, pair),
            ((info, SM), *((one, VM) for both in zip(held, others) for one in both)),
            tuple(((2 * one.shape[0], channels), BF16, VM) for one in held),
            [],
            10**6,
            8,
        )
    others = [swapped(one, bits[0]) for one in held]
    (
        second_conv_grad,
        first_conv_grad,
        first_affine_grad,
        first_shift_grad,
        second_affine_grad,
        second_shift_grad,
        second_bias_grad,
    ) = call(
        functools.partial(final_kernel, orders, rows),
        (
            (info, SM),
            (held[0], VM),
            (others[0], VM),
            (held[1], VM),
            (others[1], VM),
        ),
        (
            ((3 * channels, channels), F32, VM),
            ((3 * channels, channels), F32, VM),
            *(
                (((style_vec.shape[1], 2 * channels), F32, VM), ((1, 2 * channels), F32, VM)) * 2
            ),
            ((1, channels), F32, VM),
        ),
        [],
        10**6,
        20,
    )
    placed = scattered(placed, second_chunk, 1, info, send_order[0])
    lanes = channels // 128
    phonemes_grad = (
        placed.reshape(slot_count // 8, lanes, 8, 128)
        .transpose(0, 2, 1, 3)
        .reshape(slot_count, channels)
    )
    return (
        frames_out,
        phonemes_grad,
        style_grad,
        first_affine_grad,
        first_shift_grad[0],
        first_conv_grad,
        second_affine_grad,
        second_shift_grad[0],
        second_conv_grad,
        second_bias_grad[0],
    )


def solution(mesh):
    split, whole = ("seq", "tm"), P()
    in_specs = (
        P("seq", None),
        P("seq", None),
        P("seq", None),
        P("seq", None),
        P(split),
        P(split, None),
        P("seq", None),
        *([whole] * 7),
        P(split, None),
    )
    out_specs = (P(split, None), P("seq", None), P("seq", None), *([whole] * 7))
    return jax.shard_map(
        on_device, mesh=mesh, in_specs=in_specs, out_specs=out_specs, check_vma=False
    )
```

```python
import functools

import jax
import jax.numpy as jnp
from jax import lax
from jax.experimental import pallas as pl
from jax.experimental.pallas import tpu as pltpu
from jax.sharding import PartitionSpec as P

EPSILON = 1e-05
ROOT_HALF = 0.7071067811865476
PRECISE = lax.Precision.HIGHEST
F32, BF16, I32 = jnp.float32, jnp.bfloat16, jnp.int32
UTTS = 4
PAD = 16
ROWS = 1024
BLOCK = 128
WIDE = 256
MIB = 2**20

STAT_ROWS = 24
FIRST_ROW, LAST_ROW, EXTRA_ROW, FIRST_GRAD, LAST_GRAD = 16, 17, 18, 19, 20
SMALL_ROWS = 48
BITS_AT = 12


def owner_at(ends, position):
    return sum((position >= end).astype(I32) for end in ends)


def tile_of(ref, index, offset=0):
    return ref.at[pl.ds(pl.multiple_of(offset + index * ROWS, PAD), ROWS), :]


class Stream:
    def __init__(self, source, target, sems, source_offset=0, target_offset=0):
        self.ends = (source, source_offset, target, target_offset)
        self.sems = sems
        self.tiles = sems.shape[0]

    def tile(self, index):
        source, source_offset, target, target_offset = self.ends
        return pltpu.make_async_copy(
            tile_of(source, index, source_offset),
            tile_of(target, index, target_offset),
            self.sems.at[index],
        )

    def start(self):
        for index in range(self.tiles):
            self.tile(index).start()

    def finish(self):
        for index in range(self.tiles):
            self.tile(index).wait()


def edge_copies(source, target, sems):
    last = source.shape[0] - PAD
    return [
        pltpu.make_async_copy(
            source.at[pl.ds(at, PAD), :], target.at[pl.ds(at, PAD), :], sems.at[k]
        )
        for k, at in enumerate((0, last))
    ]


def rows_of(start, shape):
    return start + lax.broadcasted_iota(I32, shape, 0)


def fold_rows(values):
    return jnp.sum(values.reshape(values.shape[0] // 8, 8, values.shape[1]), axis=0)


def by_utterance(ends, start, count, uniform_body, mixed_body):
    low, high = owner_at(ends, start), owner_at(ends, start + count - 1)

    @pl.when(low == high)
    def _():
        uniform_body(low)

    @pl.when(low != high)
    def _():
        def step(u, carry):
            lower = jnp.int32(-1)
            upper = jnp.int32(2**30)
            for k in range(UTTS):
                lower = jnp.where(u == k + 1, ends[k], lower)
                upper = jnp.where(u == k, ends[k], upper)

            def mask(shape):
                rows = rows_of(start, shape)
                return (rows >= lower) & (rows < upper)

            mixed_body(u, mask)
            return carry

        lax.fori_loop(low, high + 1, step, 0)


class Blocks:
    def __init__(self, ends, base, channels):
        self.ends, self.base, self.channels = ends, base, channels

    def plain(self, start, body):
        for inside in range(0, ROWS, BLOCK):
            first = self.base + start + inside
            low = owner_at(self.ends, first)
            alone = (low == owner_at(self.ends, first + BLOCK - 1)).astype(F32)
            body(start + inside, low, alone)

    def mixed(self, start, body):
        def step(i, carry):
            at = pl.multiple_of(start + i * BLOCK, BLOCK)
            by_utterance(
                self.ends,
                self.base + at,
                BLOCK,
                lambda u: None,
                lambda u, mask: body(at, u, mask((BLOCK, self.channels))),
            )
            return carry

        low = owner_at(self.ends, self.base + start)

        @pl.when(low != owner_at(self.ends, self.base + start + ROWS - 1))
        def _():
            lax.fori_loop(0, ROWS // BLOCK, step, 0)


def row(ref, index):
    return ref[pl.ds(index, 1), :]


def logistic(values):
    return 0.5 * jnp.tanh(0.5 * values) + 0.5


def taps_of(padded_ref, ends, start, base):
    channels = padded_ref.shape[1]
    block = padded_ref[pl.ds(start, ROWS + 2 * PAD), :].astype(F32)
    positions = rows_of(base + start, (ROWS, channels))
    cut_left = positions == ends[0]
    cut_right = positions + 1 == ends[0]
    for end in ends[1:]:
        cut_left = cut_left | (positions == end)
        cut_right = cut_right | (positions + 1 == end)
    before = jnp.where(cut_left, 0.0, block[PAD - 1 : PAD - 1 + ROWS]).astype(BF16)
    after = jnp.where(cut_right, 0.0, block[PAD + 1 : PAD + 1 + ROWS]).astype(BF16)
    return before, padded_ref[pl.ds(start + PAD, ROWS), :], after


def convolved(taps, weight_ref):
    channels = weight_ref.shape[1]
    return sum(
        jnp.dot(tap, weight_ref[k * channels : (k + 1) * channels, :], preferred_element_type=F32)
        for k, tap in enumerate(taps)
    )


def for_blocks(first, count, size, body, unroll=1):
    def step(i, carry):
        body(pl.multiple_of(first + i * size, size))
        return carry

    lax.fori_loop(0, count // size, step, 0, unroll=unroll)


def for_tiles(count, body):
    def step(i, carry):
        body(i, pl.multiple_of(i * ROWS, ROWS))
        return carry

    lax.fori_loop(0, count // ROWS, step, 0)


def wait_next(streams, i, count):
    @pl.when(i + 1 < count // ROWS)
    def _():
        for stream in streams:
            stream.tile(i + 1).wait()


def sum_over_tm(own_ref, other_refs, first, count):
    one, two, three = other_refs
    part = pl.ds(first, count)
    return (own_ref[part, :] + two[part, :]) + (one[part, :] + three[part, :])


def finish_stats(acc_ref, stat_ref):
    for kind in range(2):
        for u in range(8):
            at = kind * 8 + u
            if u < UTTS:
                first = (kind * (UTTS + 1) + u) * 8
                stat_ref[at : at + 1, :] = jnp.sum(
                    acc_ref[first : first + 8, :], axis=0, keepdims=True
                )
            else:
                stat_ref[at : at + 1, :] = jnp.zeros_like(stat_ref[at : at + 1, :])
    stat_ref[16:24, :] = jnp.zeros_like(stat_ref[16:24, :])


ACC_ROWS = 2 * (UTTS + 1) * 8


def add_stats(acc_ref, u, first, second, weight=None):
    for kind, term in enumerate((first, second)):
        at = pl.ds(pl.multiple_of((kind * (UTTS + 1) + u) * 8, 8), 8)
        term = fold_rows(term)
        acc_ref[at, :] += term if weight is None else term * weight


def read_ends(info_ref):
    return [info_ref[k] for k in range(UTTS)]


def halo_owner(info_ref, ends, base, frames):
    before = jnp.where(base == 0, UTTS, owner_at(ends, base - 1))
    return before, owner_at(ends, base + frames)


def gradient_kernel(
    info_ref,
    cot_hbm,
    weight_ref,
    out_hbm,
    padded_hbm,
    bias_ref,
    cot_ref,
    padded_ref,
    out_ref,
    cot_sems,
    padded_sems,
    out_sems,
):
    frames, channels = cot_ref.shape
    ends = read_ends(info_ref)
    base = info_ref[8]
    cot_in = Stream(cot_hbm, cot_ref, cot_sems)
    padded_out = Stream(padded_ref, padded_hbm, padded_sems, PAD)
    outward = Stream(out_ref, out_hbm, out_sems)
    cot_in.start()
    padded_ref[0:PAD, :] = jnp.zeros((PAD, channels), BF16)
    padded_ref[PAD + frames :, :] = jnp.zeros((PAD, channels), BF16)
    bias_ref[...] = jnp.zeros_like(bias_ref)

    def scale(start):
        here = cot_ref[pl.ds(start, BLOCK), :].astype(F32) * ROOT_HALF
        here = jnp.where(rows_of(base + start, (BLOCK, channels)) < ends[UTTS - 1], here, 0.0)
        rounded = here.astype(BF16)
        padded_ref[pl.ds(start + PAD, BLOCK), :] = rounded
        bias_ref[0:8, :] += fold_rows(rounded.astype(F32))

    def scale_tile(i, start):
        cot_in.tile(i).wait()
        for_blocks(start, ROWS, BLOCK, scale)
        padded_out.tile(i).start()

    for_tiles(frames, scale_tile)

    def conv(i, start):
        before, here, after = taps_of(padded_ref, ends, start, base)
        total = convolved((after, here, before), weight_ref)
        out_ref[pl.ds(start, ROWS), :] = total.astype(BF16)
        outward.tile(i).start()

    for_tiles(frames, conv)
    bias_ref[8:9, :] = padded_ref[PAD : 2 * PAD, :].astype(F32)[0:1]
    bias_ref[9:10, :] = padded_ref[frames : frames + PAD, :].astype(F32)[PAD - 1 :]
    padded_out.finish()
    outward.finish()


def upsample_kernel(
    info_ref,
    offset_ref,
    before_ref,
    own_ref,
    after_ref,
    align_hbm,
    bias_ref,
    out_ref,
    out_hbm,
    wide_hbm,
    stat_ref,
    buffer_ref,
    acc_ref,
    align_ref,
    wide_ref,
    align_sems,
    out_sems,
    wide_sems,
):
    frames, channels = out_ref.shape
    align_in = Stream(align_hbm, align_ref, align_sems)
    outward = Stream(out_ref, out_hbm, out_sems)
    wide_out = Stream(wide_ref, wide_hbm, wide_sems)
    align_in.start()
    window = align_ref.shape[1]
    tiles = offset_ref.shape[0]
    rows = frames // tiles
    halo, own = before_ref.shape[0], own_ref.shape[0]
    ends = read_ends(info_ref)
    slot_ends = [info_ref[UTTS + k] for k in range(UTTS)]
    base, slot_base = info_ref[8], info_ref[9]
    buffer_ref[0:halo, :] = before_ref[...]
    buffer_ref[halo : halo + own, :] = own_ref[...]
    buffer_ref[halo + own : 2 * halo + own, :] = after_ref[...]
    buffer_ref[2 * halo + own :, :] = jnp.zeros_like(buffer_ref[2 * halo + own :, :])
    acc_ref[...] = jnp.zeros_like(acc_ref)

    def step(i):
        start = pl.multiple_of(i * rows, rows)
        shift = offset_ref[i] - slot_base
        aligned = pl.multiple_of((shift // PAD) * PAD, PAD)
        block = align_ref[pl.ds(start, rows), :].astype(F32)
        block = jnp.concatenate([block, jnp.zeros((rows, WIDE - window), F32)], axis=1)
        block = pltpu.roll(block, shift - aligned, 1)
        slots = slot_base + aligned + lax.broadcasted_iota(I32, (rows, WIDE), 1)
        slot_owner = owner_at(slot_ends, slots)
        frame_owner = owner_at(ends, rows_of(base + start, (rows, WIDE)))
        match = (slot_owner == frame_owner) & (frame_owner < UTTS)
        block = jnp.where(match, block, 0.0).astype(BF16)
        wide_ref[pl.ds(start, rows), :] = block
        out_ref[pl.ds(start, rows), :] = jnp.dot(
            block, buffer_ref[pl.ds(aligned, WIDE), :], preferred_element_type=F32
        )

    def blocks(i, start):
        align_in.tile(i).wait()
        each = ROWS // rows

        def four(k, carry):
            for n in range(4):
                step(i * each + k * 4 + n)
            return carry

        lax.fori_loop(0, each // 4, four, 0)
        outward.tile(i).start()
        wide_out.tile(i).start()
        for_blocks(
            start, ROWS, BLOCK, lambda at: value_sums(out_ref, acc_ref, ends, base, at)
        )

    for_tiles(frames, blocks)
    finish_stats(acc_ref, stat_ref)
    stat_ref[FIRST_ROW : FIRST_ROW + 1, :] = out_ref[0:1, :]
    stat_ref[LAST_ROW : LAST_ROW + 1, :] = out_ref[frames - 1 : frames, :]
    stat_ref[EXTRA_ROW : EXTRA_ROW + 1, :] = jnp.sum(bias_ref[0:8, :], axis=0, keepdims=True)
    stat_ref[FIRST_GRAD : FIRST_GRAD + 2, :] = bias_ref[8:10, :]
    outward.finish()
    wide_out.finish()


def value_sums(out_ref, acc_ref, ends, base, start):
    channels = out_ref.shape[1]

    def uniform(u):
        here = out_ref[pl.ds(start, BLOCK), :]
        add_stats(acc_ref, u, here, here * here)

    def mixed(u, mask):
        here = jnp.where(mask((BLOCK, channels)), out_ref[pl.ds(start, BLOCK), :], 0.0)
        add_stats(acc_ref, u, here, here * here)

    by_utterance(ends, base + start, BLOCK, uniform, mixed)


def write_coefficients(own_ref, other_refs, inverse_ref, params_ref, coef_ref):
    channels = inverse_ref.shape[1]
    inverse = inverse_ref[...]
    total = sum_over_tm(own_ref, other_refs, 0, 8)
    square = sum_over_tm(own_ref, other_refs, 8, 8)
    mean = total * inverse
    real = inverse > 0.0
    rstd = jnp.where(real, lax.rsqrt(square * inverse - mean * mean + EPSILON), 0.0)
    gain = jnp.where(real, 1.0 + params_ref[:, 0:channels], 0.0)
    shift = jnp.where(real, params_ref[:, channels : 2 * channels], 0.0)
    coef_ref[0:8, :] = rstd
    coef_ref[8:16, :] = mean * rstd
    coef_ref[16:24, :] = gain * rstd
    coef_ref[24:32, :] = 0.5 * gain
    coef_ref[32:40, :] = 0.5 * shift
    coef_ref[40:48, :] = 0.5 * gain * rstd
    coef_ref[48:56, :] = 0.5 * (shift - mean * gain * rstd)


UNIT, HALF_OF_UNIT, HALF_OF_VALUE = (0, 8), (24, 32), (40, 48)


def unit_of(values, coef_ref, u):
    return values * row(coef_ref, u) - row(coef_ref, 8 + u)


def half_normed(values, coef_ref, u, rows):
    return values * row(coef_ref, rows[0] + u) + row(coef_ref, rows[1] + u)


def twice_logistic(half):
    return jnp.tanh(half) + 1.0


def activation(values, coef_ref, u):
    half = half_normed(values, coef_ref, u, HALF_OF_VALUE)
    return half * twice_logistic(half)


def edge_rows(padded_ref, before, after):
    channels = padded_ref.shape[1]
    padded_ref[0:PAD, :] = jnp.broadcast_to(before, (PAD, channels)).astype(BF16)
    last = padded_ref.shape[0] - PAD
    padded_ref[last:, :] = jnp.broadcast_to(after, (PAD, channels)).astype(BF16)


def first_conv_kernel(
    info_ref,
    values_ref,
    own_ref,
    one_ref,
    two_ref,
    three_ref,
    inverse_ref,
    params_ref,
    weight_ref,
    turned_ref,
    act_hbm,
    out_ref,
    out_hbm,
    unit_hbm,
    coef_ref,
    stat_ref,
    edge_ref,
    added_ref,
    acc_ref,
    act_ref,
    unit_ref,
    act_sems,
    edge_sems,
    out_sems,
    unit_sems,
):
    frames, channels = values_ref.shape
    tiles = frames // ROWS
    act_out = Stream(act_ref, act_hbm, act_sems, PAD, PAD)
    unit_out = Stream(unit_ref, unit_hbm, unit_sems)
    outward = Stream(out_ref, out_hbm, out_sems)
    ends = read_ends(info_ref)
    base = info_ref[8]
    blocks = Blocks(ends, base, channels)
    write_coefficients(own_ref, (one_ref, two_ref, three_ref), inverse_ref, params_ref, coef_ref)
    acc_ref[...] = jnp.zeros_like(acc_ref)
    owner_before, owner_after = halo_owner(info_ref, ends, base, frames)
    edge_rows(
        act_ref,
        activation(row(one_ref, LAST_ROW), coef_ref, owner_before),
        activation(row(three_ref, FIRST_ROW), coef_ref, owner_after),
    )
    edges = edge_copies(act_ref, act_hbm, edge_sems)
    for edge in edges:
        edge.start()

    def act_parts(at, u):
        unit = unit_of(values_ref[pl.ds(at, BLOCK), :], coef_ref, u)
        half = half_normed(unit, coef_ref, u, HALF_OF_UNIT)
        return unit, half * twice_logistic(half)

    def act_plain(at, u, alone):
        unit, act = act_parts(at, u)
        unit_ref[pl.ds(at, BLOCK), :] = unit.astype(BF16)
        act_ref[pl.ds(at + PAD, BLOCK), :] = act.astype(BF16)

    def act_mixed(at, u, keep):
        here, there = pl.ds(at, BLOCK), pl.ds(at + PAD, BLOCK)
        unit, act = act_parts(at, u)
        unit_ref[here, :] = jnp.where(keep, unit, unit_ref[here, :].astype(F32)).astype(BF16)
        act_ref[there, :] = jnp.where(keep, act, act_ref[there, :].astype(F32)).astype(BF16)

    def sums_plain(at, u, alone):
        here = out_ref[pl.ds(at, BLOCK), :]
        add_stats(acc_ref, u, here, here * here, alone)

    def sums_mixed(at, u, keep):
        here = jnp.where(keep, out_ref[pl.ds(at, BLOCK), :], 0.0)
        add_stats(acc_ref, u, here, here * here)

    for turn in range(-1, tiles + 1):
        if turn + 1 < tiles:
            blocks.plain((turn + 1) * ROWS, act_plain)
        if 0 <= turn < tiles:
            start = turn * ROWS
            out_ref[start : start + ROWS, :] = convolved(
                taps_of(act_ref, ends, start, base), weight_ref
            )
        if turn > 0:
            blocks.plain((turn - 1) * ROWS, sums_plain)
        if turn + 1 < tiles:
            blocks.mixed((turn + 1) * ROWS, act_mixed)
            act_out.tile(turn + 1).start()
            unit_out.tile(turn + 1).start()
        if 0 <= turn < tiles:
            outward.tile(turn).start()
        if turn > 0:
            blocks.mixed((turn - 1) * ROWS, sums_mixed)
    edge_ref[...] = jnp.zeros_like(edge_ref)
    added_ref[...] = jnp.zeros_like(added_ref)
    neighbours = (
        (one_ref, LAST_GRAD, owner_before, owner_at(ends, base), 2 * channels),
        (three_ref, FIRST_GRAD, owner_after, owner_at(ends, base + frames - 1), 0),
    )
    for k, (ref, at, theirs, ours, tap) in enumerate(neighbours):
        valid = (theirs == ours) & (ours < UTTS)
        edge_ref[k : k + 1, :] = jnp.where(valid, ref[at : at + 1, :], 0.0)
        rows = jnp.broadcast_to(edge_ref[k : k + 1, :], (PAD, channels)).astype(BF16)
        added_ref[k : k + 1, :] = jnp.dot(
            rows, turned_ref[tap : tap + channels, :], preferred_element_type=F32
        )[0:1]
    finish_stats(acc_ref, stat_ref)
    stat_ref[FIRST_ROW : FIRST_ROW + 1, :] = out_ref[0:1, :]
    stat_ref[LAST_ROW : LAST_ROW + 1, :] = out_ref[frames - 1 : frames, :]
    act_out.finish()
    unit_out.finish()
    outward.finish()
    for edge in edges:
        edge.wait()


def slope_and_sums(gradient, values, coef_ref, u, rows):
    half = half_normed(values, coef_ref, u, rows)
    gate = twice_logistic(half)
    act = half * gate
    inner = gradient * (gate * (half - 0.5 * act + 0.5))
    return act, inner, inner * values


def second_norm_kernel(
    info_ref,
    gradient_hbm,
    values_ref,
    own_ref,
    one_ref,
    two_ref,
    three_ref,
    inverse_ref,
    params_ref,
    added_ref,
    act_hbm,
    inner_hbm,
    coef_ref,
    stat_ref,
    acc_ref,
    gradient_ref,
    act_ref,
    inner_ref,
    gradient_sems,
    act_sems,
    edge_sems,
    inner_sems,
):
    frames, channels = values_ref.shape
    gradient_in = Stream(gradient_hbm, gradient_ref, gradient_sems)
    outward = [
        Stream(act_ref, act_hbm, act_sems, PAD, PAD),
        Stream(inner_ref, inner_hbm, inner_sems),
    ]
    gradient_in.start()
    ends = read_ends(info_ref)
    base = info_ref[8]
    write_coefficients(own_ref, (one_ref, two_ref, three_ref), inverse_ref, params_ref, coef_ref)
    acc_ref[...] = jnp.zeros_like(acc_ref)
    owner_before, owner_after = halo_owner(info_ref, ends, base, frames)
    edge_rows(
        act_ref,
        activation(row(one_ref, LAST_ROW), coef_ref, owner_before),
        activation(row(three_ref, FIRST_ROW), coef_ref, owner_after),
    )

    edges = edge_copies(act_ref, act_hbm, edge_sems)
    for edge in edges:
        edge.start()

    def step(start):
        here = pl.ds(start, BLOCK)
        there = pl.ds(start + PAD, BLOCK)

        def parts(u):
            return slope_and_sums(
                gradient_ref[here, :].astype(F32), values_ref[here, :], coef_ref, u, HALF_OF_VALUE
            )

        def uniform(u):
            act, inner, cross = parts(u)
            act_ref[there, :] = act.astype(BF16)
            inner_ref[here, :] = inner.astype(BF16)
            add_stats(acc_ref, u, inner, cross)

        def mixed(u, mask):
            keep = mask((BLOCK, channels))
            act, inner, cross = parts(u)
            act_ref[there, :] = jnp.where(keep, act, act_ref[there, :].astype(F32)).astype(BF16)
            old = inner_ref[here, :].astype(F32)
            inner_ref[here, :] = jnp.where(keep, inner, old).astype(BF16)
            add_stats(acc_ref, u, jnp.where(keep, inner, 0.0), jnp.where(keep, cross, 0.0))

        by_utterance(ends, base + start, BLOCK, uniform, mixed)

    def tile(i, start):
        gradient_in.tile(i).wait()
        for k, at in enumerate((0, frames - PAD)):

            @pl.when(i == at // ROWS)
            def _(k=k, at=at):
                edge = gradient_ref[at : at + PAD, :].astype(F32)
                inside = rows_of(0, (PAD, channels)) == k * (PAD - 1)
                edge = edge + jnp.where(inside, added_ref[k : k + 1, :], 0.0)
                gradient_ref[at : at + PAD, :] = edge.astype(BF16)

        for_blocks(start, ROWS, BLOCK, step)
        for stream in outward:
            stream.tile(i).start()

    for_tiles(frames, tile)
    finish_stats(acc_ref, stat_ref)
    stat_ref[FIRST_ROW : FIRST_ROW + 1, :] = inner_ref[0:PAD, :].astype(F32)[0:1]
    stat_ref[LAST_ROW : LAST_ROW + 1, :] = inner_ref[frames - PAD :, :].astype(F32)[PAD - 1 :]
    for stream in outward:
        stream.finish()
    for edge in edges:
        edge.wait()


def second_conv_kernel(
    info_ref,
    act_hbm,
    values_hbm,
    weight_ref,
    bias_ref,
    out_hbm,
    act_ref,
    values_ref,
    out_ref,
    act_sems,
    edge_sems,
    values_sems,
    out_sems,
):
    frames, channels = values_ref.shape
    ends = read_ends(info_ref)
    base = info_ref[8]
    bias = bias_ref[...].astype(F32)
    act_in = Stream(act_hbm, act_ref, act_sems, PAD, PAD)
    values_in = Stream(values_hbm, values_ref, values_sems)
    outward = Stream(out_ref, out_hbm, out_sems)
    edges = edge_copies(act_hbm, act_ref, edge_sems)
    for edge in edges:
        edge.start()
    act_in.start()
    values_in.start()
    for edge in edges:
        edge.wait()
    act_in.tile(0).wait()

    def step(i, start):
        here = pl.ds(start, ROWS)
        wait_next([act_in], i, frames)
        values_in.tile(i).wait()
        branch = convolved(taps_of(act_ref, ends, start, base), weight_ref) + bias
        valid = rows_of(base + start, (ROWS, channels)) < ends[UTTS - 1]
        total = jnp.where(valid, (values_ref[here, :] + branch) * ROOT_HALF, 0.0)
        out_ref[here, :] = total.astype(BF16)
        outward.tile(i).start()

    for_tiles(frames, step)
    outward.finish()


def weight_gradient_kernel(
    info_ref,
    act_hbm,
    gradient_hbm,
    edge_ref,
    keep_ref,
    give_ref,
    out_ref,
    act_ref,
    gradient_ref,
    act_sems,
    gradient_sems,
):
    frames = act_ref.shape[0] - 2 * PAD
    channels = act_ref.shape[1]
    ends = read_ends(info_ref)
    base = info_ref[8]
    act_in = Stream(act_hbm, act_ref, act_sems, PAD, PAD)
    gradient_in = Stream(gradient_hbm, gradient_ref, gradient_sems, 0, PAD)
    for index in range(frames // ROWS):
        gradient_in.tile(index).start()
        act_in.tile(index).start()
    out_ref[...] = jnp.zeros_like(out_ref)
    edge_rows(gradient_ref, edge_ref[0:1, :], edge_ref[1:2, :])
    gradient_in.tile(0).wait()

    def step(i, start):
        wait_next([gradient_in], i, frames)
        act_in.tile(i).wait()
        before, here, after = taps_of(gradient_ref, ends, start, base)
        act = act_ref[pl.ds(start + PAD, ROWS), :]
        for k, tap in enumerate((after, here, before)):
            out_ref[k * channels : (k + 1) * channels, :] += lax.dot_general(
                act, tap, (((0,), (0,)), ((), ())), preferred_element_type=F32
            )

    for_tiles(frames, step)
    write_halves(info_ref, 0, out_ref, keep_ref, give_ref)


def write_halves(info_ref, bit, total_ref, keep_ref, give_ref):
    half = keep_ref.shape[0]
    mine = info_ref[BITS_AT + bit]
    keep_ref[...] = total_ref[pl.ds(pl.multiple_of(mine * half, PAD), half), :]
    give_ref[...] = total_ref[pl.ds(pl.multiple_of((1 - mine) * half, PAD), half), :].astype(BF16)


def halves_kernel(bits, info_ref, *refs):
    count = len(bits)
    inputs, outputs, totals = refs[: 2 * count], refs[2 * count : 4 * count], refs[4 * count :]
    for k, bit in enumerate(bits):
        totals[k][...] = inputs[2 * k][...] + inputs[2 * k + 1][...].astype(F32)
        write_halves(info_ref, bit, totals[k], outputs[2 * k], outputs[2 * k + 1])


def join_kernel(bits, info_ref, *refs):
    count = len(bits)
    for k, bit in enumerate(bits):
        part_ref, other_ref, out_ref = refs[2 * k], refs[2 * k + 1], refs[2 * count + k]
        half = part_ref.shape[0]
        mine = info_ref[BITS_AT + bit]
        out_ref[pl.ds(pl.multiple_of(mine * half, PAD), half), :] = part_ref[...]
        out_ref[pl.ds(pl.multiple_of((1 - mine) * half, PAD), half), :] = other_ref[...]


def block_order(order):
    places = []
    for index in range(1 << (len(order) + 1)):
        source, joined = index & 1, 0
        for at, bit in enumerate(order):
            source = 2 * source + ((index >> bit) & 1)
            joined += ((index >> bit) & 1) << at
        places.append((index & 1, source, joined))
    return places


def final_kernel(
    orders,
    rows,
    info_ref,
    second_ref,
    second_other_ref,
    first_ref,
    first_other_ref,
    second_out_ref,
    first_out_ref,
    first_affine_ref,
    first_shift_ref,
    second_affine_ref,
    second_shift_ref,
    bias_ref,
):
    channels = second_ref.shape[1]
    mine = info_ref[BITS_AT]
    gathered = []
    pairs = (
        (second_ref, second_other_ref, second_out_ref, rows + SMALL_ROWS),
        (first_ref, first_other_ref, first_out_ref, rows),
    )
    for k, (part_ref, other_ref, out_ref, step) in enumerate(pairs):
        for core, source, joined in block_order(orders[k]):
            here = pl.ds(joined * step, step)
            block = jnp.where(
                mine == core, part_ref[here, :].astype(F32), other_ref[here, :].astype(F32)
            )
            out_ref[source * rows : (source + 1) * rows, :] = block[:rows]
            if k == 0:
                gathered.append(block[rows:])
    styles = jnp.concatenate([block[32:40, 0:128] for block in gathered], axis=0)
    for at, (affine_ref, shift_ref) in enumerate(
        ((first_affine_ref, first_shift_ref), (second_affine_ref, second_shift_ref))
    ):
        for side in range(2):
            first = 16 * at + 8 * side
            sums = jnp.concatenate([block[first : first + 8] for block in gathered], axis=0)
            lanes = slice(side * channels, (side + 1) * channels)
            affine_ref[:, lanes] = lax.dot_general(
                styles, sums, (((0,), (0,)), ((), ())), precision=PRECISE
            )
            shift_ref[:, lanes] = jnp.sum(sums, axis=0, keepdims=True)
    biases = jnp.concatenate([block[40:48] for block in gathered], axis=0)
    bias_ref[...] = jnp.sum(biases, axis=0, keepdims=True)


def back_coefficients(own_ref, other_refs, inverse_ref, coef_ref, back_ref, of_values):
    inverse = inverse_ref[...]
    rstd, mean_rstd, scale = coef_ref[0:8, :], coef_ref[8:16, :], coef_ref[16:24, :]
    total = sum_over_tm(own_ref, other_refs, 0, 8)
    cross = sum_over_tm(own_ref, other_refs, 8, 8)
    if of_values:
        cross = rstd * cross - mean_rstd * total
    back_ref[0:8, :] = total
    back_ref[8:16, :] = cross
    slant = scale * cross * inverse
    back_ref[16:24, :] = scale * total * inverse - (mean_rstd * slant if of_values else 0.0)
    back_ref[24:32, :] = rstd * slant if of_values else slant
    back_ref[32:40, :] = scale


def inward(inner, values, back_ref, u):
    return inner * row(back_ref, 32 + u) - row(back_ref, 16 + u) - values * row(back_ref, 24 + u)


def first_back_kernel(
    info_ref,
    inner_hbm,
    middle_hbm,
    own_ref,
    one_ref,
    two_ref,
    three_ref,
    middle_one_ref,
    middle_three_ref,
    inverse_ref,
    coef_two_ref,
    coef_one_ref,
    unit_one_hbm,
    weight_ref,
    gradient_hbm,
    edge_ref,
    out_hbm,
    back_ref,
    stat_ref,
    acc_ref,
    full_ref,
    inner_ref,
    middle_ref,
    unit_one_ref,
    out_ref,
    gradient_ref,
    inner_sems,
    two_sems,
    one_sems,
    out_sems,
    gradient_sems,
):
    frames, channels = unit_one_ref.shape
    early = [
        Stream(inner_hbm, inner_ref, inner_sems),
        Stream(middle_hbm, middle_ref, two_sems),
    ]
    late = Stream(unit_one_hbm, unit_one_ref, one_sems)
    outward = Stream(out_ref, out_hbm, out_sems)
    gradient_out = Stream(gradient_ref, gradient_hbm, gradient_sems, PAD)
    for index in range(frames // ROWS):
        for stream in (*early, late):
            stream.tile(index).start()
    ends = read_ends(info_ref)
    base = info_ref[8]
    back_coefficients(own_ref, (one_ref, two_ref, three_ref), inverse_ref, coef_two_ref, back_ref, True)
    acc_ref[...] = jnp.zeros_like(acc_ref)
    owner_before, owner_after = halo_owner(info_ref, ends, base, frames)
    edge_rows(
        gradient_ref,
        inward(
            row(one_ref, LAST_ROW),
            row(middle_one_ref, LAST_ROW),
            back_ref,
            owner_before,
        ),
        inward(
            row(three_ref, FIRST_ROW),
            row(middle_three_ref, FIRST_ROW),
            back_ref,
            owner_after,
        ),
    )

    def back_step(start):
        here = pl.ds(start, BLOCK)
        there = pl.ds(start + PAD, BLOCK)

        def now(u):
            return inward(
                inner_ref[here, :].astype(F32), middle_ref[here, :], back_ref, u
            )

        def uniform(u):
            gradient_ref[there, :] = now(u).astype(BF16)

        def mixed(u, mask):
            old = gradient_ref[there, :].astype(F32)
            gradient_ref[there, :] = jnp.where(mask((BLOCK, channels)), now(u), old).astype(BF16)

        by_utterance(ends, base + start, BLOCK, uniform, mixed)

    edge_ref[0:8, :] = gradient_ref[0:PAD, :].astype(F32)[0:8]
    edge_ref[1:2, :] = gradient_ref[PAD + frames :, :].astype(F32)[0:1]

    def back_tile(i):
        for stream in early:
            stream.tile(i).wait()
        for_blocks(pl.multiple_of(i * ROWS, ROWS), ROWS, BLOCK, back_step)
        gradient_out.tile(i).start()

    back_tile(0)

    def slope_step(start, row_start):
        here = pl.ds(start, BLOCK)

        def parts(u):
            unit = unit_one_ref[here, :].astype(F32)
            _, inner, cross = slope_and_sums(
                full_ref[pl.ds(row_start, BLOCK), :], unit, coef_one_ref, u, HALF_OF_UNIT
            )
            return inner, cross

        def uniform(u):
            inner, cross = parts(u)
            out_ref[here, :] = inner.astype(BF16)
            add_stats(acc_ref, u, inner, cross)

        def mixed(u, mask):
            keep = mask((BLOCK, channels))
            inner, cross = parts(u)
            old = out_ref[here, :].astype(F32)
            out_ref[here, :] = jnp.where(keep, inner, old).astype(BF16)
            add_stats(acc_ref, u, jnp.where(keep, inner, 0.0), jnp.where(keep, cross, 0.0))

        by_utterance(ends, base + start, BLOCK, uniform, mixed)

    def conv(i, start):
        @pl.when(i + 1 < frames // ROWS)
        def _():
            back_tile(i + 1)

        late.tile(i).wait()
        before, here, after = taps_of(gradient_ref, ends, start, base)
        full_ref[...] = convolved((after, here, before), weight_ref)
        for_blocks(0, ROWS, BLOCK, lambda inside: slope_step(start + inside, inside))
        outward.tile(i).start()

    for_tiles(frames, conv)
    finish_stats(acc_ref, stat_ref)
    outward.finish()
    gradient_out.finish()


def buffer_gradient_kernel(
    info_ref,
    offset_ref,
    inner_hbm,
    unit_hbm,
    cot_hbm,
    wide_hbm,
    own_ref,
    one_ref,
    two_ref,
    three_ref,
    inverse_ref,
    coef_ref,
    before_ref,
    out_ref,
    after_ref,
    back_ref,
    up_ref,
    total_ref,
    inner_ref,
    unit_ref,
    cot_ref,
    wide_ref,
    inner_sems,
    unit_sems,
    cot_sems,
    wide_sems,
):
    frames, channels = unit_ref.shape
    streams = [
        Stream(inner_hbm, inner_ref, inner_sems),
        Stream(unit_hbm, unit_ref, unit_sems),
        Stream(cot_hbm, cot_ref, cot_sems),
        Stream(wide_hbm, wide_ref, wide_sems),
    ]
    for index in range(frames // ROWS):
        for stream in streams:
            stream.tile(index).start()
    tiles = offset_ref.shape[0]
    rows = frames // tiles
    halo, own = before_ref.shape[0], out_ref.shape[0]
    ends = read_ends(info_ref)
    base, slot_base = info_ref[8], info_ref[9]
    back_coefficients(
        own_ref, (one_ref, two_ref, three_ref), inverse_ref, coef_ref, back_ref, False
    )
    total_ref[...] = jnp.zeros_like(total_ref)
    span = rows + PAD

    def up_step(start):
        here = pl.ds(start, BLOCK)

        def upward(u):
            lead = cot_ref[here, :].astype(F32) * ROOT_HALF
            return lead + inward(
                inner_ref[here, :].astype(F32), unit_ref[here, :].astype(F32), back_ref, u
            )

        def uniform(u):
            up_ref[here, :] = upward(u).astype(BF16)

        def mixed(u, mask):
            old = up_ref[here, :].astype(F32)
            up_ref[here, :] = jnp.where(mask((BLOCK, channels)), upward(u), old).astype(BF16)

        by_utterance(ends, base + start, BLOCK, uniform, mixed)

    def step(i):
        start = pl.multiple_of(i * rows, rows)
        here = pl.ds(start, rows)
        shift = offset_ref[i] - slot_base
        aligned = pl.multiple_of((shift // PAD) * PAD, PAD)
        part = lax.dot_general(
            wide_ref[here, :], up_ref[here, :], (((0,), (0,)), ((), ())), preferred_element_type=F32
        )
        total_ref[pl.ds(aligned, span), :] += part[0:span]

    def blocks(i, start):
        for stream in streams:
            stream.tile(i).wait()
        for_blocks(start, ROWS, BLOCK, up_step)
        each = ROWS // rows

        def four(k, carry):
            for n in range(4):
                step(i * each + k * 4 + n)
            return carry

        lax.fori_loop(0, each // 4, four, 0)

    for_tiles(frames, blocks)
    before_ref[...] = total_ref[0:halo, :]
    out_ref[...] = total_ref[halo : halo + own, :]
    after_ref[...] = total_ref[halo + own : 2 * halo + own, :]


def scatter_kernel(places, copies, info_ref, order_ref, *refs):
    parts, out_ref, tmp_ref = refs[: len(places)], refs[-2], refs[-1]
    groups, piece, channels = parts[0].shape
    lanes = channels // 128
    me = info_ref[10]
    for old_ref in refs[len(places) : -2]:

        def copy(start, old_ref=old_ref):
            out_ref[pl.ds(start, ROWS), :] = old_ref[pl.ds(start, ROWS), :]

        for_blocks(0, out_ref.shape[0], ROWS, copy)
    for back, part_ref in zip(places, parts):
        source = lax.rem(me + copies - back, copies)

        def body(g, carry, part_ref=part_ref, source=source):
            for b in range(piece // 16):
                both = part_ref[g, b * 16 : b * 16 + 16, :].astype(F32)
                for h in range(2):
                    for q in range(lanes):
                        tmp_ref[pl.ds(((2 * b + h) * lanes + q) * 8, 8), :] = both[
                            8 * h : 8 * h + 8, q * 128 : (q + 1) * 128
                        ]
            first = (g * copies + source) * piece
            for r in range(piece):
                out_ref[pl.ds(order_ref[first + r], lanes, stride=8), :] = tmp_ref[
                    pl.ds((r // 8) * 8 * lanes + r % 8, lanes, stride=8), :
                ]
            return carry

        lax.fori_loop(0, groups, body, 0)


VM = pl.BlockSpec(memory_space=pltpu.VMEM)
SM = pl.BlockSpec(memory_space=pltpu.SMEM)


HB = pl.BlockSpec(memory_space=pltpu.HBM)


def call(kernel, inputs, outputs, scratch, flops, limit):
    return pl.pallas_call(
        kernel,
        in_specs=[spec for _, spec in inputs],
        out_specs=tuple(spec for _, _, spec in outputs),
        out_shape=tuple(
            pltpu.HBM(shape, dtype) if spec is HB else jax.ShapeDtypeStruct(shape, dtype)
            for shape, dtype, spec in outputs
        ),
        scratch_shapes=[
            pltpu.SemaphoreType.DMA((one,)) if isinstance(one, int) else pltpu.VMEM(*one)
            for one in scratch
        ],
        compiler_params=pltpu.CompilerParams(vmem_limit_bytes=limit * MIB),
        cost_estimate=pl.CostEstimate(flops=flops, bytes_accessed=flops // 200, transcendentals=0),
    )(
        *(
            pltpu.with_memory_space_constraint(array, pltpu.HBM) if spec is HB else array
            for array, spec in inputs
        )
    )


def scattered(old, parts, places, copies, info, order):
    piece, channels = parts[0].shape[1:]
    lanes = channels // 128
    kept = [] if old is None else [old]
    return pl.pallas_call(
        functools.partial(scatter_kernel, places, copies),
        in_specs=[SM, SM] + [VM] * (len(parts) + len(kept)),
        out_specs=VM,
        out_shape=jax.ShapeDtypeStruct((order.shape[0] * lanes, 128), F32),
        scratch_shapes=[pltpu.VMEM((piece * lanes, 128), F32)],
        input_output_aliases={2 + len(parts): 0} if kept else {},
        compiler_params=pltpu.CompilerParams(vmem_limit_bytes=22 * MIB),
        cost_estimate=pl.CostEstimate(flops=10**6, bytes_accessed=10**4, transcendentals=0),
    )(info, order, *parts, *kept)


def shifted(values, axis, step):
    devices = lax.axis_size(axis)
    return lax.ppermute(values, axis, [(i, (i + step) % devices) for i in range(devices)])


def others_over_tm(values):
    return [shifted(values, "tm", d) for d in (1, 2, 3)]


def from_neighbours(first_rows, last_rows):
    devices = lax.axis_size("tm")
    up = [(i, i + 1) for i in range(devices - 1)]
    down = [(i + 1, i) for i in range(devices - 1)]
    return lax.ppermute(last_rows, "tm", up), lax.ppermute(first_rows, "tm", down)


def swapped(values, bit):
    devices = lax.axis_size("seq")
    return lax.ppermute(values, "seq", [(i, i ^ (1 << bit)) for i in range(devices)])


def after(values, *others):
    return lax.optimization_barrier((values, others))[0]


def summed_over_tm(parts):
    copies, tm_index = lax.axis_size("tm"), lax.axis_index("tm")
    rows, channels = parts[0].shape
    pieces = jnp.stack(parts).reshape(len(parts), copies, rows // copies, channels)
    part = lax.dynamic_index_in_dim(pieces, tm_index, 1, False)
    sent = pieces.astype(BF16)
    for step in (1, 3, 2):
        give = lax.dynamic_index_in_dim(sent, (tm_index + step) % copies, 1, False)
        part = part + shifted(give, "tm", step).astype(F32)
    return part.astype(BF16)


def gathered_over_tm(part):
    copies, tm_index = lax.axis_size("tm"), lax.axis_index("tm")
    count, rows, channels = part.shape
    every = jnp.zeros((count, copies, rows, channels), BF16)
    every = lax.dynamic_update_index_in_dim(every, part, tm_index, 1)
    for step in (1, 3, 2):
        every = lax.dynamic_update_index_in_dim(
            every, shifted(part, "tm", step), (tm_index - step) % copies, 1
        )
    return every.reshape(count, copies * rows, channels)


def on_device(
    phonemes,
    send_order,
    phoneme_counts,
    frame_lengths,
    tile_offsets,
    alignment,
    style_vec,
    first_affine_weight,
    first_affine_bias,
    first_conv_weight,
    second_affine_weight,
    second_affine_bias,
    second_conv_weight,
    second_conv_bias,
    cotangent,
):
    frames, channels = cotangent.shape
    slot_count = phonemes.shape[0]
    groups = lax.axis_size("seq")
    copies = lax.axis_size("tm")
    seq_index, tm_index = lax.axis_index("seq"), lax.axis_index("tm")
    piece_rows = slot_count // groups // copies
    local_rows = slot_count // copies
    tiles = tile_offsets.shape[0]
    window = alignment.shape[1]
    halo = window // 2
    lengths = frame_lengths[0]
    conv_flops = 2 * frames * 3 * channels * channels

    info = jnp.concatenate(
        [
            jnp.cumsum(lengths),
            jnp.cumsum(phoneme_counts[0]),
            (tm_index * frames)[None],
            (tm_index * local_rows - halo)[None],
            tm_index[None],
            (seq_index < groups // 2)[None].astype(I32),
            (seq_index[None] >> jnp.arange(12, dtype=I32)) & 1,
        ]
    ).astype(I32)
    inverse = jnp.zeros((8, channels), F32).at[0:UTTS].set(
        jnp.broadcast_to(1.0 / lengths.astype(F32)[:, None], (UTTS, channels))
    )
    style_rows = jnp.zeros((8, style_vec.shape[1]), BF16).at[0:UTTS].set(style_vec)
    params_one = jnp.dot(style_rows, first_affine_weight, preferred_element_type=F32) + (
        first_affine_bias.astype(F32)
    )
    params_two = jnp.dot(style_rows, second_affine_weight, preferred_element_type=F32) + (
        second_affine_bias.astype(F32)
    )

    def turned(weight):
        return (
            weight.reshape(3, channels, channels).transpose(0, 2, 1).reshape(3 * channels, channels)
        )

    tiles_of = frames // ROWS
    full, padded = (frames, channels), (frames + 2 * PAD, channels)
    stats_shape, coef_shape = (STAT_ROWS, channels), (56, channels)
    small_acc = ((ACC_ROWS, channels), F32)

    order = send_order[0].reshape(groups, copies, piece_rows)
    mine = lax.dynamic_index_in_dim(order, tm_index, 1, False)
    outgoing = jnp.take(phonemes, mine.reshape(-1), axis=0, mode="clip")
    received = lax.all_to_all(
        outgoing.reshape(groups, piece_rows, channels), "seq", 0, 0, tiled=True
    ).reshape(local_rows, channels)

    second_turned = turned(second_conv_weight)
    grad_act_two, grad_branch, bias_part = call(
        gradient_kernel,
        (
            (info, SM),
            (cotangent, HB),
            (second_turned, VM),
        ),
        ((full, BF16, HB), (full, BF16, HB), ((16, channels), F32, VM)),
        [(full, BF16), (padded, BF16), (full, BF16), tiles_of, tiles_of, tiles_of],
        conv_flops,
        32,
    )

    received, bias_part = lax.optimization_barrier((received, bias_part))
    slots_before, slots_after = from_neighbours(received[:halo], received[-halo:])
    upsampled, upsampled_far, wide, stat = call(
        upsample_kernel,
        (
            (info, SM),
            (tile_offsets, SM),
            (slots_before, VM),
            (received, VM),
            (slots_after, VM),
            (alignment, HB),
            (bias_part, VM),
        ),
        (
            (full, F32, VM),
            (full, F32, HB),
            ((frames, WIDE), BF16, HB),
            (stats_shape, F32, VM),
        ),
        [
            ((local_rows + WIDE, channels), BF16),
            small_acc,
            ((frames, window), BF16),
            ((frames, WIDE), BF16),
            tiles_of,
            tiles_of,
            tiles_of,
        ],
        2 * frames * WIDE * channels,
        20,
    )
    others = others_over_tm(stat)
    bias_total = (stat[EXTRA_ROW] + others[1][EXTRA_ROW]) + (
        others[0][EXTRA_ROW] + others[2][EXTRA_ROW]
    )

    act_one, middle, middle_far, unit_one, coef_one, stat_two, grad_edges, added = call(
        first_conv_kernel,
        (
            (info, SM),
            (upsampled, VM),
            *((one, VM) for one in (stat, *others)),
            (inverse, VM),
            (params_one, VM),
            (first_conv_weight, VM),
            (second_turned, VM),
        ),
        (
            (padded, BF16, HB),
            (full, F32, VM),
            (full, F32, HB),
            (full, BF16, HB),
            (coef_shape, F32, VM),
            (stats_shape, F32, VM),
            ((8, channels), F32, VM),
            ((8, channels), F32, VM),
        ),
        [small_acc, (padded, BF16), (full, BF16), tiles_of, 2, tiles_of, tiles_of],
        conv_flops,
        28,
    )
    others_two = others_over_tm(stat_two)

    act_two, inner_two, coef_two, stat_three = call(
        second_norm_kernel,
        (
            (info, SM),
            (grad_act_two, HB),
            (middle, VM),
            *((one, VM) for one in (stat_two, *others_two)),
            (inverse, VM),
            (params_two, VM),
            (added, VM),
        ),
        (
            (padded, BF16, HB),
            (full, BF16, HB),
            (coef_shape, F32, VM),
            (stats_shape, F32, VM),
        ),
        [
            small_acc,
            (full, BF16),
            (padded, BF16),
            (full, BF16),
            tiles_of,
            tiles_of,
            2,
            tiles_of,
        ],
        2 * frames * channels * 100,
        28,
    )
    others_three = others_over_tm(stat_three)
    grad_middle, middle_edges, inner_one, back_two, stat_four = call(
        first_back_kernel,
        (
            (info, SM),
            (inner_two, HB),
            (middle_far, HB),
            *((one, VM) for one in (stat_three, *others_three)),
            (others_two[0], VM),
            (others_two[2], VM),
            (inverse, VM),
            (coef_two, VM),
            (coef_one, VM),
            (unit_one, HB),
            (turned(first_conv_weight), VM),
        ),
        (
            (full, BF16, HB),
            ((8, channels), F32, VM),
            (full, BF16, HB),
            ((40, channels), F32, VM),
            (stats_shape, F32, VM),
        ),
        [
            small_acc,
            ((ROWS, channels), F32),
            (full, BF16),
            (full, F32),
            (full, BF16),
            (full, BF16),
            (padded, BF16),
            *([tiles_of] * 5),
        ],
        conv_flops,
        40,
    )
    others_four = others_over_tm(stat_four)
    grad_before, grad_own, grad_after, back_one = call(
        buffer_gradient_kernel,
        (
            (info, SM),
            (tile_offsets, SM),
            (inner_one, HB),
            (unit_one, HB),
            (cotangent, HB),
            (wide, HB),
            *((one, VM) for one in (stat_four, *others_four)),
            (inverse, VM),
            (coef_one, VM),
        ),
        (
            ((halo, channels), F32, VM),
            ((local_rows, channels), F32, VM),
            ((halo, channels), F32, VM),
            ((40, channels), F32, VM),
        ),
        [
            (full, BF16),
            ((local_rows + WIDE, channels), F32),
            *([(full, BF16)] * 3),
            ((frames, WIDE), BF16),
            *([tiles_of] * 4),
        ],
        2 * frames * WIDE * channels,
        36,
    )

    row_places = (send_order[0] >> 3) * (8 * (channels // 128)) + (send_order[0] & 7)
    from_before, from_after = from_neighbours(grad_before, grad_after)
    return_rows = jnp.concatenate(
        [grad_own[:halo] + from_before, grad_own[halo:-halo], grad_own[-halo:] + from_after]
    ).astype(BF16)
    returned = lax.all_to_all(
        return_rows.reshape(groups, piece_rows, channels), "seq", 0, 0, tiled=True
    )

    bits = [b for b in range(12) if (1 << b) < groups]
    orders = (bits[1:], bits[1:][::-1])
    second_keep, second_give = call(
        weight_gradient_kernel,
        ((info, SM), (after(act_two, back_one), HB), (grad_branch, HB), (grad_edges, VM)),
        (((3 * channels // 2, channels), F32, VM), ((3 * channels // 2, channels), BF16, VM)),
        [((3 * channels, channels), F32), (padded, BF16), (padded, BF16), tiles_of, tiles_of],
        10**6,
        24,
    )

    returned, second_keep, second_give = lax.optimization_barrier(
        (returned, second_keep, second_give)
    )
    rounds = [returned, shifted(returned, "tm", 1)]
    first_keep, first_give = call(
        weight_gradient_kernel,
        ((info, SM), (act_one, HB), (after(grad_middle, returned), HB), (middle_edges, VM)),
        (((3 * channels // 2, channels), F32, VM), ((3 * channels // 2, channels), BF16, VM)),
        [((3 * channels, channels), F32), (padded, BF16), (padded, BF16), tiles_of, tiles_of],
        10**6,
        24,
    )

    keeps, gives = [second_keep, first_keep], [second_give, first_give]
    gots = [swapped(give, bits[0]) for give in gives]
    for turn, pair in enumerate(zip(*orders)):
        count = keeps[0].shape[0] // 2
        out = call(
            functools.partial(halves_kernel, pair),
            ((info, SM), *((one, VM) for both in zip(keeps, gots) for one in both)),
            (((count, channels), F32, VM), ((count, channels), BF16, VM)) * 2,
            [((2 * count, channels), F32)] * 2,
            10**6,
            16,
        )
        keeps, gives = [out[0], out[2]], [out[1], out[3]]
        if turn == 0:
            rounds[1], keeps, gives = lax.optimization_barrier((rounds[1], keeps, gives))
            rounds.append(shifted(rounds[1], "tm", 1))
        gots = [swapped(give, bit) for give, bit in zip(gives, pair)]
    row_sums = [keep + got.astype(F32) for keep, got in zip(keeps, gots)]
    placed = scattered(None, rounds[:2], (0, 1), copies, info, row_places)
    rounds[2], row_sums, placed = lax.optimization_barrier((rounds[2], row_sums, placed))
    sums = gathered_over_tm(summed_over_tm(row_sums))
    rounds[2], sums = lax.optimization_barrier((rounds[2], sums))
    rounds.append(shifted(rounds[2], "tm", 1))

    act_two, _ = lax.optimization_barrier((act_two, sums))
    (frames_out,) = call(
        second_conv_kernel,
        (
            (info, SM),
            (act_two, HB),
            (upsampled_far, HB),
            (second_conv_weight, VM),
            (second_conv_bias[None], VM),
        ),
        ((full, BF16, HB),),
        [(padded, BF16), (full, F32), (full, BF16), tiles_of, 2, tiles_of, tiles_of],
        10**6,
        36,
    )


    params_grad = [
        jnp.concatenate([back[8 : 8 + UTTS], back[0:UTTS]], axis=1) for back in (back_one, back_two)
    ]
    style_grad = jnp.dot(
        params_grad[0], first_affine_weight.astype(F32).T, precision=PRECISE
    ) + jnp.dot(params_grad[1], second_affine_weight.astype(F32).T, precision=PRECISE)
    style_block = jnp.zeros((8, channels), BF16).at[:, : style_rows.shape[1]].set(style_rows)
    small = jnp.concatenate(
        [
            back_one[8:16].astype(BF16),
            back_one[0:8].astype(BF16),
            back_two[8:16].astype(BF16),
            back_two[0:8].astype(BF16),
            style_block,
            jnp.zeros((8, channels), BF16).at[0].set(bias_total.astype(BF16)),
        ]
    )
    rows = sums.shape[1]
    held = [jnp.concatenate([sums[0], small]), sums[1]]
    for pair in zip(*orders):
        others = [swapped(one, bit) for one, bit in zip(held, pair)]
        held = call(
            functools.partial(join_kernel, pair),
            ((info, SM), *((one, VM) for both in zip(held, others) for one in both)),
            tuple(((2 * one.shape[0], channels), BF16, VM) for one in held),
            [],
            10**6,
            16,
        )
    rounds[3], held, frames_out = lax.optimization_barrier((rounds[3], list(held), frames_out))
    others = [swapped(one, bits[0]) for one in held]
    (
        second_conv_grad,
        first_conv_grad,
        first_affine_grad,
        first_shift_grad,
        second_affine_grad,
        second_shift_grad,
        second_bias_grad,
    ) = call(
        functools.partial(final_kernel, orders, rows),
        (
            (info, SM),
            (held[0], VM),
            (others[0], VM),
            (held[1], VM),
            (others[1], VM),
        ),
        (
            ((3 * channels, channels), F32, VM),
            ((3 * channels, channels), F32, VM),
            *(
                (((style_vec.shape[1], 2 * channels), F32, VM), ((1, 2 * channels), F32, VM)) * 2
            ),
            ((1, channels), F32, VM),
        ),
        [],
        10**6,
        28,
    )
    placed = scattered(placed, rounds[2:], (2, 3), copies, info, row_places)
    lanes = channels // 128
    phonemes_grad = (
        placed.reshape(slot_count // 8, lanes, 8, 128)
        .transpose(0, 2, 1, 3)
        .reshape(slot_count, channels)
    )
    return (
        frames_out,
        phonemes_grad,
        style_grad,
        first_affine_grad,
        first_shift_grad[0],
        first_conv_grad,
        second_affine_grad,
        second_shift_grad[0],
        second_conv_grad,
        second_bias_grad[0],
    )


def solution(mesh):
    split, whole = ("seq", "tm"), P()
    in_specs = (
        P("seq", None),
        P("seq", None),
        P("seq", None),
        P("seq", None),
        P(split),
        P(split, None),
        P("seq", None),
        *([whole] * 7),
        P(split, None),
    )
    out_specs = (P(split, None), P("seq", None), P("seq", None), *([whole] * 7))
    return jax.shard_map(
        on_device, mesh=mesh, in_specs=in_specs, out_specs=out_specs, check_vma=False
    )
```

```python
import functools

import jax
import jax.numpy as jnp
from jax import lax
from jax.experimental import pallas as pl
from jax.experimental.pallas import tpu as pltpu
from jax.sharding import PartitionSpec as P

EPSILON = 1e-05
ROOT_HALF = 0.7071067811865476
PRECISE = lax.Precision.HIGHEST
F32, BF16, I32 = jnp.float32, jnp.bfloat16, jnp.int32
UTTS = 4
PAD = 16
ROWS = 1024
BLOCK = 128
WIDE = 256
MIB = 2**20

STAT_ROWS = 24
FIRST_ROW, LAST_ROW, EXTRA_ROW, FIRST_GRAD, LAST_GRAD = 16, 17, 18, 19, 20
SMALL_ROWS = 48
BITS_AT = 12


def owner_at(ends, position):
    return sum((position >= end).astype(I32) for end in ends)


def tile_of(ref, index, offset=0):
    return ref.at[pl.ds(pl.multiple_of(offset + index * ROWS, PAD), ROWS), :]


class Stream:
    def __init__(self, source, target, sems, source_offset=0, target_offset=0):
        self.ends = (source, source_offset, target, target_offset)
        self.sems = sems
        self.tiles = sems.shape[0]

    def tile(self, index):
        source, source_offset, target, target_offset = self.ends
        return pltpu.make_async_copy(
            tile_of(source, index, source_offset),
            tile_of(target, index, target_offset),
            self.sems.at[index],
        )

    def start(self):
        for index in range(self.tiles):
            self.tile(index).start()

    def finish(self):
        for index in range(self.tiles):
            self.tile(index).wait()


def edge_copies(source, target, sems):
    last = source.shape[0] - PAD
    return [
        pltpu.make_async_copy(
            source.at[pl.ds(at, PAD), :], target.at[pl.ds(at, PAD), :], sems.at[k]
        )
        for k, at in enumerate((0, last))
    ]


def rows_of(start, shape):
    return start + lax.broadcasted_iota(I32, shape, 0)


def fold_rows(values):
    return jnp.sum(values.reshape(values.shape[0] // 8, 8, values.shape[1]), axis=0)


def by_utterance(ends, start, count, uniform_body, mixed_body):
    low, high = owner_at(ends, start), owner_at(ends, start + count - 1)

    @pl.when(low == high)
    def _():
        uniform_body(low)

    @pl.when(low != high)
    def _():
        def step(u, carry):
            lower = jnp.int32(-1)
            upper = jnp.int32(2**30)
            for k in range(UTTS):
                lower = jnp.where(u == k + 1, ends[k], lower)
                upper = jnp.where(u == k, ends[k], upper)

            def mask(shape):
                rows = rows_of(start, shape)
                return (rows >= lower) & (rows < upper)

            mixed_body(u, mask)
            return carry

        lax.fori_loop(low, high + 1, step, 0)


class Blocks:
    def __init__(self, ends, base, channels):
        self.ends, self.base, self.channels = ends, base, channels

    def plain(self, start, body):
        for inside in range(0, ROWS, BLOCK):
            first = self.base + start + inside
            low = owner_at(self.ends, first)
            alone = (low == owner_at(self.ends, first + BLOCK - 1)).astype(F32)
            body(start + inside, low, alone)

    def mixed(self, start, body):
        def step(i, carry):
            at = pl.multiple_of(start + i * BLOCK, BLOCK)
            by_utterance(
                self.ends,
                self.base + at,
                BLOCK,
                lambda u: None,
                lambda u, mask: body(at, u, mask((BLOCK, self.channels))),
            )
            return carry

        low = owner_at(self.ends, self.base + start)

        @pl.when(low != owner_at(self.ends, self.base + start + ROWS - 1))
        def _():
            lax.fori_loop(0, ROWS // BLOCK, step, 0)


def row(ref, index):
    return ref[pl.ds(index, 1), :]


def logistic(values):
    return 0.5 * jnp.tanh(0.5 * values) + 0.5


def taps_of(padded_ref, ends, start, base):
    channels = padded_ref.shape[1]
    block = padded_ref[pl.ds(start, ROWS + 2 * PAD), :].astype(F32)
    positions = rows_of(base + start, (ROWS, channels))
    cut_left = positions == ends[0]
    cut_right = positions + 1 == ends[0]
    for end in ends[1:]:
        cut_left = cut_left | (positions == end)
        cut_right = cut_right | (positions + 1 == end)
    before = jnp.where(cut_left, 0.0, block[PAD - 1 : PAD - 1 + ROWS]).astype(BF16)
    after = jnp.where(cut_right, 0.0, block[PAD + 1 : PAD + 1 + ROWS]).astype(BF16)
    return before, padded_ref[pl.ds(start + PAD, ROWS), :], after


def convolved(taps, weight_ref):
    channels = weight_ref.shape[1]
    return sum(
        jnp.dot(tap, weight_ref[k * channels : (k + 1) * channels, :], preferred_element_type=F32)
        for k, tap in enumerate(taps)
    )


def for_blocks(first, count, size, body, unroll=1):
    def step(i, carry):
        body(pl.multiple_of(first + i * size, size))
        return carry

    lax.fori_loop(0, count // size, step, 0, unroll=unroll)


def for_tiles(count, body):
    def step(i, carry):
        body(i, pl.multiple_of(i * ROWS, ROWS))
        return carry

    lax.fori_loop(0, count // ROWS, step, 0)


def wait_next(streams, i, count):
    @pl.when(i + 1 < count // ROWS)
    def _():
        for stream in streams:
            stream.tile(i + 1).wait()


def sum_over_tm(own_ref, other_refs, first, count):
    one, two, three = other_refs
    part = pl.ds(first, count)
    return (own_ref[part, :] + two[part, :]) + (one[part, :] + three[part, :])


def finish_stats(acc_ref, stat_ref):
    for kind in range(2):
        for u in range(8):
            at = kind * 8 + u
            if u < UTTS:
                first = (kind * (UTTS + 1) + u) * 8
                stat_ref[at : at + 1, :] = jnp.sum(
                    acc_ref[first : first + 8, :], axis=0, keepdims=True
                )
            else:
                stat_ref[at : at + 1, :] = jnp.zeros_like(stat_ref[at : at + 1, :])
    stat_ref[16:24, :] = jnp.zeros_like(stat_ref[16:24, :])


ACC_ROWS = 2 * (UTTS + 1) * 8


def add_stats(acc_ref, u, first, second, weight=None):
    for kind, term in enumerate((first, second)):
        at = pl.ds(pl.multiple_of((kind * (UTTS + 1) + u) * 8, 8), 8)
        term = fold_rows(term)
        acc_ref[at, :] += term if weight is None else term * weight


def read_ends(info_ref):
    return [info_ref[k] for k in range(UTTS)]


def halo_owner(info_ref, ends, base, frames):
    before = jnp.where(base == 0, UTTS, owner_at(ends, base - 1))
    return before, owner_at(ends, base + frames)


def gradient_kernel(
    info_ref,
    cot_hbm,
    weight_ref,
    out_hbm,
    padded_hbm,
    bias_ref,
    cot_ref,
    padded_ref,
    out_ref,
    cot_sems,
    padded_sems,
    out_sems,
):
    frames, channels = cot_ref.shape
    ends = read_ends(info_ref)
    base = info_ref[8]
    cot_in = Stream(cot_hbm, cot_ref, cot_sems)
    padded_out = Stream(padded_ref, padded_hbm, padded_sems, PAD)
    outward = Stream(out_ref, out_hbm, out_sems)
    cot_in.start()
    padded_ref[0:PAD, :] = jnp.zeros((PAD, channels), BF16)
    padded_ref[PAD + frames :, :] = jnp.zeros((PAD, channels), BF16)
    bias_ref[...] = jnp.zeros_like(bias_ref)

    def scale(start):
        here = cot_ref[pl.ds(start, BLOCK), :].astype(F32) * ROOT_HALF
        here = jnp.where(rows_of(base + start, (BLOCK, channels)) < ends[UTTS - 1], here, 0.0)
        rounded = here.astype(BF16)
        padded_ref[pl.ds(start + PAD, BLOCK), :] = rounded
        bias_ref[0:8, :] += fold_rows(rounded.astype(F32))

    def scale_tile(i, start):
        cot_in.tile(i).wait()
        for_blocks(start, ROWS, BLOCK, scale)
        padded_out.tile(i).start()

    for_tiles(frames, scale_tile)

    def conv(i, start):
        before, here, after = taps_of(padded_ref, ends, start, base)
        total = convolved((after, here, before), weight_ref)
        out_ref[pl.ds(start, ROWS), :] = total.astype(BF16)
        outward.tile(i).start()

    for_tiles(frames, conv)
    bias_ref[8:9, :] = padded_ref[PAD : 2 * PAD, :].astype(F32)[0:1]
    bias_ref[9:10, :] = padded_ref[frames : frames + PAD, :].astype(F32)[PAD - 1 :]
    padded_out.finish()
    outward.finish()


def upsample_kernel(
    info_ref,
    offset_ref,
    rows_ref,
    align_hbm,
    bias_ref,
    out_ref,
    out_hbm,
    wide_hbm,
    stat_ref,
    buffer_ref,
    acc_ref,
    align_ref,
    wide_ref,
    align_sems,
    out_sems,
    wide_sems,
):
    frames, channels = out_ref.shape
    align_in = Stream(align_hbm, align_ref, align_sems)
    outward = Stream(out_ref, out_hbm, out_sems)
    wide_out = Stream(wide_ref, wide_hbm, wide_sems)
    align_in.start()
    window = align_ref.shape[1]
    tiles = offset_ref.shape[0]
    rows = frames // tiles
    groups, both = rows_ref.shape[:2]
    halo = window // 2
    piece = next(n for n in range(both // 2, both) if both - n == min(halo, n))
    own, extra = groups * piece, both - piece
    ends = read_ends(info_ref)
    slot_ends = [info_ref[UTTS + k] for k in range(UTTS)]
    base, slot_base = info_ref[8], info_ref[9]
    for s in range(groups):
        buffer_ref[halo + s * piece : halo + (s + 1) * piece, :] = rows_ref[s, 0:piece, :]
    for n in range(halo // extra):
        buffer_ref[n * extra : (n + 1) * extra, :] = rows_ref[
            groups - halo // extra + n, piece:both, :
        ]
        at = halo + own + n * extra
        buffer_ref[at : at + extra, :] = rows_ref[n, piece:both, :]
    buffer_ref[2 * halo + own :, :] = jnp.zeros_like(buffer_ref[2 * halo + own :, :])
    acc_ref[...] = jnp.zeros_like(acc_ref)

    def step(i):
        start = pl.multiple_of(i * rows, rows)
        shift = offset_ref[i] - slot_base
        aligned = pl.multiple_of((shift // PAD) * PAD, PAD)
        block = align_ref[pl.ds(start, rows), :].astype(F32)
        block = jnp.concatenate([block, jnp.zeros((rows, WIDE - window), F32)], axis=1)
        block = pltpu.roll(block, shift - aligned, 1)
        slots = slot_base + aligned + lax.broadcasted_iota(I32, (rows, WIDE), 1)
        slot_owner = owner_at(slot_ends, slots)
        frame_owner = owner_at(ends, rows_of(base + start, (rows, WIDE)))
        match = (slot_owner == frame_owner) & (frame_owner < UTTS)
        block = jnp.where(match, block, 0.0).astype(BF16)
        wide_ref[pl.ds(start, rows), :] = block
        out_ref[pl.ds(start, rows), :] = jnp.dot(
            block, buffer_ref[pl.ds(aligned, WIDE), :], preferred_element_type=F32
        )

    def blocks(i, start):
        align_in.tile(i).wait()
        each = ROWS // rows

        def four(k, carry):
            for n in range(4):
                step(i * each + k * 4 + n)
            return carry

        lax.fori_loop(0, each // 4, four, 0)
        outward.tile(i).start()
        wide_out.tile(i).start()
        for_blocks(
            start, ROWS, BLOCK, lambda at: value_sums(out_ref, acc_ref, ends, base, at)
        )

    for_tiles(frames, blocks)
    finish_stats(acc_ref, stat_ref)
    stat_ref[FIRST_ROW : FIRST_ROW + 1, :] = out_ref[0:1, :]
    stat_ref[LAST_ROW : LAST_ROW + 1, :] = out_ref[frames - 1 : frames, :]
    stat_ref[EXTRA_ROW : EXTRA_ROW + 1, :] = jnp.sum(bias_ref[0:8, :], axis=0, keepdims=True)
    stat_ref[FIRST_GRAD : FIRST_GRAD + 2, :] = bias_ref[8:10, :]
    outward.finish()
    wide_out.finish()


def value_sums(out_ref, acc_ref, ends, base, start):
    channels = out_ref.shape[1]

    def uniform(u):
        here = out_ref[pl.ds(start, BLOCK), :]
        add_stats(acc_ref, u, here, here * here)

    def mixed(u, mask):
        here = jnp.where(mask((BLOCK, channels)), out_ref[pl.ds(start, BLOCK), :], 0.0)
        add_stats(acc_ref, u, here, here * here)

    by_utterance(ends, base + start, BLOCK, uniform, mixed)


def write_coefficients(own_ref, other_refs, inverse_ref, params_ref, coef_ref):
    channels = inverse_ref.shape[1]
    inverse = inverse_ref[...]
    total = sum_over_tm(own_ref, other_refs, 0, 8)
    square = sum_over_tm(own_ref, other_refs, 8, 8)
    mean = total * inverse
    real = inverse > 0.0
    rstd = jnp.where(real, lax.rsqrt(square * inverse - mean * mean + EPSILON), 0.0)
    gain = jnp.where(real, 1.0 + params_ref[:, 0:channels], 0.0)
    shift = jnp.where(real, params_ref[:, channels : 2 * channels], 0.0)
    coef_ref[0:8, :] = rstd
    coef_ref[8:16, :] = mean * rstd
    coef_ref[16:24, :] = gain * rstd
    coef_ref[24:32, :] = 0.5 * gain
    coef_ref[32:40, :] = 0.5 * shift
    coef_ref[40:48, :] = 0.5 * gain * rstd
    coef_ref[48:56, :] = 0.5 * (shift - mean * gain * rstd)
    coef_ref[56:57, :] = row(other_refs[0], LAST_ROW)
    coef_ref[57:58, :] = row(other_refs[2], FIRST_ROW)


UNIT, HALF_OF_UNIT, HALF_OF_VALUE = (0, 8), (24, 32), (40, 48)


def unit_of(values, coef_ref, u):
    return values * row(coef_ref, u) - row(coef_ref, 8 + u)


def half_normed(values, coef_ref, u, rows):
    return values * row(coef_ref, rows[0] + u) + row(coef_ref, rows[1] + u)


def twice_logistic(half):
    return jnp.tanh(half) + 1.0


def activation(values, coef_ref, u):
    half = half_normed(values, coef_ref, u, HALF_OF_VALUE)
    return half * twice_logistic(half)


def edge_rows(padded_ref, before, after):
    channels = padded_ref.shape[1]
    padded_ref[0:PAD, :] = jnp.broadcast_to(before, (PAD, channels)).astype(BF16)
    last = padded_ref.shape[0] - PAD
    padded_ref[last:, :] = jnp.broadcast_to(after, (PAD, channels)).astype(BF16)


def first_conv_kernel(
    info_ref,
    values_ref,
    own_ref,
    one_ref,
    two_ref,
    three_ref,
    inverse_ref,
    params_ref,
    weight_ref,
    turned_ref,
    act_hbm,
    out_ref,
    out_hbm,
    unit_hbm,
    coef_ref,
    stat_ref,
    edge_ref,
    added_ref,
    acc_ref,
    act_ref,
    unit_ref,
    act_sems,
    edge_sems,
    out_sems,
    unit_sems,
):
    frames, channels = values_ref.shape
    tiles = frames // ROWS
    act_out = Stream(act_ref, act_hbm, act_sems, PAD, PAD)
    unit_out = Stream(unit_ref, unit_hbm, unit_sems)
    outward = Stream(out_ref, out_hbm, out_sems)
    ends = read_ends(info_ref)
    base = info_ref[8]
    blocks = Blocks(ends, base, channels)
    write_coefficients(own_ref, (one_ref, two_ref, three_ref), inverse_ref, params_ref, coef_ref)
    acc_ref[...] = jnp.zeros_like(acc_ref)
    owner_before, owner_after = halo_owner(info_ref, ends, base, frames)
    edge_rows(
        act_ref,
        activation(row(one_ref, LAST_ROW), coef_ref, owner_before),
        activation(row(three_ref, FIRST_ROW), coef_ref, owner_after),
    )
    edges = edge_copies(act_ref, act_hbm, edge_sems)
    for edge in edges:
        edge.start()

    def act_parts(at, u):
        unit = unit_of(values_ref[pl.ds(at, BLOCK), :], coef_ref, u)
        half = half_normed(unit, coef_ref, u, HALF_OF_UNIT)
        return unit, half * twice_logistic(half)

    def act_plain(at, u, alone):
        unit, act = act_parts(at, u)
        unit_ref[pl.ds(at, BLOCK), :] = unit.astype(BF16)
        act_ref[pl.ds(at + PAD, BLOCK), :] = act.astype(BF16)

    def act_mixed(at, u, keep):
        here, there = pl.ds(at, BLOCK), pl.ds(at + PAD, BLOCK)
        unit, act = act_parts(at, u)
        unit_ref[here, :] = jnp.where(keep, unit, unit_ref[here, :].astype(F32)).astype(BF16)
        act_ref[there, :] = jnp.where(keep, act, act_ref[there, :].astype(F32)).astype(BF16)

    def sums_plain(at, u, alone):
        here = out_ref[pl.ds(at, BLOCK), :]
        add_stats(acc_ref, u, here, here * here, alone)

    def sums_mixed(at, u, keep):
        here = jnp.where(keep, out_ref[pl.ds(at, BLOCK), :], 0.0)
        add_stats(acc_ref, u, here, here * here)

    for turn in range(-1, tiles + 1):
        if turn + 1 < tiles:
            blocks.plain((turn + 1) * ROWS, act_plain)
        if 0 <= turn < tiles:
            start = turn * ROWS
            out_ref[start : start + ROWS, :] = convolved(
                taps_of(act_ref, ends, start, base), weight_ref
            )
        if turn > 0:
            blocks.plain((turn - 1) * ROWS, sums_plain)
        if turn + 1 < tiles:
            blocks.mixed((turn + 1) * ROWS, act_mixed)
            act_out.tile(turn + 1).start()
            unit_out.tile(turn + 1).start()
        if 0 <= turn < tiles:
            outward.tile(turn).start()
        if turn > 0:
            blocks.mixed((turn - 1) * ROWS, sums_mixed)
    edge_ref[...] = jnp.zeros_like(edge_ref)
    added_ref[...] = jnp.zeros_like(added_ref)
    neighbours = (
        (one_ref, LAST_GRAD, owner_before, owner_at(ends, base), 2 * channels),
        (three_ref, FIRST_GRAD, owner_after, owner_at(ends, base + frames - 1), 0),
    )
    for k, (ref, at, theirs, ours, tap) in enumerate(neighbours):
        valid = (theirs == ours) & (ours < UTTS)
        edge_ref[k : k + 1, :] = jnp.where(valid, ref[at : at + 1, :], 0.0)
        rows = jnp.broadcast_to(edge_ref[k : k + 1, :], (PAD, channels)).astype(BF16)
        added_ref[k : k + 1, :] = jnp.dot(
            rows, turned_ref[tap : tap + channels, :], preferred_element_type=F32
        )[0:1]
    finish_stats(acc_ref, stat_ref)
    stat_ref[FIRST_ROW : FIRST_ROW + 1, :] = out_ref[0:1, :]
    stat_ref[LAST_ROW : LAST_ROW + 1, :] = out_ref[frames - 1 : frames, :]
    act_out.finish()
    unit_out.finish()
    outward.finish()
    for edge in edges:
        edge.wait()


def slope_and_sums(gradient, values, coef_ref, u, rows):
    half = half_normed(values, coef_ref, u, rows)
    gate = twice_logistic(half)
    act = half * gate
    inner = gradient * (gate * (half - 0.5 * act + 0.5))
    return act, inner, inner * values


def second_norm_kernel(
    info_ref,
    gradient_hbm,
    values_ref,
    own_ref,
    one_ref,
    two_ref,
    three_ref,
    inverse_ref,
    params_ref,
    added_ref,
    act_hbm,
    inner_hbm,
    coef_ref,
    stat_ref,
    acc_ref,
    gradient_ref,
    act_ref,
    inner_ref,
    gradient_sems,
    act_sems,
    edge_sems,
    inner_sems,
):
    frames, channels = values_ref.shape
    gradient_in = Stream(gradient_hbm, gradient_ref, gradient_sems)
    outward = [
        Stream(act_ref, act_hbm, act_sems, PAD, PAD),
        Stream(inner_ref, inner_hbm, inner_sems),
    ]
    gradient_in.start()
    ends = read_ends(info_ref)
    base = info_ref[8]
    write_coefficients(own_ref, (one_ref, two_ref, three_ref), inverse_ref, params_ref, coef_ref)
    acc_ref[...] = jnp.zeros_like(acc_ref)
    owner_before, owner_after = halo_owner(info_ref, ends, base, frames)
    edge_rows(
        act_ref,
        activation(row(one_ref, LAST_ROW), coef_ref, owner_before),
        activation(row(three_ref, FIRST_ROW), coef_ref, owner_after),
    )

    edges = edge_copies(act_ref, act_hbm, edge_sems)
    for edge in edges:
        edge.start()

    def step(start):
        here = pl.ds(start, BLOCK)
        there = pl.ds(start + PAD, BLOCK)

        def parts(u):
            return slope_and_sums(
                gradient_ref[here, :].astype(F32), values_ref[here, :], coef_ref, u, HALF_OF_VALUE
            )

        def uniform(u):
            act, inner, cross = parts(u)
            act_ref[there, :] = act.astype(BF16)
            inner_ref[here, :] = inner.astype(BF16)
            add_stats(acc_ref, u, inner, cross)

        def mixed(u, mask):
            keep = mask((BLOCK, channels))
            act, inner, cross = parts(u)
            act_ref[there, :] = jnp.where(keep, act, act_ref[there, :].astype(F32)).astype(BF16)
            old = inner_ref[here, :].astype(F32)
            inner_ref[here, :] = jnp.where(keep, inner, old).astype(BF16)
            add_stats(acc_ref, u, jnp.where(keep, inner, 0.0), jnp.where(keep, cross, 0.0))

        by_utterance(ends, base + start, BLOCK, uniform, mixed)

    def tile(i, start):
        gradient_in.tile(i).wait()
        for k, at in enumerate((0, frames - PAD)):

            @pl.when(i == at // ROWS)
            def _(k=k, at=at):
                edge = gradient_ref[at : at + PAD, :].astype(F32)
                inside = rows_of(0, (PAD, channels)) == k * (PAD - 1)
                edge = edge + jnp.where(inside, added_ref[k : k + 1, :], 0.0)
                gradient_ref[at : at + PAD, :] = edge.astype(BF16)

        for_blocks(start, ROWS, BLOCK, step)
        for stream in outward:
            stream.tile(i).start()

    for_tiles(frames, tile)
    finish_stats(acc_ref, stat_ref)
    stat_ref[FIRST_ROW : FIRST_ROW + 1, :] = inner_ref[0:PAD, :].astype(F32)[0:1]
    stat_ref[LAST_ROW : LAST_ROW + 1, :] = inner_ref[frames - PAD :, :].astype(F32)[PAD - 1 :]
    for stream in outward:
        stream.finish()
    for edge in edges:
        edge.wait()


def second_conv_kernel(
    info_ref,
    act_hbm,
    values_hbm,
    weight_ref,
    bias_ref,
    out_hbm,
    act_ref,
    values_ref,
    out_ref,
    act_sems,
    edge_sems,
    values_sems,
    out_sems,
):
    frames, channels = values_ref.shape
    ends = read_ends(info_ref)
    base = info_ref[8]
    bias = bias_ref[...].astype(F32)
    act_in = Stream(act_hbm, act_ref, act_sems, PAD, PAD)
    values_in = Stream(values_hbm, values_ref, values_sems)
    outward = Stream(out_ref, out_hbm, out_sems)
    edges = edge_copies(act_hbm, act_ref, edge_sems)
    for edge in edges:
        edge.start()
    act_in.start()
    values_in.start()
    for edge in edges:
        edge.wait()
    act_in.tile(0).wait()

    def step(i, start):
        here = pl.ds(start, ROWS)
        wait_next([act_in], i, frames)
        values_in.tile(i).wait()
        branch = convolved(taps_of(act_ref, ends, start, base), weight_ref) + bias
        valid = rows_of(base + start, (ROWS, channels)) < ends[UTTS - 1]
        total = jnp.where(valid, (values_ref[here, :] + branch) * ROOT_HALF, 0.0)
        out_ref[here, :] = total.astype(BF16)
        outward.tile(i).start()

    for_tiles(frames, step)
    outward.finish()


def weight_gradient_kernel(
    info_ref,
    act_hbm,
    gradient_hbm,
    edge_ref,
    keep_ref,
    give_ref,
    out_ref,
    act_ref,
    gradient_ref,
    act_sems,
    gradient_sems,
):
    frames = act_ref.shape[0] - 2 * PAD
    channels = act_ref.shape[1]
    ends = read_ends(info_ref)
    base = info_ref[8]
    act_in = Stream(act_hbm, act_ref, act_sems, PAD, PAD)
    gradient_in = Stream(gradient_hbm, gradient_ref, gradient_sems, 0, PAD)
    for index in range(frames // ROWS):
        gradient_in.tile(index).start()
        act_in.tile(index).start()
    out_ref[...] = jnp.zeros_like(out_ref)
    edge_rows(gradient_ref, edge_ref[0:1, :], edge_ref[1:2, :])
    gradient_in.tile(0).wait()

    def step(i, start):
        wait_next([gradient_in], i, frames)
        act_in.tile(i).wait()
        before, here, after = taps_of(gradient_ref, ends, start, base)
        act = act_ref[pl.ds(start + PAD, ROWS), :]
        for k, tap in enumerate((after, here, before)):
            out_ref[k * channels : (k + 1) * channels, :] += lax.dot_general(
                act, tap, (((0,), (0,)), ((), ())), preferred_element_type=F32
            )

    for_tiles(frames, step)
    write_halves(info_ref, 0, out_ref, keep_ref, give_ref)


def write_halves(info_ref, bit, total_ref, keep_ref, give_ref):
    half = keep_ref.shape[0]
    mine = info_ref[BITS_AT + bit]
    keep_ref[...] = total_ref[pl.ds(pl.multiple_of(mine * half, PAD), half), :]
    give_ref[...] = total_ref[pl.ds(pl.multiple_of((1 - mine) * half, PAD), half), :].astype(BF16)


def halves_kernel(bits, info_ref, *refs):
    count = len(bits)
    inputs, outputs, totals = refs[: 2 * count], refs[2 * count : 4 * count], refs[4 * count :]
    for k, bit in enumerate(bits):
        totals[k][...] = inputs[2 * k][...] + inputs[2 * k + 1][...].astype(F32)
        write_halves(info_ref, bit, totals[k], outputs[2 * k], outputs[2 * k + 1])


def join_kernel(bits, info_ref, *refs):
    count = len(bits)
    for k, bit in enumerate(bits):
        part_ref, other_ref, out_ref = refs[2 * k], refs[2 * k + 1], refs[2 * count + k]
        half = part_ref.shape[0]
        mine = info_ref[BITS_AT + bit]
        out_ref[pl.ds(pl.multiple_of(mine * half, PAD), half), :] = part_ref[...]
        out_ref[pl.ds(pl.multiple_of((1 - mine) * half, PAD), half), :] = other_ref[...]


def block_order(order):
    places = []
    for index in range(1 << (len(order) + 1)):
        source, joined = index & 1, 0
        for at, bit in enumerate(order):
            source = 2 * source + ((index >> bit) & 1)
            joined += ((index >> bit) & 1) << at
        places.append((index & 1, source, joined))
    return places


def final_kernel(
    orders,
    rows,
    info_ref,
    second_ref,
    second_other_ref,
    first_ref,
    first_other_ref,
    second_out_ref,
    first_out_ref,
    first_affine_ref,
    first_shift_ref,
    second_affine_ref,
    second_shift_ref,
    bias_ref,
):
    channels = second_ref.shape[1]
    mine = info_ref[BITS_AT]
    gathered = []
    pairs = (
        (second_ref, second_other_ref, second_out_ref, rows + SMALL_ROWS),
        (first_ref, first_other_ref, first_out_ref, rows),
    )
    for k, (part_ref, other_ref, out_ref, step) in enumerate(pairs):
        for core, source, joined in block_order(orders[k]):
            here = pl.ds(joined * step, step)
            block = jnp.where(
                mine == core, part_ref[here, :].astype(F32), other_ref[here, :].astype(F32)
            )
            out_ref[source * rows : (source + 1) * rows, :] = block[:rows]
            if k == 0:
                gathered.append(block[rows:])
    styles = jnp.concatenate([block[32:40, 0:128] for block in gathered], axis=0)
    for at, (affine_ref, shift_ref) in enumerate(
        ((first_affine_ref, first_shift_ref), (second_affine_ref, second_shift_ref))
    ):
        for side in range(2):
            first = 16 * at + 8 * side
            sums = jnp.concatenate([block[first : first + 8] for block in gathered], axis=0)
            lanes = slice(side * channels, (side + 1) * channels)
            affine_ref[:, lanes] = lax.dot_general(
                styles, sums, (((0,), (0,)), ((), ())), precision=PRECISE
            )
            shift_ref[:, lanes] = jnp.sum(sums, axis=0, keepdims=True)
    biases = jnp.concatenate([block[40:48] for block in gathered], axis=0)
    bias_ref[...] = jnp.sum(biases, axis=0, keepdims=True)


def back_coefficients(own_ref, other_refs, inverse_ref, coef_ref, back_ref, of_values):
    inverse = inverse_ref[...]
    rstd, mean_rstd, scale = coef_ref[0:8, :], coef_ref[8:16, :], coef_ref[16:24, :]
    total = sum_over_tm(own_ref, other_refs, 0, 8)
    cross = sum_over_tm(own_ref, other_refs, 8, 8)
    if of_values:
        cross = rstd * cross - mean_rstd * total
    back_ref[0:8, :] = total
    back_ref[8:16, :] = cross
    slant = scale * cross * inverse
    back_ref[16:24, :] = scale * total * inverse - (mean_rstd * slant if of_values else 0.0)
    back_ref[24:32, :] = rstd * slant if of_values else slant
    back_ref[32:40, :] = scale


def inward(inner, values, back_ref, u):
    return inner * row(back_ref, 32 + u) - row(back_ref, 16 + u) - values * row(back_ref, 24 + u)


def first_back_kernel(
    info_ref,
    inner_hbm,
    middle_hbm,
    own_ref,
    one_ref,
    two_ref,
    three_ref,
    inverse_ref,
    coef_two_ref,
    coef_one_ref,
    unit_one_hbm,
    weight_ref,
    gradient_hbm,
    edge_ref,
    out_hbm,
    back_ref,
    stat_ref,
    acc_ref,
    full_ref,
    inner_ref,
    middle_ref,
    unit_one_ref,
    out_ref,
    gradient_ref,
    inner_sems,
    two_sems,
    one_sems,
    out_sems,
    gradient_sems,
):
    frames, channels = unit_one_ref.shape
    early = [
        Stream(inner_hbm, inner_ref, inner_sems),
        Stream(middle_hbm, middle_ref, two_sems),
    ]
    late = Stream(unit_one_hbm, unit_one_ref, one_sems)
    outward = Stream(out_ref, out_hbm, out_sems)
    gradient_out = Stream(gradient_ref, gradient_hbm, gradient_sems, PAD)
    for index in range(frames // ROWS):
        for stream in (*early, late):
            stream.tile(index).start()
    ends = read_ends(info_ref)
    base = info_ref[8]
    back_coefficients(own_ref, (one_ref, two_ref, three_ref), inverse_ref, coef_two_ref, back_ref, True)
    acc_ref[...] = jnp.zeros_like(acc_ref)
    owner_before, owner_after = halo_owner(info_ref, ends, base, frames)
    edge_rows(
        gradient_ref,
        inward(
            row(one_ref, LAST_ROW),
            row(coef_two_ref, 56),
            back_ref,
            owner_before,
        ),
        inward(
            row(three_ref, FIRST_ROW),
            row(coef_two_ref, 57),
            back_ref,
            owner_after,
        ),
    )

    def back_step(start):
        here = pl.ds(start, BLOCK)
        there = pl.ds(start + PAD, BLOCK)

        def now(u):
            return inward(
                inner_ref[here, :].astype(F32), middle_ref[here, :], back_ref, u
            )

        def uniform(u):
            gradient_ref[there, :] = now(u).astype(BF16)

        def mixed(u, mask):
            old = gradient_ref[there, :].astype(F32)
            gradient_ref[there, :] = jnp.where(mask((BLOCK, channels)), now(u), old).astype(BF16)

        by_utterance(ends, base + start, BLOCK, uniform, mixed)

    edge_ref[0:8, :] = gradient_ref[0:PAD, :].astype(F32)[0:8]
    edge_ref[1:2, :] = gradient_ref[PAD + frames :, :].astype(F32)[0:1]

    def back_tile(i):
        for stream in early:
            stream.tile(i).wait()
        for_blocks(pl.multiple_of(i * ROWS, ROWS), ROWS, BLOCK, back_step)
        gradient_out.tile(i).start()

    back_tile(0)

    def slope_step(start, row_start):
        here = pl.ds(start, BLOCK)

        def parts(u):
            unit = unit_one_ref[here, :].astype(F32)
            _, inner, cross = slope_and_sums(
                full_ref[pl.ds(row_start, BLOCK), :], unit, coef_one_ref, u, HALF_OF_UNIT
            )
            return inner, cross

        def uniform(u):
            inner, cross = parts(u)
            out_ref[here, :] = inner.astype(BF16)
            add_stats(acc_ref, u, inner, cross)

        def mixed(u, mask):
            keep = mask((BLOCK, channels))
            inner, cross = parts(u)
            old = out_ref[here, :].astype(F32)
            out_ref[here, :] = jnp.where(keep, inner, old).astype(BF16)
            add_stats(acc_ref, u, jnp.where(keep, inner, 0.0), jnp.where(keep, cross, 0.0))

        by_utterance(ends, base + start, BLOCK, uniform, mixed)

    def conv(i, start):
        @pl.when(i + 1 < frames // ROWS)
        def _():
            back_tile(i + 1)

        late.tile(i).wait()
        before, here, after = taps_of(gradient_ref, ends, start, base)
        full_ref[...] = convolved((after, here, before), weight_ref)
        for_blocks(0, ROWS, BLOCK, lambda inside: slope_step(start + inside, inside))
        outward.tile(i).start()

    for_tiles(frames, conv)
    finish_stats(acc_ref, stat_ref)
    outward.finish()
    gradient_out.finish()


def buffer_gradient_kernel(
    info_ref,
    offset_ref,
    inner_hbm,
    unit_hbm,
    cot_hbm,
    wide_hbm,
    own_ref,
    one_ref,
    two_ref,
    three_ref,
    inverse_ref,
    coef_ref,
    before_ref,
    out_ref,
    after_ref,
    back_ref,
    up_ref,
    total_ref,
    inner_ref,
    unit_ref,
    cot_ref,
    wide_ref,
    inner_sems,
    unit_sems,
    cot_sems,
    wide_sems,
):
    frames, channels = unit_ref.shape
    streams = [
        Stream(inner_hbm, inner_ref, inner_sems),
        Stream(unit_hbm, unit_ref, unit_sems),
        Stream(cot_hbm, cot_ref, cot_sems),
        Stream(wide_hbm, wide_ref, wide_sems),
    ]
    for index in range(frames // ROWS):
        for stream in streams:
            stream.tile(index).start()
    tiles = offset_ref.shape[0]
    rows = frames // tiles
    halo, own = before_ref.shape[0], out_ref.shape[0]
    ends = read_ends(info_ref)
    base, slot_base = info_ref[8], info_ref[9]
    back_coefficients(
        own_ref, (one_ref, two_ref, three_ref), inverse_ref, coef_ref, back_ref, False
    )
    total_ref[...] = jnp.zeros_like(total_ref)
    span = rows + PAD

    def up_step(start):
        here = pl.ds(start, BLOCK)

        def upward(u):
            lead = cot_ref[here, :].astype(F32) * ROOT_HALF
            return lead + inward(
                inner_ref[here, :].astype(F32), unit_ref[here, :].astype(F32), back_ref, u
            )

        def uniform(u):
            up_ref[here, :] = upward(u).astype(BF16)

        def mixed(u, mask):
            old = up_ref[here, :].astype(F32)
            up_ref[here, :] = jnp.where(mask((BLOCK, channels)), upward(u), old).astype(BF16)

        by_utterance(ends, base + start, BLOCK, uniform, mixed)

    def step(i):
        start = pl.multiple_of(i * rows, rows)
        here = pl.ds(start, rows)
        shift = offset_ref[i] - slot_base
        aligned = pl.multiple_of((shift // PAD) * PAD, PAD)
        part = lax.dot_general(
            wide_ref[here, :], up_ref[here, :], (((0,), (0,)), ((), ())), preferred_element_type=F32
        )
        total_ref[pl.ds(aligned, span), :] += part[0:span]

    def blocks(i, start):
        for stream in streams:
            stream.tile(i).wait()
        for_blocks(start, ROWS, BLOCK, up_step)
        each = ROWS // rows

        def four(k, carry):
            for n in range(4):
                step(i * each + k * 4 + n)
            return carry

        lax.fori_loop(0, each // 4, four, 0)

    for_tiles(frames, blocks)
    before_ref[...] = total_ref[0:halo, :]
    out_ref[...] = total_ref[halo : halo + own, :]
    after_ref[...] = total_ref[halo + own : 2 * halo + own, :]


def scatter_kernel(places, copies, info_ref, order_ref, *refs):
    parts, out_ref, tmp_ref = refs[: len(places)], refs[-2], refs[-1]
    groups, piece, channels = parts[0].shape
    lanes = channels // 128
    me = info_ref[10]
    for old_ref in refs[len(places) : -2]:

        def copy(start, old_ref=old_ref):
            out_ref[pl.ds(start, ROWS), :] = old_ref[pl.ds(start, ROWS), :]

        for_blocks(0, out_ref.shape[0], ROWS, copy)
    for back, part_ref in zip(places, parts):
        source = lax.rem(me + copies - back, copies)

        def body(g, carry, part_ref=part_ref, source=source):
            for b in range(piece // 16):
                both = part_ref[g, b * 16 : b * 16 + 16, :].astype(F32)
                for h in range(2):
                    for q in range(lanes):
                        tmp_ref[pl.ds(((2 * b + h) * lanes + q) * 8, 8), :] = both[
                            8 * h : 8 * h + 8, q * 128 : (q + 1) * 128
                        ]
            first = (g * copies + source) * piece
            for r in range(piece):
                out_ref[pl.ds(order_ref[first + r], lanes, stride=8), :] = tmp_ref[
                    pl.ds((r // 8) * 8 * lanes + r % 8, lanes, stride=8), :
                ]
            return carry

        lax.fori_loop(0, groups, body, 0)


VM = pl.BlockSpec(memory_space=pltpu.VMEM)
SM = pl.BlockSpec(memory_space=pltpu.SMEM)


HB = pl.BlockSpec(memory_space=pltpu.HBM)


def call(kernel, inputs, outputs, scratch, flops, limit):
    return pl.pallas_call(
        kernel,
        in_specs=[spec for _, spec in inputs],
        out_specs=tuple(spec for _, _, spec in outputs),
        out_shape=tuple(
            pltpu.HBM(shape, dtype) if spec is HB else jax.ShapeDtypeStruct(shape, dtype)
            for shape, dtype, spec in outputs
        ),
        scratch_shapes=[
            pltpu.SemaphoreType.DMA((one,)) if isinstance(one, int) else pltpu.VMEM(*one)
            for one in scratch
        ],
        compiler_params=pltpu.CompilerParams(vmem_limit_bytes=limit * MIB),
        cost_estimate=pl.CostEstimate(flops=flops, bytes_accessed=flops // 200, transcendentals=0),
    )(
        *(
            pltpu.with_memory_space_constraint(array, pltpu.HBM) if spec is HB else array
            for array, spec in inputs
        )
    )


def scattered(old, parts, places, copies, info, order):
    piece, channels = parts[0].shape[1:]
    lanes = channels // 128
    kept = [] if old is None else [old]
    return pl.pallas_call(
        functools.partial(scatter_kernel, places, copies),
        in_specs=[SM, SM] + [VM] * (len(parts) + len(kept)),
        out_specs=VM,
        out_shape=(pltpu.VMEM if old is None else jax.ShapeDtypeStruct)(
            (order.shape[0] * lanes, 128), F32
        ),
        scratch_shapes=[pltpu.VMEM((piece * lanes, 128), F32)],
        input_output_aliases={2 + len(parts): 0} if kept else {},
        compiler_params=pltpu.CompilerParams(vmem_limit_bytes=22 * MIB),
        cost_estimate=pl.CostEstimate(flops=10**6, bytes_accessed=10**4, transcendentals=0),
    )(info, order, *parts, *kept)


def shifted(values, axis, step):
    devices = lax.axis_size(axis)
    return lax.ppermute(values, axis, [(i, (i + step) % devices) for i in range(devices)])


def others_over_tm(values):
    return [shifted(values, "tm", d) for d in (1, 2, 3)]


def from_neighbours(first_rows, last_rows):
    devices = lax.axis_size("tm")
    up = [(i, i + 1) for i in range(devices - 1)]
    down = [(i + 1, i) for i in range(devices - 1)]
    return lax.ppermute(last_rows, "tm", up), lax.ppermute(first_rows, "tm", down)


def swapped(values, bit):
    devices = lax.axis_size("seq")
    return lax.ppermute(values, "seq", [(i, i ^ (1 << bit)) for i in range(devices)])


def after(values, *others):
    return lax.optimization_barrier((values, others))[0]


def summed_over_tm(parts):
    copies, tm_index = lax.axis_size("tm"), lax.axis_index("tm")
    rows, channels = parts[0].shape
    pieces = jnp.stack(parts).reshape(len(parts), copies, rows // copies, channels)
    part = lax.dynamic_index_in_dim(pieces, tm_index, 1, False)
    sent = pieces.astype(BF16)
    for step in (1, 3, 2):
        give = lax.dynamic_index_in_dim(sent, (tm_index + step) % copies, 1, False)
        part = part + shifted(give, "tm", step).astype(F32)
    return part.astype(BF16)


def gathered_over_tm(part):
    copies, tm_index = lax.axis_size("tm"), lax.axis_index("tm")
    count, rows, channels = part.shape
    every = jnp.zeros((count, copies, rows, channels), BF16)
    every = lax.dynamic_update_index_in_dim(every, part, tm_index, 1)
    for step in (1, 3, 2):
        every = lax.dynamic_update_index_in_dim(
            every, shifted(part, "tm", step), (tm_index - step) % copies, 1
        )
    return every.reshape(count, copies * rows, channels)


def on_device(
    phonemes,
    send_order,
    phoneme_counts,
    frame_lengths,
    tile_offsets,
    alignment,
    style_vec,
    first_affine_weight,
    first_affine_bias,
    first_conv_weight,
    second_affine_weight,
    second_affine_bias,
    second_conv_weight,
    second_conv_bias,
    cotangent,
):
    frames, channels = cotangent.shape
    slot_count = phonemes.shape[0]
    groups = lax.axis_size("seq")
    copies = lax.axis_size("tm")
    seq_index, tm_index = lax.axis_index("seq"), lax.axis_index("tm")
    piece_rows = slot_count // groups // copies
    local_rows = slot_count // copies
    tiles = tile_offsets.shape[0]
    window = alignment.shape[1]
    halo = window // 2
    lengths = frame_lengths[0]
    conv_flops = 2 * frames * 3 * channels * channels

    info = jnp.concatenate(
        [
            jnp.cumsum(lengths),
            jnp.cumsum(phoneme_counts[0]),
            (tm_index * frames)[None],
            (tm_index * local_rows - halo)[None],
            tm_index[None],
            (seq_index < groups // 2)[None].astype(I32),
            (seq_index[None] >> jnp.arange(12, dtype=I32)) & 1,
        ]
    ).astype(I32)
    inverse = jnp.zeros((8, channels), F32).at[0:UTTS].set(
        jnp.broadcast_to(1.0 / lengths.astype(F32)[:, None], (UTTS, channels))
    )
    style_rows = jnp.zeros((8, style_vec.shape[1]), BF16).at[0:UTTS].set(style_vec)
    params_one = jnp.dot(style_rows, first_affine_weight, preferred_element_type=F32) + (
        first_affine_bias.astype(F32)
    )
    params_two = jnp.dot(style_rows, second_affine_weight, preferred_element_type=F32) + (
        second_affine_bias.astype(F32)
    )

    def turned(weight):
        return (
            weight.reshape(3, channels, channels).transpose(0, 2, 1).reshape(3 * channels, channels)
        )

    tiles_of = frames // ROWS
    full, padded = (frames, channels), (frames + 2 * PAD, channels)
    stats_shape, coef_shape = (STAT_ROWS, channels), (64, channels)
    small_acc = ((ACC_ROWS, channels), F32)

    order = send_order[0].reshape(groups, copies, piece_rows)
    extra = min(halo, piece_rows)
    from_first = seq_index < groups // 2
    mine = lax.dynamic_index_in_dim(order, tm_index, 1, False)
    following = lax.dynamic_index_in_dim(order, jnp.minimum(tm_index + 1, copies - 1), 1, False)
    leading = lax.dynamic_index_in_dim(order, jnp.maximum(tm_index - 1, 0), 1, False)
    beside = jnp.where(from_first, following[:, :extra], leading[:, piece_rows - extra :])
    mine = jnp.concatenate([mine, beside], axis=1)
    outgoing = jnp.take(phonemes, mine.reshape(-1), axis=0, mode="clip")
    received = lax.all_to_all(
        outgoing.reshape(groups, piece_rows + extra, channels), "seq", 0, 0, tiled=True
    )

    second_turned = turned(second_conv_weight)
    grad_act_two, grad_branch, bias_part = call(
        gradient_kernel,
        (
            (info, SM),
            (cotangent, HB),
            (second_turned, VM),
        ),
        ((full, BF16, HB), (full, BF16, HB), ((16, channels), F32, VM)),
        [(full, BF16), (padded, BF16), (full, BF16), tiles_of, tiles_of, tiles_of],
        conv_flops,
        32,
    )

    received, bias_part = lax.optimization_barrier((received, bias_part))
    upsampled, upsampled_far, wide, stat = call(
        upsample_kernel,
        (
            (info, SM),
            (tile_offsets, SM),
            (received, VM),
            (alignment, HB),
            (bias_part, VM),
        ),
        (
            (full, F32, VM),
            (full, F32, HB),
            ((frames, WIDE), BF16, HB),
            (stats_shape, F32, VM),
        ),
        [
            ((local_rows + WIDE, channels), BF16),
            small_acc,
            ((frames, window), BF16),
            ((frames, WIDE), BF16),
            tiles_of,
            tiles_of,
            tiles_of,
        ],
        2 * frames * WIDE * channels,
        20,
    )
    others = others_over_tm(stat)
    bias_total = (stat[EXTRA_ROW] + others[1][EXTRA_ROW]) + (
        others[0][EXTRA_ROW] + others[2][EXTRA_ROW]
    )

    act_one, middle, middle_far, unit_one, coef_one, stat_two, grad_edges, added = call(
        first_conv_kernel,
        (
            (info, SM),
            (upsampled, VM),
            *((one, VM) for one in (stat, *others)),
            (inverse, VM),
            (params_one, VM),
            (first_conv_weight, VM),
            (second_turned, VM),
        ),
        (
            (padded, BF16, HB),
            (full, F32, VM),
            (full, F32, HB),
            (full, BF16, HB),
            (coef_shape, F32, VM),
            (stats_shape, F32, VM),
            ((8, channels), F32, VM),
            ((8, channels), F32, VM),
        ),
        [small_acc, (padded, BF16), (full, BF16), tiles_of, 2, tiles_of, tiles_of],
        conv_flops,
        28,
    )
    others_two = others_over_tm(stat_two)

    act_two, inner_two, coef_two, stat_three = call(
        second_norm_kernel,
        (
            (info, SM),
            (grad_act_two, HB),
            (middle, VM),
            *((one, VM) for one in (stat_two, *others_two)),
            (inverse, VM),
            (params_two, VM),
            (added, VM),
        ),
        (
            (padded, BF16, HB),
            (full, BF16, HB),
            (coef_shape, F32, VM),
            (stats_shape, F32, VM),
        ),
        [
            small_acc,
            (full, BF16),
            (padded, BF16),
            (full, BF16),
            tiles_of,
            tiles_of,
            2,
            tiles_of,
        ],
        2 * frames * channels * 100,
        28,
    )
    others_three = others_over_tm(stat_three)
    grad_middle, middle_edges, inner_one, back_two, stat_four = call(
        first_back_kernel,
        (
            (info, SM),
            (inner_two, HB),
            (middle_far, HB),
            *((one, VM) for one in (stat_three, *others_three)),
            (inverse, VM),
            (coef_two, VM),
            (coef_one, VM),
            (unit_one, HB),
            (turned(first_conv_weight), VM),
        ),
        (
            (full, BF16, HB),
            ((8, channels), F32, VM),
            (full, BF16, HB),
            ((40, channels), F32, VM),
            (stats_shape, F32, VM),
        ),
        [
            small_acc,
            ((ROWS, channels), F32),
            (full, BF16),
            (full, F32),
            (full, BF16),
            (full, BF16),
            (padded, BF16),
            *([tiles_of] * 5),
        ],
        conv_flops,
        40,
    )
    others_four = others_over_tm(stat_four)
    grad_before, grad_own, grad_after, back_one = call(
        buffer_gradient_kernel,
        (
            (info, SM),
            (tile_offsets, SM),
            (inner_one, HB),
            (unit_one, HB),
            (cotangent, HB),
            (wide, HB),
            *((one, VM) for one in (stat_four, *others_four)),
            (inverse, VM),
            (coef_one, VM),
        ),
        (
            ((halo, channels), F32, VM),
            ((local_rows, channels), F32, VM),
            ((halo, channels), F32, VM),
            ((40, channels), F32, VM),
        ),
        [
            (full, BF16),
            ((local_rows + WIDE, channels), F32),
            *([(full, BF16)] * 3),
            ((frames, WIDE), BF16),
            *([tiles_of] * 4),
        ],
        2 * frames * WIDE * channels,
        36,
    )

    row_places = (send_order[0] >> 3) * (8 * (channels // 128)) + (send_order[0] & 7)
    from_before, from_after = from_neighbours(grad_before, grad_after)
    return_rows = jnp.concatenate(
        [grad_own[:halo] + from_before, grad_own[halo:-halo], grad_own[-halo:] + from_after]
    ).astype(BF16)
    returned = lax.all_to_all(
        return_rows.reshape(groups, piece_rows, channels), "seq", 0, 0, tiled=True
    )

    bits = [b for b in range(12) if (1 << b) < groups]
    orders = (bits[1:], bits[1:][::-1])
    second_keep, second_give = call(
        weight_gradient_kernel,
        ((info, SM), (after(act_two, back_one), HB), (grad_branch, HB), (grad_edges, VM)),
        (((3 * channels // 2, channels), F32, VM), ((3 * channels // 2, channels), BF16, VM)),
        [((3 * channels, channels), F32), (padded, BF16), (padded, BF16), tiles_of, tiles_of],
        10**6,
        24,
    )

    returned, second_keep, second_give = lax.optimization_barrier(
        (returned, second_keep, second_give)
    )
    rounds = [returned, shifted(returned, "tm", 1)]
    first_keep, first_give = call(
        weight_gradient_kernel,
        ((info, SM), (act_one, HB), (after(grad_middle, returned), HB), (middle_edges, VM)),
        (((3 * channels // 2, channels), F32, VM), ((3 * channels // 2, channels), BF16, VM)),
        [((3 * channels, channels), F32), (padded, BF16), (padded, BF16), tiles_of, tiles_of],
        10**6,
        24,
    )

    keeps, gives = [second_keep, first_keep], [second_give, first_give]
    gots = [swapped(give, bits[0]) for give in gives]
    for turn, pair in enumerate(zip(*orders)):
        count = keeps[0].shape[0] // 2
        out = call(
            functools.partial(halves_kernel, pair),
            ((info, SM), *((one, VM) for both in zip(keeps, gots) for one in both)),
            (((count, channels), F32, VM), ((count, channels), BF16, VM)) * 2,
            [((2 * count, channels), F32)] * 2,
            10**6,
            16,
        )
        keeps, gives = [out[0], out[2]], [out[1], out[3]]
        if turn == 0:
            rounds[1], keeps, gives = lax.optimization_barrier((rounds[1], keeps, gives))
            rounds.append(shifted(rounds[1], "tm", 1))
        gots = [swapped(give, bit) for give, bit in zip(gives, pair)]
    row_sums = [keep + got.astype(F32) for keep, got in zip(keeps, gots)]
    placed = scattered(None, rounds[:2], (0, 1), copies, info, row_places)
    rounds[2], row_sums, placed = lax.optimization_barrier((rounds[2], row_sums, placed))
    sums = gathered_over_tm(summed_over_tm(row_sums))
    rounds[2], sums = lax.optimization_barrier((rounds[2], sums))
    rounds.append(shifted(rounds[2], "tm", 1))

    act_two, _ = lax.optimization_barrier((act_two, sums))
    (frames_out,) = call(
        second_conv_kernel,
        (
            (info, SM),
            (act_two, HB),
            (upsampled_far, HB),
            (second_conv_weight, VM),
            (second_conv_bias[None], VM),
        ),
        ((full, BF16, HB),),
        [(padded, BF16), (full, F32), (full, BF16), tiles_of, 2, tiles_of, tiles_of],
        10**6,
        36,
    )


    params_grad = [
        jnp.concatenate([back[8 : 8 + UTTS], back[0:UTTS]], axis=1) for back in (back_one, back_two)
    ]
    style_grad = jnp.dot(
        params_grad[0], first_affine_weight.astype(F32).T, precision=PRECISE
    ) + jnp.dot(params_grad[1], second_affine_weight.astype(F32).T, precision=PRECISE)
    style_block = jnp.zeros((8, channels), BF16).at[:, : style_rows.shape[1]].set(style_rows)
    small = jnp.concatenate(
        [
            back_one[8:16].astype(BF16),
            back_one[0:8].astype(BF16),
            back_two[8:16].astype(BF16),
            back_two[0:8].astype(BF16),
            style_block,
            jnp.zeros((8, channels), BF16).at[0].set(bias_total.astype(BF16)),
        ]
    )
    rows = sums.shape[1]
    held = [jnp.concatenate([sums[0], small]), sums[1]]
    for pair in zip(*orders):
        others = [swapped(one, bit) for one, bit in zip(held, pair)]
        held = call(
            functools.partial(join_kernel, pair),
            ((info, SM), *((one, VM) for both in zip(held, others) for one in both)),
            tuple(((2 * one.shape[0], channels), BF16, VM) for one in held),
            [],
            10**6,
            16,
        )
    rounds[3], held, frames_out = lax.optimization_barrier((rounds[3], list(held), frames_out))
    others = [swapped(one, bits[0]) for one in held]
    (
        second_conv_grad,
        first_conv_grad,
        first_affine_grad,
        first_shift_grad,
        second_affine_grad,
        second_shift_grad,
        second_bias_grad,
    ) = call(
        functools.partial(final_kernel, orders, rows),
        (
            (info, SM),
            (held[0], VM),
            (others[0], VM),
            (held[1], VM),
            (others[1], VM),
        ),
        (
            ((3 * channels, channels), F32, VM),
            ((3 * channels, channels), F32, VM),
            *(
                (((style_vec.shape[1], 2 * channels), F32, VM), ((1, 2 * channels), F32, VM)) * 2
            ),
            ((1, channels), F32, VM),
        ),
        [],
        10**6,
        28,
    )
    placed = scattered(placed, rounds[2:], (2, 3), copies, info, row_places)
    lanes = channels // 128
    phonemes_grad = (
        placed.reshape(slot_count // 8, lanes, 8, 128)
        .transpose(0, 2, 1, 3)
        .reshape(slot_count, channels)
    )
    return (
        frames_out,
        phonemes_grad,
        style_grad,
        first_affine_grad,
        first_shift_grad[0],
        first_conv_grad,
        second_affine_grad,
        second_shift_grad[0],
        second_conv_grad,
        second_bias_grad[0],
    )


def solution(mesh):
    split, whole = ("seq", "tm"), P()
    in_specs = (
        P("seq", None),
        P("seq", None),
        P("seq", None),
        P("seq", None),
        P(split),
        P(split, None),
        P("seq", None),
        *([whole] * 7),
        P(split, None),
    )
    out_specs = (P(split, None), P("seq", None), P("seq", None), *([whole] * 7))
    return jax.shard_map(
        on_device, mesh=mesh, in_specs=in_specs, out_specs=out_specs, check_vma=False
    )
```

```python
import functools

import jax
import jax.numpy as jnp
from jax import lax
from jax.experimental import pallas as pl
from jax.experimental.pallas import tpu as pltpu
from jax.sharding import PartitionSpec as P

EPSILON = 1e-05
ROOT_HALF = 0.7071067811865476
PRECISE = lax.Precision.HIGHEST
F32, BF16, I32 = jnp.float32, jnp.bfloat16, jnp.int32
UTTS = 4
PAD = 16
ROWS = 1024
BLOCK = 128
WIDE = 256
MIB = 2**20

STAT_ROWS = 24
FIRST_ROW, LAST_ROW, EXTRA_ROW, FIRST_GRAD, LAST_GRAD = 16, 17, 18, 19, 20
SMALL_ROWS = 48
BITS_AT = 12


def owner_at(ends, position):
    return sum((position >= end).astype(I32) for end in ends)


def tile_of(ref, index, offset=0):
    return ref.at[pl.ds(pl.multiple_of(offset + index * ROWS, PAD), ROWS), :]


class Stream:
    def __init__(self, source, target, sems, source_offset=0, target_offset=0):
        self.ends = (source, source_offset, target, target_offset)
        self.sems = sems
        self.tiles = sems.shape[0]

    def tile(self, index):
        source, source_offset, target, target_offset = self.ends
        return pltpu.make_async_copy(
            tile_of(source, index, source_offset),
            tile_of(target, index, target_offset),
            self.sems.at[index],
        )

    def start(self):
        for index in range(self.tiles):
            self.tile(index).start()

    def finish(self):
        for index in range(self.tiles):
            self.tile(index).wait()


def edge_copies(source, target, sems):
    last = source.shape[0] - PAD
    return [
        pltpu.make_async_copy(
            source.at[pl.ds(at, PAD), :], target.at[pl.ds(at, PAD), :], sems.at[k]
        )
        for k, at in enumerate((0, last))
    ]


def rows_of(start, shape):
    return start + lax.broadcasted_iota(I32, shape, 0)


def fold_rows(values):
    return jnp.sum(values.reshape(values.shape[0] // 8, 8, values.shape[1]), axis=0)


def by_utterance(ends, start, count, uniform_body, mixed_body):
    low, high = owner_at(ends, start), owner_at(ends, start + count - 1)

    @pl.when(low == high)
    def _():
        uniform_body(low)

    @pl.when(low != high)
    def _():
        def step(u, carry):
            lower = jnp.int32(-1)
            upper = jnp.int32(2**30)
            for k in range(UTTS):
                lower = jnp.where(u == k + 1, ends[k], lower)
                upper = jnp.where(u == k, ends[k], upper)

            def mask(shape):
                rows = rows_of(start, shape)
                return (rows >= lower) & (rows < upper)

            mixed_body(u, mask)
            return carry

        lax.fori_loop(low, high + 1, step, 0)


class Blocks:
    def __init__(self, ends, base, channels):
        self.ends, self.base, self.channels = ends, base, channels

    def plain(self, start, body):
        for inside in range(0, ROWS, BLOCK):
            first = self.base + start + inside
            low = owner_at(self.ends, first)
            alone = (low == owner_at(self.ends, first + BLOCK - 1)).astype(F32)
            body(start + inside, low, alone)

    def mixed(self, start, body):
        def step(i, carry):
            at = pl.multiple_of(start + i * BLOCK, BLOCK)
            by_utterance(
                self.ends,
                self.base + at,
                BLOCK,
                lambda u: None,
                lambda u, mask: body(at, u, mask((BLOCK, self.channels))),
            )
            return carry

        low = owner_at(self.ends, self.base + start)

        @pl.when(low != owner_at(self.ends, self.base + start + ROWS - 1))
        def _():
            lax.fori_loop(0, ROWS // BLOCK, step, 0)


def row(ref, index):
    return ref[pl.ds(index, 1), :]


def logistic(values):
    return 0.5 * jnp.tanh(0.5 * values) + 0.5


def taps_of(padded_ref, ends, start, base):
    channels = padded_ref.shape[1]
    block = padded_ref[pl.ds(start, ROWS + 2 * PAD), :].astype(F32)
    positions = rows_of(base + start, (ROWS, channels))
    cut_left = positions == ends[0]
    cut_right = positions + 1 == ends[0]
    for end in ends[1:]:
        cut_left = cut_left | (positions == end)
        cut_right = cut_right | (positions + 1 == end)
    before = jnp.where(cut_left, 0.0, block[PAD - 1 : PAD - 1 + ROWS]).astype(BF16)
    after = jnp.where(cut_right, 0.0, block[PAD + 1 : PAD + 1 + ROWS]).astype(BF16)
    return before, padded_ref[pl.ds(start + PAD, ROWS), :], after


def convolved(taps, weight_ref):
    channels = weight_ref.shape[1]
    return sum(
        jnp.dot(tap, weight_ref[k * channels : (k + 1) * channels, :], preferred_element_type=F32)
        for k, tap in enumerate(taps)
    )


def convolved_back(taps, weight_ref):
    channels = weight_ref.shape[1]
    return sum(
        lax.dot_general(
            tap,
            weight_ref[k * channels : (k + 1) * channels, :],
            (((1,), (1,)), ((), ())),
            preferred_element_type=F32,
        )
        for k, tap in enumerate(taps)
    )


def for_blocks(first, count, size, body, unroll=1):
    def step(i, carry):
        body(pl.multiple_of(first + i * size, size))
        return carry

    lax.fori_loop(0, count // size, step, 0, unroll=unroll)


def for_tiles(count, body):
    def step(i, carry):
        body(i, pl.multiple_of(i * ROWS, ROWS))
        return carry

    lax.fori_loop(0, count // ROWS, step, 0)


def wait_next(streams, i, count):
    @pl.when(i + 1 < count // ROWS)
    def _():
        for stream in streams:
            stream.tile(i + 1).wait()


def sum_over_tm(own_ref, other_refs, first, count):
    one, two, three = other_refs
    part = pl.ds(first, count)
    return (own_ref[part, :] + two[part, :]) + (one[part, :] + three[part, :])


def finish_stats(acc_ref, stat_ref):
    for kind in range(2):
        for u in range(8):
            at = kind * 8 + u
            if u < UTTS:
                first = (kind * (UTTS + 1) + u) * 8
                stat_ref[at : at + 1, :] = jnp.sum(
                    acc_ref[first : first + 8, :], axis=0, keepdims=True
                )
            else:
                stat_ref[at : at + 1, :] = jnp.zeros_like(stat_ref[at : at + 1, :])
    stat_ref[16:24, :] = jnp.zeros_like(stat_ref[16:24, :])


ACC_ROWS = 2 * (UTTS + 1) * 8


def add_stats(acc_ref, u, first, second, weight=None):
    for kind, term in enumerate((first, second)):
        at = pl.ds(pl.multiple_of((kind * (UTTS + 1) + u) * 8, 8), 8)
        term = fold_rows(term)
        acc_ref[at, :] += term if weight is None else term * weight


def read_ends(info_ref):
    return [info_ref[k] for k in range(UTTS)]


def halo_owner(info_ref, ends, base, frames):
    before = jnp.where(base == 0, UTTS, owner_at(ends, base - 1))
    return before, owner_at(ends, base + frames)


def gradient_kernel(
    info_ref,
    cot_hbm,
    weight_ref,
    out_hbm,
    padded_hbm,
    bias_ref,
    cot_ref,
    padded_ref,
    out_ref,
    cot_sems,
    padded_sems,
    out_sems,
):
    frames, channels = cot_ref.shape
    ends = read_ends(info_ref)
    base = info_ref[8]
    cot_in = Stream(cot_hbm, cot_ref, cot_sems)
    padded_out = Stream(padded_ref, padded_hbm, padded_sems, PAD)
    outward = Stream(out_ref, out_hbm, out_sems)
    cot_in.start()
    padded_ref[0:PAD, :] = jnp.zeros((PAD, channels), BF16)
    padded_ref[PAD + frames :, :] = jnp.zeros((PAD, channels), BF16)
    bias_ref[...] = jnp.zeros_like(bias_ref)

    def scale(start):
        here = cot_ref[pl.ds(start, BLOCK), :].astype(F32) * ROOT_HALF
        here = jnp.where(rows_of(base + start, (BLOCK, channels)) < ends[UTTS - 1], here, 0.0)
        rounded = here.astype(BF16)
        padded_ref[pl.ds(start + PAD, BLOCK), :] = rounded
        bias_ref[0:8, :] += fold_rows(rounded.astype(F32))

    def scale_tile(i, start):
        cot_in.tile(i).wait()
        for_blocks(start, ROWS, BLOCK, scale)
        padded_out.tile(i).start()

    for_tiles(frames, scale_tile)

    def conv(i, start):
        before, here, after = taps_of(padded_ref, ends, start, base)
        total = convolved((after, here, before), weight_ref)
        out_ref[pl.ds(start, ROWS), :] = total.astype(BF16)
        outward.tile(i).start()

    for_tiles(frames, conv)
    bias_ref[8:9, :] = padded_ref[PAD : 2 * PAD, :].astype(F32)[0:1]
    bias_ref[9:10, :] = padded_ref[frames : frames + PAD, :].astype(F32)[PAD - 1 :]
    padded_out.finish()
    outward.finish()


def upsample_kernel(
    info_ref,
    offset_ref,
    rows_ref,
    align_hbm,
    bias_ref,
    out_ref,
    out_hbm,
    wide_hbm,
    stat_ref,
    buffer_ref,
    acc_ref,
    align_ref,
    wide_ref,
    align_sems,
    out_sems,
    wide_sems,
):
    frames, channels = out_ref.shape
    align_in = Stream(align_hbm, align_ref, align_sems)
    outward = Stream(out_ref, out_hbm, out_sems)
    wide_out = Stream(wide_ref, wide_hbm, wide_sems)
    align_in.start()
    window = align_ref.shape[1]
    tiles = offset_ref.shape[0]
    rows = frames // tiles
    groups, both = rows_ref.shape[:2]
    halo = window // 2
    piece = next(n for n in range(both // 2, both) if both - n == min(halo, n))
    own, extra = groups * piece, both - piece
    ends = read_ends(info_ref)
    slot_ends = [info_ref[UTTS + k] for k in range(UTTS)]
    base, slot_base = info_ref[8], info_ref[9]
    for s in range(groups):
        buffer_ref[halo + s * piece : halo + (s + 1) * piece, :] = rows_ref[s, 0:piece, :]
    for n in range(halo // extra):
        buffer_ref[n * extra : (n + 1) * extra, :] = rows_ref[
            groups - halo // extra + n, piece:both, :
        ]
        at = halo + own + n * extra
        buffer_ref[at : at + extra, :] = rows_ref[n, piece:both, :]
    buffer_ref[2 * halo + own :, :] = jnp.zeros_like(buffer_ref[2 * halo + own :, :])
    acc_ref[...] = jnp.zeros_like(acc_ref)

    def step(i):
        start = pl.multiple_of(i * rows, rows)
        shift = offset_ref[i] - slot_base
        aligned = pl.multiple_of((shift // PAD) * PAD, PAD)
        block = align_ref[pl.ds(start, rows), :].astype(F32)
        block = jnp.concatenate([block, jnp.zeros((rows, WIDE - window), F32)], axis=1)
        block = pltpu.roll(block, shift - aligned, 1)
        slots = slot_base + aligned + lax.broadcasted_iota(I32, (rows, WIDE), 1)
        slot_owner = owner_at(slot_ends, slots)
        frame_owner = owner_at(ends, rows_of(base + start, (rows, WIDE)))
        match = (slot_owner == frame_owner) & (frame_owner < UTTS)
        block = jnp.where(match, block, 0.0).astype(BF16)
        wide_ref[pl.ds(start, rows), :] = block
        out_ref[pl.ds(start, rows), :] = jnp.dot(
            block, buffer_ref[pl.ds(aligned, WIDE), :], preferred_element_type=F32
        )

    def blocks(i, start):
        align_in.tile(i).wait()
        each = ROWS // rows

        def four(k, carry):
            for n in range(4):
                step(i * each + k * 4 + n)
            return carry

        lax.fori_loop(0, each // 4, four, 0)
        outward.tile(i).start()
        wide_out.tile(i).start()
        for_blocks(
            start, ROWS, BLOCK, lambda at: value_sums(out_ref, acc_ref, ends, base, at)
        )

    for_tiles(frames, blocks)
    finish_stats(acc_ref, stat_ref)
    stat_ref[FIRST_ROW : FIRST_ROW + 1, :] = out_ref[0:1, :]
    stat_ref[LAST_ROW : LAST_ROW + 1, :] = out_ref[frames - 1 : frames, :]
    stat_ref[EXTRA_ROW : EXTRA_ROW + 1, :] = jnp.sum(bias_ref[0:8, :], axis=0, keepdims=True)
    stat_ref[FIRST_GRAD : FIRST_GRAD + 2, :] = bias_ref[8:10, :]
    outward.finish()
    wide_out.finish()


def value_sums(out_ref, acc_ref, ends, base, start):
    channels = out_ref.shape[1]

    def uniform(u):
        here = out_ref[pl.ds(start, BLOCK), :]
        add_stats(acc_ref, u, here, here * here)

    def mixed(u, mask):
        here = jnp.where(mask((BLOCK, channels)), out_ref[pl.ds(start, BLOCK), :], 0.0)
        add_stats(acc_ref, u, here, here * here)

    by_utterance(ends, base + start, BLOCK, uniform, mixed)


def write_coefficients(own_ref, other_refs, inverse_ref, params_ref, coef_ref):
    channels = inverse_ref.shape[1]
    inverse = inverse_ref[...]
    total = sum_over_tm(own_ref, other_refs, 0, 8)
    square = sum_over_tm(own_ref, other_refs, 8, 8)
    mean = total * inverse
    real = inverse > 0.0
    rstd = jnp.where(real, lax.rsqrt(square * inverse - mean * mean + EPSILON), 0.0)
    gain = jnp.where(real, 1.0 + params_ref[:, 0:channels], 0.0)
    shift = jnp.where(real, params_ref[:, channels : 2 * channels], 0.0)
    coef_ref[0:8, :] = rstd
    coef_ref[8:16, :] = mean * rstd
    coef_ref[16:24, :] = gain * rstd
    coef_ref[24:32, :] = 0.5 * gain
    coef_ref[32:40, :] = 0.5 * shift
    coef_ref[40:48, :] = 0.5 * gain * rstd
    coef_ref[48:56, :] = 0.5 * (shift - mean * gain * rstd)
    coef_ref[56:57, :] = row(other_refs[0], LAST_ROW)
    coef_ref[57:58, :] = row(other_refs[2], FIRST_ROW)


UNIT, HALF_OF_UNIT, HALF_OF_VALUE = (0, 8), (24, 32), (40, 48)


def unit_of(values, coef_ref, u):
    return values * row(coef_ref, u) - row(coef_ref, 8 + u)


def half_normed(values, coef_ref, u, rows):
    return values * row(coef_ref, rows[0] + u) + row(coef_ref, rows[1] + u)


def twice_logistic(half):
    return jnp.tanh(half) + 1.0


def activation(values, coef_ref, u):
    half = half_normed(values, coef_ref, u, HALF_OF_VALUE)
    return half * twice_logistic(half)


def edge_rows(padded_ref, before, after):
    channels = padded_ref.shape[1]
    padded_ref[0:PAD, :] = jnp.broadcast_to(before, (PAD, channels)).astype(BF16)
    last = padded_ref.shape[0] - PAD
    padded_ref[last:, :] = jnp.broadcast_to(after, (PAD, channels)).astype(BF16)


def first_conv_kernel(
    info_ref,
    values_ref,
    own_ref,
    one_ref,
    two_ref,
    three_ref,
    inverse_ref,
    params_ref,
    weight_ref,
    turned_ref,
    act_hbm,
    out_ref,
    out_hbm,
    unit_hbm,
    coef_ref,
    stat_ref,
    edge_ref,
    added_ref,
    acc_ref,
    act_ref,
    unit_ref,
    act_sems,
    edge_sems,
    out_sems,
    unit_sems,
):
    frames, channels = values_ref.shape
    tiles = frames // ROWS
    act_out = Stream(act_ref, act_hbm, act_sems, PAD, PAD)
    unit_out = Stream(unit_ref, unit_hbm, unit_sems)
    outward = Stream(out_ref, out_hbm, out_sems)
    ends = read_ends(info_ref)
    base = info_ref[8]
    blocks = Blocks(ends, base, channels)
    write_coefficients(own_ref, (one_ref, two_ref, three_ref), inverse_ref, params_ref, coef_ref)
    acc_ref[...] = jnp.zeros_like(acc_ref)
    owner_before, owner_after = halo_owner(info_ref, ends, base, frames)
    edge_rows(
        act_ref,
        activation(row(one_ref, LAST_ROW), coef_ref, owner_before),
        activation(row(three_ref, FIRST_ROW), coef_ref, owner_after),
    )
    edges = edge_copies(act_ref, act_hbm, edge_sems)
    for edge in edges:
        edge.start()

    def act_parts(at, u):
        unit = unit_of(values_ref[pl.ds(at, BLOCK), :], coef_ref, u)
        half = half_normed(unit, coef_ref, u, HALF_OF_UNIT)
        return unit, half * twice_logistic(half)

    def act_plain(at, u, alone):
        unit, act = act_parts(at, u)
        unit_ref[pl.ds(at, BLOCK), :] = unit.astype(BF16)
        act_ref[pl.ds(at + PAD, BLOCK), :] = act.astype(BF16)

    def act_mixed(at, u, keep):
        here, there = pl.ds(at, BLOCK), pl.ds(at + PAD, BLOCK)
        unit, act = act_parts(at, u)
        unit_ref[here, :] = jnp.where(keep, unit, unit_ref[here, :].astype(F32)).astype(BF16)
        act_ref[there, :] = jnp.where(keep, act, act_ref[there, :].astype(F32)).astype(BF16)

    def sums_plain(at, u, alone):
        here = out_ref[pl.ds(at, BLOCK), :]
        add_stats(acc_ref, u, here, here * here, alone)

    def sums_mixed(at, u, keep):
        here = jnp.where(keep, out_ref[pl.ds(at, BLOCK), :], 0.0)
        add_stats(acc_ref, u, here, here * here)

    for turn in range(-1, tiles + 1):
        if turn + 1 < tiles:
            blocks.plain((turn + 1) * ROWS, act_plain)
        if 0 <= turn < tiles:
            start = turn * ROWS
            out_ref[start : start + ROWS, :] = convolved(
                taps_of(act_ref, ends, start, base), weight_ref
            )
        if turn > 0:
            blocks.plain((turn - 1) * ROWS, sums_plain)
        if turn + 1 < tiles:
            blocks.mixed((turn + 1) * ROWS, act_mixed)
            act_out.tile(turn + 1).start()
            unit_out.tile(turn + 1).start()
        if 0 <= turn < tiles:
            outward.tile(turn).start()
        if turn > 0:
            blocks.mixed((turn - 1) * ROWS, sums_mixed)
    edge_ref[...] = jnp.zeros_like(edge_ref)
    added_ref[...] = jnp.zeros_like(added_ref)
    neighbours = (
        (one_ref, LAST_GRAD, owner_before, owner_at(ends, base), 2 * channels),
        (three_ref, FIRST_GRAD, owner_after, owner_at(ends, base + frames - 1), 0),
    )
    for k, (ref, at, theirs, ours, tap) in enumerate(neighbours):
        valid = (theirs == ours) & (ours < UTTS)
        edge_ref[k : k + 1, :] = jnp.where(valid, ref[at : at + 1, :], 0.0)
        rows = jnp.broadcast_to(edge_ref[k : k + 1, :], (PAD, channels)).astype(BF16)
        added_ref[k : k + 1, :] = jnp.dot(
            rows, turned_ref[tap : tap + channels, :], preferred_element_type=F32
        )[0:1]
    finish_stats(acc_ref, stat_ref)
    stat_ref[FIRST_ROW : FIRST_ROW + 1, :] = out_ref[0:1, :]
    stat_ref[LAST_ROW : LAST_ROW + 1, :] = out_ref[frames - 1 : frames, :]
    act_out.finish()
    unit_out.finish()
    outward.finish()
    for edge in edges:
        edge.wait()


def slope_and_sums(gradient, values, coef_ref, u, rows):
    half = half_normed(values, coef_ref, u, rows)
    gate = twice_logistic(half)
    act = half * gate
    inner = gradient * (gate * (half - 0.5 * act + 0.5))
    return act, inner, inner * values


def second_norm_kernel(
    info_ref,
    gradient_hbm,
    values_ref,
    own_ref,
    one_ref,
    two_ref,
    three_ref,
    inverse_ref,
    params_ref,
    added_ref,
    act_hbm,
    inner_hbm,
    coef_ref,
    stat_ref,
    acc_ref,
    gradient_ref,
    act_ref,
    inner_ref,
    gradient_sems,
    act_sems,
    edge_sems,
    inner_sems,
):
    frames, channels = values_ref.shape
    gradient_in = Stream(gradient_hbm, gradient_ref, gradient_sems)
    outward = [
        Stream(act_ref, act_hbm, act_sems, PAD, PAD),
        Stream(inner_ref, inner_hbm, inner_sems),
    ]
    gradient_in.start()
    ends = read_ends(info_ref)
    base = info_ref[8]
    write_coefficients(own_ref, (one_ref, two_ref, three_ref), inverse_ref, params_ref, coef_ref)
    acc_ref[...] = jnp.zeros_like(acc_ref)
    owner_before, owner_after = halo_owner(info_ref, ends, base, frames)
    edge_rows(
        act_ref,
        activation(row(one_ref, LAST_ROW), coef_ref, owner_before),
        activation(row(three_ref, FIRST_ROW), coef_ref, owner_after),
    )

    edges = edge_copies(act_ref, act_hbm, edge_sems)
    for edge in edges:
        edge.start()

    def step(start):
        here = pl.ds(start, BLOCK)
        there = pl.ds(start + PAD, BLOCK)

        def parts(u):
            return slope_and_sums(
                gradient_ref[here, :].astype(F32), values_ref[here, :], coef_ref, u, HALF_OF_VALUE
            )

        def uniform(u):
            act, inner, cross = parts(u)
            act_ref[there, :] = act.astype(BF16)
            inner_ref[here, :] = inner.astype(BF16)
            add_stats(acc_ref, u, inner, cross)

        def mixed(u, mask):
            keep = mask((BLOCK, channels))
            act, inner, cross = parts(u)
            act_ref[there, :] = jnp.where(keep, act, act_ref[there, :].astype(F32)).astype(BF16)
            old = inner_ref[here, :].astype(F32)
            inner_ref[here, :] = jnp.where(keep, inner, old).astype(BF16)
            add_stats(acc_ref, u, jnp.where(keep, inner, 0.0), jnp.where(keep, cross, 0.0))

        by_utterance(ends, base + start, BLOCK, uniform, mixed)

    def tile(i, start):
        gradient_in.tile(i).wait()
        for k, at in enumerate((0, frames - PAD)):

            @pl.when(i == at // ROWS)
            def _(k=k, at=at):
                edge = gradient_ref[at : at + PAD, :].astype(F32)
                inside = rows_of(0, (PAD, channels)) == k * (PAD - 1)
                edge = edge + jnp.where(inside, added_ref[k : k + 1, :], 0.0)
                gradient_ref[at : at + PAD, :] = edge.astype(BF16)

        for_blocks(start, ROWS, BLOCK, step)
        for stream in outward:
            stream.tile(i).start()

    for_tiles(frames, tile)
    finish_stats(acc_ref, stat_ref)
    stat_ref[FIRST_ROW : FIRST_ROW + 1, :] = inner_ref[0:PAD, :].astype(F32)[0:1]
    stat_ref[LAST_ROW : LAST_ROW + 1, :] = inner_ref[frames - PAD :, :].astype(F32)[PAD - 1 :]
    for stream in outward:
        stream.finish()
    for edge in edges:
        edge.wait()


def second_conv_kernel(
    info_ref,
    act_hbm,
    values_hbm,
    weight_ref,
    bias_ref,
    out_hbm,
    act_ref,
    values_ref,
    out_ref,
    act_sems,
    edge_sems,
    values_sems,
    out_sems,
):
    frames, channels = values_ref.shape
    ends = read_ends(info_ref)
    base = info_ref[8]
    bias = bias_ref[...].astype(F32)
    act_in = Stream(act_hbm, act_ref, act_sems, PAD, PAD)
    values_in = Stream(values_hbm, values_ref, values_sems)
    outward = Stream(out_ref, out_hbm, out_sems)
    edges = edge_copies(act_hbm, act_ref, edge_sems)
    for edge in edges:
        edge.start()
    act_in.start()
    values_in.start()
    for edge in edges:
        edge.wait()
    act_in.tile(0).wait()

    def step(i, start):
        here = pl.ds(start, ROWS)
        wait_next([act_in], i, frames)
        values_in.tile(i).wait()
        branch = convolved(taps_of(act_ref, ends, start, base), weight_ref) + bias
        valid = rows_of(base + start, (ROWS, channels)) < ends[UTTS - 1]
        total = jnp.where(valid, (values_ref[here, :] + branch) * ROOT_HALF, 0.0)
        out_ref[here, :] = total.astype(BF16)
        outward.tile(i).start()

    for_tiles(frames, step)
    outward.finish()


def weight_gradient_kernel(
    info_ref,
    act_hbm,
    gradient_hbm,
    edge_ref,
    keep_ref,
    give_ref,
    out_ref,
    act_ref,
    gradient_ref,
    act_sems,
    gradient_sems,
):
    frames = act_ref.shape[0] - 2 * PAD
    channels = act_ref.shape[1]
    ends = read_ends(info_ref)
    base = info_ref[8]
    act_in = Stream(act_hbm, act_ref, act_sems, PAD, PAD)
    gradient_in = Stream(gradient_hbm, gradient_ref, gradient_sems, 0, PAD)
    for index in range(frames // ROWS):
        gradient_in.tile(index).start()
        act_in.tile(index).start()
    out_ref[...] = jnp.zeros_like(out_ref)
    edge_rows(gradient_ref, edge_ref[0:1, :], edge_ref[1:2, :])
    gradient_in.tile(0).wait()

    def step(i, start):
        wait_next([gradient_in], i, frames)
        act_in.tile(i).wait()
        before, here, after = taps_of(gradient_ref, ends, start, base)
        act = act_ref[pl.ds(start + PAD, ROWS), :]
        for k, tap in enumerate((after, here, before)):
            out_ref[k * channels : (k + 1) * channels, :] += lax.dot_general(
                act, tap, (((0,), (0,)), ((), ())), preferred_element_type=F32
            )

    for_tiles(frames, step)
    write_halves(info_ref, 0, out_ref, keep_ref, give_ref)


def write_halves(info_ref, bit, total_ref, keep_ref, give_ref):
    half = keep_ref.shape[0]
    mine = info_ref[BITS_AT + bit]
    keep_ref[...] = total_ref[pl.ds(pl.multiple_of(mine * half, PAD), half), :]
    give_ref[...] = total_ref[pl.ds(pl.multiple_of((1 - mine) * half, PAD), half), :].astype(BF16)


def halves_kernel(bits, info_ref, *refs):
    count = len(bits)
    inputs, outputs, totals = refs[: 2 * count], refs[2 * count : 4 * count], refs[4 * count :]
    for k, bit in enumerate(bits):
        totals[k][...] = inputs[2 * k][...] + inputs[2 * k + 1][...].astype(F32)
        write_halves(info_ref, bit, totals[k], outputs[2 * k], outputs[2 * k + 1])


def join_kernel(bits, info_ref, *refs):
    count = len(bits)
    for k, bit in enumerate(bits):
        part_ref, other_ref, out_ref = refs[2 * k], refs[2 * k + 1], refs[2 * count + k]
        half = part_ref.shape[0]
        mine = info_ref[BITS_AT + bit]
        out_ref[pl.ds(pl.multiple_of(mine * half, PAD), half), :] = part_ref[...]
        out_ref[pl.ds(pl.multiple_of((1 - mine) * half, PAD), half), :] = other_ref[...]


def block_order(order):
    places = []
    for index in range(1 << (len(order) + 1)):
        source, joined = index & 1, 0
        for at, bit in enumerate(order):
            source = 2 * source + ((index >> bit) & 1)
            joined += ((index >> bit) & 1) << at
        places.append((index & 1, source, joined))
    return places


def final_kernel(
    orders,
    rows,
    info_ref,
    second_ref,
    second_other_ref,
    first_ref,
    first_other_ref,
    second_out_ref,
    first_out_ref,
    first_affine_ref,
    first_shift_ref,
    second_affine_ref,
    second_shift_ref,
    bias_ref,
):
    channels = second_ref.shape[1]
    mine = info_ref[BITS_AT]
    gathered = []
    pairs = (
        (second_ref, second_other_ref, second_out_ref, rows + SMALL_ROWS),
        (first_ref, first_other_ref, first_out_ref, rows),
    )
    for k, (part_ref, other_ref, out_ref, step) in enumerate(pairs):
        for core, source, joined in block_order(orders[k]):
            here = pl.ds(joined * step, step)
            block = jnp.where(
                mine == core, part_ref[here, :].astype(F32), other_ref[here, :].astype(F32)
            )
            out_ref[source * rows : (source + 1) * rows, :] = block[:rows]
            if k == 0:
                gathered.append(block[rows:])
    styles = jnp.concatenate([block[32:40, 0:128] for block in gathered], axis=0)
    for at, (affine_ref, shift_ref) in enumerate(
        ((first_affine_ref, first_shift_ref), (second_affine_ref, second_shift_ref))
    ):
        for side in range(2):
            first = 16 * at + 8 * side
            sums = jnp.concatenate([block[first : first + 8] for block in gathered], axis=0)
            lanes = slice(side * channels, (side + 1) * channels)
            affine_ref[:, lanes] = lax.dot_general(
                styles, sums, (((0,), (0,)), ((), ())), precision=PRECISE
            )
            shift_ref[:, lanes] = jnp.sum(sums, axis=0, keepdims=True)
    biases = jnp.concatenate([block[40:48] for block in gathered], axis=0)
    bias_ref[...] = jnp.sum(biases, axis=0, keepdims=True)


def back_coefficients(own_ref, other_refs, inverse_ref, coef_ref, back_ref, of_values):
    inverse = inverse_ref[...]
    rstd, mean_rstd, scale = coef_ref[0:8, :], coef_ref[8:16, :], coef_ref[16:24, :]
    total = sum_over_tm(own_ref, other_refs, 0, 8)
    cross = sum_over_tm(own_ref, other_refs, 8, 8)
    if of_values:
        cross = rstd * cross - mean_rstd * total
    back_ref[0:8, :] = total
    back_ref[8:16, :] = cross
    slant = scale * cross * inverse
    back_ref[16:24, :] = scale * total * inverse - (mean_rstd * slant if of_values else 0.0)
    back_ref[24:32, :] = rstd * slant if of_values else slant
    back_ref[32:40, :] = scale


def inward(inner, values, back_ref, u):
    return inner * row(back_ref, 32 + u) - row(back_ref, 16 + u) - values * row(back_ref, 24 + u)


def first_back_kernel(
    info_ref,
    inner_hbm,
    middle_hbm,
    own_ref,
    one_ref,
    two_ref,
    three_ref,
    inverse_ref,
    coef_two_ref,
    coef_one_ref,
    unit_one_hbm,
    weight_ref,
    gradient_hbm,
    edge_ref,
    out_hbm,
    back_ref,
    stat_ref,
    acc_ref,
    full_ref,
    inner_ref,
    middle_ref,
    unit_one_ref,
    out_ref,
    gradient_ref,
    inner_sems,
    two_sems,
    one_sems,
    out_sems,
    gradient_sems,
):
    frames, channels = unit_one_ref.shape
    early = [
        Stream(inner_hbm, inner_ref, inner_sems),
        Stream(middle_hbm, middle_ref, two_sems),
    ]
    late = Stream(unit_one_hbm, unit_one_ref, one_sems)
    outward = Stream(out_ref, out_hbm, out_sems)
    gradient_out = Stream(gradient_ref, gradient_hbm, gradient_sems, PAD)
    for index in range(frames // ROWS):
        for stream in (*early, late):
            stream.tile(index).start()
    ends = read_ends(info_ref)
    base = info_ref[8]
    back_coefficients(own_ref, (one_ref, two_ref, three_ref), inverse_ref, coef_two_ref, back_ref, True)
    acc_ref[...] = jnp.zeros_like(acc_ref)
    owner_before, owner_after = halo_owner(info_ref, ends, base, frames)
    edge_rows(
        gradient_ref,
        inward(
            row(one_ref, LAST_ROW),
            row(coef_two_ref, 56),
            back_ref,
            owner_before,
        ),
        inward(
            row(three_ref, FIRST_ROW),
            row(coef_two_ref, 57),
            back_ref,
            owner_after,
        ),
    )

    def back_step(start):
        here = pl.ds(start, BLOCK)
        there = pl.ds(start + PAD, BLOCK)

        def now(u):
            return inward(
                inner_ref[here, :].astype(F32), middle_ref[here, :], back_ref, u
            )

        def uniform(u):
            gradient_ref[there, :] = now(u).astype(BF16)

        def mixed(u, mask):
            old = gradient_ref[there, :].astype(F32)
            gradient_ref[there, :] = jnp.where(mask((BLOCK, channels)), now(u), old).astype(BF16)

        by_utterance(ends, base + start, BLOCK, uniform, mixed)

    edge_ref[0:8, :] = gradient_ref[0:PAD, :].astype(F32)[0:8]
    edge_ref[1:2, :] = gradient_ref[PAD + frames :, :].astype(F32)[0:1]

    def back_tile(i):
        for stream in early:
            stream.tile(i).wait()
        for_blocks(pl.multiple_of(i * ROWS, ROWS), ROWS, BLOCK, back_step)
        gradient_out.tile(i).start()

    back_tile(0)

    def slope_step(start, row_start):
        here = pl.ds(start, BLOCK)

        def parts(u):
            unit = unit_one_ref[here, :].astype(F32)
            _, inner, cross = slope_and_sums(
                full_ref[pl.ds(row_start, BLOCK), :], unit, coef_one_ref, u, HALF_OF_UNIT
            )
            return inner, cross

        def uniform(u):
            inner, cross = parts(u)
            out_ref[here, :] = inner.astype(BF16)
            add_stats(acc_ref, u, inner, cross)

        def mixed(u, mask):
            keep = mask((BLOCK, channels))
            inner, cross = parts(u)
            old = out_ref[here, :].astype(F32)
            out_ref[here, :] = jnp.where(keep, inner, old).astype(BF16)
            add_stats(acc_ref, u, jnp.where(keep, inner, 0.0), jnp.where(keep, cross, 0.0))

        by_utterance(ends, base + start, BLOCK, uniform, mixed)

    def conv(i, start):
        @pl.when(i + 1 < frames // ROWS)
        def _():
            back_tile(i + 1)

        late.tile(i).wait()
        before, here, after = taps_of(gradient_ref, ends, start, base)
        full_ref[...] = convolved_back((after, here, before), weight_ref)
        for_blocks(0, ROWS, BLOCK, lambda inside: slope_step(start + inside, inside))
        outward.tile(i).start()

    for_tiles(frames, conv)
    finish_stats(acc_ref, stat_ref)
    outward.finish()
    gradient_out.finish()


def buffer_gradient_kernel(
    info_ref,
    offset_ref,
    inner_hbm,
    unit_hbm,
    cot_hbm,
    wide_hbm,
    own_ref,
    one_ref,
    two_ref,
    three_ref,
    inverse_ref,
    coef_ref,
    before_ref,
    out_ref,
    after_ref,
    back_ref,
    up_ref,
    total_ref,
    inner_ref,
    unit_ref,
    cot_ref,
    wide_ref,
    inner_sems,
    unit_sems,
    cot_sems,
    wide_sems,
):
    frames, channels = unit_ref.shape
    streams = [
        Stream(inner_hbm, inner_ref, inner_sems),
        Stream(unit_hbm, unit_ref, unit_sems),
        Stream(cot_hbm, cot_ref, cot_sems),
        Stream(wide_hbm, wide_ref, wide_sems),
    ]
    for index in range(frames // ROWS):
        for stream in streams:
            stream.tile(index).start()
    tiles = offset_ref.shape[0]
    rows = frames // tiles
    halo, own = before_ref.shape[0], out_ref.shape[0]
    ends = read_ends(info_ref)
    base, slot_base = info_ref[8], info_ref[9]
    back_coefficients(
        own_ref, (one_ref, two_ref, three_ref), inverse_ref, coef_ref, back_ref, False
    )
    total_ref[...] = jnp.zeros_like(total_ref)
    span = rows + PAD

    def up_step(start):
        here = pl.ds(start, BLOCK)

        def upward(u):
            lead = cot_ref[here, :].astype(F32) * ROOT_HALF
            return lead + inward(
                inner_ref[here, :].astype(F32), unit_ref[here, :].astype(F32), back_ref, u
            )

        def uniform(u):
            up_ref[here, :] = upward(u).astype(BF16)

        def mixed(u, mask):
            old = up_ref[here, :].astype(F32)
            up_ref[here, :] = jnp.where(mask((BLOCK, channels)), upward(u), old).astype(BF16)

        by_utterance(ends, base + start, BLOCK, uniform, mixed)

    def step(i):
        start = pl.multiple_of(i * rows, rows)
        here = pl.ds(start, rows)
        shift = offset_ref[i] - slot_base
        aligned = pl.multiple_of((shift // PAD) * PAD, PAD)
        part = lax.dot_general(
            wide_ref[here, :], up_ref[here, :], (((0,), (0,)), ((), ())), preferred_element_type=F32
        )
        total_ref[pl.ds(aligned, span), :] += part[0:span]

    def blocks(i, start):
        for stream in streams:
            stream.tile(i).wait()
        for_blocks(start, ROWS, BLOCK, up_step)
        each = ROWS // rows

        def four(k, carry):
            for n in range(4):
                step(i * each + k * 4 + n)
            return carry

        lax.fori_loop(0, each // 4, four, 0)

    for_tiles(frames, blocks)
    before_ref[...] = total_ref[0:halo, :].astype(BF16)
    out_ref[...] = total_ref[halo : halo + own, :]
    after_ref[...] = total_ref[halo + own : 2 * halo + own, :].astype(BF16)


def scatter_kernel(places, copies, info_ref, order_ref, *refs):
    parts, out_ref, tmp_ref = refs[: len(places)], refs[-2], refs[-1]
    groups, piece, channels = parts[0].shape
    lanes = channels // 128
    me = info_ref[10]
    for old_ref in refs[len(places) : -2]:

        def copy(start, old_ref=old_ref):
            out_ref[pl.ds(start, ROWS), :] = old_ref[pl.ds(start, ROWS), :]

        for_blocks(0, out_ref.shape[0], ROWS, copy)
    for back, part_ref in zip(places, parts):
        source = lax.rem(me + copies - back, copies)

        def body(g, carry, part_ref=part_ref, source=source):
            for b in range(piece // 16):
                both = part_ref[g, b * 16 : b * 16 + 16, :].astype(F32)
                for h in range(2):
                    for q in range(lanes):
                        tmp_ref[pl.ds(((2 * b + h) * lanes + q) * 8, 8), :] = both[
                            8 * h : 8 * h + 8, q * 128 : (q + 1) * 128
                        ]
            first = (g * copies + source) * piece
            for r in range(piece):
                out_ref[pl.ds(order_ref[first + r], lanes, stride=8), :] = tmp_ref[
                    pl.ds((r // 8) * 8 * lanes + r % 8, lanes, stride=8), :
                ]
            return carry

        lax.fori_loop(0, groups, body, 0)


VM = pl.BlockSpec(memory_space=pltpu.VMEM)
SM = pl.BlockSpec(memory_space=pltpu.SMEM)


HB = pl.BlockSpec(memory_space=pltpu.HBM)


def call(kernel, inputs, outputs, scratch, flops, limit):
    return pl.pallas_call(
        kernel,
        in_specs=[spec for _, spec in inputs],
        out_specs=tuple(spec for _, _, spec in outputs),
        out_shape=tuple(
            pltpu.HBM(shape, dtype) if spec is HB else jax.ShapeDtypeStruct(shape, dtype)
            for shape, dtype, spec in outputs
        ),
        scratch_shapes=[
            pltpu.SemaphoreType.DMA((one,)) if isinstance(one, int) else pltpu.VMEM(*one)
            for one in scratch
        ],
        compiler_params=pltpu.CompilerParams(vmem_limit_bytes=limit * MIB),
        cost_estimate=pl.CostEstimate(flops=flops, bytes_accessed=flops // 200, transcendentals=0),
    )(
        *(
            pltpu.with_memory_space_constraint(array, pltpu.HBM) if spec is HB else array
            for array, spec in inputs
        )
    )


def scattered(old, parts, places, copies, info, order):
    piece, channels = parts[0].shape[1:]
    lanes = channels // 128
    kept = [] if old is None else [old]
    return pl.pallas_call(
        functools.partial(scatter_kernel, places, copies),
        in_specs=[SM, SM] + [VM] * (len(parts) + len(kept)),
        out_specs=VM,
        out_shape=(pltpu.VMEM if old is None else jax.ShapeDtypeStruct)(
            (order.shape[0] * lanes, 128), F32
        ),
        scratch_shapes=[pltpu.VMEM((piece * lanes, 128), F32)],
        input_output_aliases={2 + len(parts): 0} if kept else {},
        compiler_params=pltpu.CompilerParams(vmem_limit_bytes=22 * MIB),
        cost_estimate=pl.CostEstimate(flops=10**6, bytes_accessed=10**4, transcendentals=0),
    )(info, order, *parts, *kept)


def shifted(values, axis, step):
    devices = lax.axis_size(axis)
    return lax.ppermute(values, axis, [(i, (i + step) % devices) for i in range(devices)])


def others_over_tm(values):
    return [shifted(values, "tm", d) for d in (1, 2, 3)]


def from_neighbours(first_rows, last_rows):
    devices = lax.axis_size("tm")
    up = [(i, i + 1) for i in range(devices - 1)]
    down = [(i + 1, i) for i in range(devices - 1)]
    return lax.ppermute(last_rows, "tm", up), lax.ppermute(first_rows, "tm", down)


def swapped(values, bit):
    devices = lax.axis_size("seq")
    return lax.ppermute(values, "seq", [(i, i ^ (1 << bit)) for i in range(devices)])


def after(values, *others):
    return lax.optimization_barrier((values, others))[0]


def summed_over_tm(parts):
    copies, tm_index = lax.axis_size("tm"), lax.axis_index("tm")
    rows, channels = parts[0].shape
    pieces = jnp.stack(parts).reshape(len(parts), copies, rows // copies, channels)
    part = lax.dynamic_index_in_dim(pieces, tm_index, 1, False)
    sent = pieces.astype(BF16)
    for step in (1, 3, 2):
        give = lax.dynamic_index_in_dim(sent, (tm_index + step) % copies, 1, False)
        part = part + shifted(give, "tm", step).astype(F32)
    return part.astype(BF16)


def gathered_over_tm(part):
    copies, tm_index = lax.axis_size("tm"), lax.axis_index("tm")
    count, rows, channels = part.shape
    every = jnp.zeros((count, copies, rows, channels), BF16)
    every = lax.dynamic_update_index_in_dim(every, part, tm_index, 1)
    for step in (1, 3, 2):
        every = lax.dynamic_update_index_in_dim(
            every, shifted(part, "tm", step), (tm_index - step) % copies, 1
        )
    return every.reshape(count, copies * rows, channels)


def on_device(
    phonemes,
    send_order,
    phoneme_counts,
    frame_lengths,
    tile_offsets,
    alignment,
    style_vec,
    first_affine_weight,
    first_affine_bias,
    first_conv_weight,
    second_affine_weight,
    second_affine_bias,
    second_conv_weight,
    second_conv_bias,
    cotangent,
):
    frames, channels = cotangent.shape
    slot_count = phonemes.shape[0]
    groups = lax.axis_size("seq")
    copies = lax.axis_size("tm")
    seq_index, tm_index = lax.axis_index("seq"), lax.axis_index("tm")
    piece_rows = slot_count // groups // copies
    local_rows = slot_count // copies
    tiles = tile_offsets.shape[0]
    window = alignment.shape[1]
    halo = window // 2
    lengths = frame_lengths[0]
    conv_flops = 2 * frames * 3 * channels * channels

    info = jnp.concatenate(
        [
            jnp.cumsum(lengths),
            jnp.cumsum(phoneme_counts[0]),
            (tm_index * frames)[None],
            (tm_index * local_rows - halo)[None],
            tm_index[None],
            (seq_index < groups // 2)[None].astype(I32),
            (seq_index[None] >> jnp.arange(12, dtype=I32)) & 1,
        ]
    ).astype(I32)
    inverse = jnp.zeros((8, channels), F32).at[0:UTTS].set(
        jnp.broadcast_to(1.0 / lengths.astype(F32)[:, None], (UTTS, channels))
    )
    style_rows = jnp.zeros((8, style_vec.shape[1]), BF16).at[0:UTTS].set(style_vec)
    params_one = jnp.dot(style_rows, first_affine_weight, preferred_element_type=F32) + (
        first_affine_bias.astype(F32)
    )
    params_two = jnp.dot(style_rows, second_affine_weight, preferred_element_type=F32) + (
        second_affine_bias.astype(F32)
    )

    def turned(weight):
        return (
            weight.reshape(3, channels, channels).transpose(0, 2, 1).reshape(3 * channels, channels)
        )

    tiles_of = frames // ROWS
    full, padded = (frames, channels), (frames + 2 * PAD, channels)
    stats_shape, coef_shape = (STAT_ROWS, channels), (64, channels)
    small_acc = ((ACC_ROWS, channels), F32)

    order = send_order[0].reshape(groups, copies, piece_rows)
    extra = min(halo, piece_rows)
    from_first = seq_index < groups // 2
    mine = lax.dynamic_index_in_dim(order, tm_index, 1, False)
    following = lax.dynamic_index_in_dim(order, jnp.minimum(tm_index + 1, copies - 1), 1, False)
    leading = lax.dynamic_index_in_dim(order, jnp.maximum(tm_index - 1, 0), 1, False)
    beside = jnp.where(from_first, following[:, :extra], leading[:, piece_rows - extra :])
    mine = jnp.concatenate([mine, beside], axis=1)
    outgoing = jnp.take(phonemes, mine.reshape(-1), axis=0, mode="clip")
    received = lax.all_to_all(
        outgoing.reshape(groups, piece_rows + extra, channels), "seq", 0, 0, tiled=True
    )

    second_turned = turned(second_conv_weight)
    grad_act_two, grad_branch, bias_part = call(
        gradient_kernel,
        (
            (info, SM),
            (cotangent, HB),
            (second_turned, VM),
        ),
        ((full, BF16, HB), (full, BF16, HB), ((16, channels), F32, VM)),
        [(full, BF16), (padded, BF16), (full, BF16), tiles_of, tiles_of, tiles_of],
        conv_flops,
        32,
    )

    received, bias_part = lax.optimization_barrier((received, bias_part))
    upsampled, upsampled_far, wide, stat = call(
        upsample_kernel,
        (
            (info, SM),
            (tile_offsets, SM),
            (received, VM),
            (alignment, HB),
            (bias_part, VM),
        ),
        (
            (full, F32, VM),
            (full, F32, HB),
            ((frames, WIDE), BF16, HB),
            (stats_shape, F32, VM),
        ),
        [
            ((local_rows + WIDE, channels), BF16),
            small_acc,
            ((frames, window), BF16),
            ((frames, WIDE), BF16),
            tiles_of,
            tiles_of,
            tiles_of,
        ],
        2 * frames * WIDE * channels,
        20,
    )
    others = others_over_tm(stat)
    bias_total = (stat[EXTRA_ROW] + others[1][EXTRA_ROW]) + (
        others[0][EXTRA_ROW] + others[2][EXTRA_ROW]
    )

    act_one, middle, middle_far, unit_one, coef_one, stat_two, grad_edges, added = call(
        first_conv_kernel,
        (
            (info, SM),
            (upsampled, VM),
            *((one, VM) for one in (stat, *others)),
            (inverse, VM),
            (params_one, VM),
            (first_conv_weight, VM),
            (second_turned, VM),
        ),
        (
            (padded, BF16, HB),
            (full, F32, VM),
            (full, F32, HB),
            (full, BF16, HB),
            (coef_shape, F32, VM),
            (stats_shape, F32, VM),
            ((8, channels), F32, VM),
            ((8, channels), F32, VM),
        ),
        [small_acc, (padded, BF16), (full, BF16), tiles_of, 2, tiles_of, tiles_of],
        conv_flops,
        28,
    )
    others_two = others_over_tm(stat_two)

    act_two, inner_two, coef_two, stat_three = call(
        second_norm_kernel,
        (
            (info, SM),
            (grad_act_two, HB),
            (middle, VM),
            *((one, VM) for one in (stat_two, *others_two)),
            (inverse, VM),
            (params_two, VM),
            (added, VM),
        ),
        (
            (padded, BF16, HB),
            (full, BF16, HB),
            (coef_shape, F32, VM),
            (stats_shape, F32, VM),
        ),
        [
            small_acc,
            (full, BF16),
            (padded, BF16),
            (full, BF16),
            tiles_of,
            tiles_of,
            2,
            tiles_of,
        ],
        2 * frames * channels * 100,
        28,
    )
    others_three = others_over_tm(stat_three)
    grad_middle, middle_edges, inner_one, back_two, stat_four = call(
        first_back_kernel,
        (
            (info, SM),
            (inner_two, HB),
            (middle_far, HB),
            *((one, VM) for one in (stat_three, *others_three)),
            (inverse, VM),
            (coef_two, VM),
            (coef_one, VM),
            (unit_one, HB),
            (first_conv_weight, VM),
        ),
        (
            (full, BF16, HB),
            ((8, channels), F32, VM),
            (full, BF16, HB),
            ((40, channels), F32, VM),
            (stats_shape, F32, VM),
        ),
        [
            small_acc,
            ((ROWS, channels), F32),
            (full, BF16),
            (full, F32),
            (full, BF16),
            (full, BF16),
            (padded, BF16),
            *([tiles_of] * 5),
        ],
        conv_flops,
        40,
    )
    others_four = others_over_tm(stat_four)
    grad_before, grad_own, grad_after, back_one = call(
        buffer_gradient_kernel,
        (
            (info, SM),
            (tile_offsets, SM),
            (inner_one, HB),
            (unit_one, HB),
            (cotangent, HB),
            (wide, HB),
            *((one, VM) for one in (stat_four, *others_four)),
            (inverse, VM),
            (coef_one, VM),
        ),
        (
            ((halo, channels), BF16, VM),
            ((local_rows, channels), F32, VM),
            ((halo, channels), BF16, VM),
            ((40, channels), F32, VM),
        ),
        [
            (full, BF16),
            ((local_rows + WIDE, channels), F32),
            *([(full, BF16)] * 3),
            ((frames, WIDE), BF16),
            *([tiles_of] * 4),
        ],
        2 * frames * WIDE * channels,
        36,
    )

    row_places = (send_order[0] >> 3) * (8 * (channels // 128)) + (send_order[0] & 7)
    from_before, from_after = from_neighbours(grad_before, grad_after)
    return_rows = jnp.concatenate(
        [grad_own[:halo] + from_before, grad_own[halo:-halo], grad_own[-halo:] + from_after]
    ).astype(BF16)
    returned = lax.all_to_all(
        return_rows.reshape(groups, piece_rows, channels), "seq", 0, 0, tiled=True
    )

    bits = [b for b in range(12) if (1 << b) < groups]
    orders = (bits[1:], bits[1:][::-1])
    second_keep, second_give = call(
        weight_gradient_kernel,
        ((info, SM), (after(act_two, back_one), HB), (grad_branch, HB), (grad_edges, VM)),
        (((3 * channels // 2, channels), F32, VM), ((3 * channels // 2, channels), BF16, VM)),
        [((3 * channels, channels), F32), (padded, BF16), (padded, BF16), tiles_of, tiles_of],
        10**6,
        24,
    )

    returned, second_keep, second_give = lax.optimization_barrier(
        (returned, second_keep, second_give)
    )
    rounds = [returned, shifted(returned, "tm", 1)]
    first_keep, first_give = call(
        weight_gradient_kernel,
        ((info, SM), (act_one, HB), (after(grad_middle, returned), HB), (middle_edges, VM)),
        (((3 * channels // 2, channels), F32, VM), ((3 * channels // 2, channels), BF16, VM)),
        [((3 * channels, channels), F32), (padded, BF16), (padded, BF16), tiles_of, tiles_of],
        10**6,
        24,
    )

    keeps, gives = [second_keep, first_keep], [second_give, first_give]
    gots = [swapped(give, bits[0]) for give in gives]
    for turn, pair in enumerate(zip(*orders)):
        count = keeps[0].shape[0] // 2
        out = call(
            functools.partial(halves_kernel, pair),
            ((info, SM), *((one, VM) for both in zip(keeps, gots) for one in both)),
            (((count, channels), F32, VM), ((count, channels), BF16, VM)) * 2,
            [((2 * count, channels), F32)] * 2,
            10**6,
            16,
        )
        keeps, gives = [out[0], out[2]], [out[1], out[3]]
        if turn == 0:
            rounds[1], keeps, gives = lax.optimization_barrier((rounds[1], keeps, gives))
            rounds.append(shifted(rounds[1], "tm", 1))
        gots = [swapped(give, bit) for give, bit in zip(gives, pair)]
    row_sums = [keep + got.astype(F32) for keep, got in zip(keeps, gots)]
    placed = scattered(None, rounds[:2], (0, 1), copies, info, row_places)
    rounds[2], row_sums, placed = lax.optimization_barrier((rounds[2], row_sums, placed))
    sums = gathered_over_tm(summed_over_tm(row_sums))
    rounds[2], sums = lax.optimization_barrier((rounds[2], sums))
    rounds.append(shifted(rounds[2], "tm", 1))

    act_two, _ = lax.optimization_barrier((act_two, sums))
    (frames_out,) = call(
        second_conv_kernel,
        (
            (info, SM),
            (act_two, HB),
            (upsampled_far, HB),
            (second_conv_weight, VM),
            (second_conv_bias[None], VM),
        ),
        ((full, BF16, HB),),
        [(padded, BF16), (full, F32), (full, BF16), tiles_of, 2, tiles_of, tiles_of],
        10**6,
        36,
    )


    params_grad = [
        jnp.concatenate([back[8 : 8 + UTTS], back[0:UTTS]], axis=1) for back in (back_one, back_two)
    ]
    style_grad = jnp.dot(
        params_grad[0], first_affine_weight.astype(F32).T, precision=PRECISE
    ) + jnp.dot(params_grad[1], second_affine_weight.astype(F32).T, precision=PRECISE)
    style_block = jnp.zeros((8, channels), BF16).at[:, : style_rows.shape[1]].set(style_rows)
    small = jnp.concatenate(
        [
            back_one[8:16].astype(BF16),
            back_one[0:8].astype(BF16),
            back_two[8:16].astype(BF16),
            back_two[0:8].astype(BF16),
            style_block,
            jnp.zeros((8, channels), BF16).at[0].set(bias_total.astype(BF16)),
        ]
    )
    rows = sums.shape[1]
    held = [jnp.concatenate([sums[0], small]), sums[1]]
    for pair in zip(*orders):
        others = [swapped(one, bit) for one, bit in zip(held, pair)]
        held = call(
            functools.partial(join_kernel, pair),
            ((info, SM), *((one, VM) for both in zip(held, others) for one in both)),
            tuple(((2 * one.shape[0], channels), BF16, VM) for one in held),
            [],
            10**6,
            16,
        )
    rounds[3], held, frames_out = lax.optimization_barrier((rounds[3], list(held), frames_out))
    others = [swapped(one, bits[0]) for one in held]
    (
        second_conv_grad,
        first_conv_grad,
        first_affine_grad,
        first_shift_grad,
        second_affine_grad,
        second_shift_grad,
        second_bias_grad,
    ) = call(
        functools.partial(final_kernel, orders, rows),
        (
            (info, SM),
            (held[0], VM),
            (others[0], VM),
            (held[1], VM),
            (others[1], VM),
        ),
        (
            ((3 * channels, channels), F32, VM),
            ((3 * channels, channels), F32, VM),
            *(
                (((style_vec.shape[1], 2 * channels), F32, VM), ((1, 2 * channels), F32, VM)) * 2
            ),
            ((1, channels), F32, VM),
        ),
        [],
        10**6,
        28,
    )
    placed = scattered(placed, rounds[2:], (2, 3), copies, info, row_places)
    lanes = channels // 128
    phonemes_grad = (
        placed.reshape(slot_count // 8, lanes, 8, 128)
        .transpose(0, 2, 1, 3)
        .reshape(slot_count, channels)
    )
    return (
        frames_out,
        phonemes_grad,
        style_grad,
        first_affine_grad,
        first_shift_grad[0],
        first_conv_grad,
        second_affine_grad,
        second_shift_grad[0],
        second_conv_grad,
        second_bias_grad[0],
    )


def solution(mesh):
    split, whole = ("seq", "tm"), P()
    in_specs = (
        P("seq", None),
        P("seq", None),
        P("seq", None),
        P("seq", None),
        P(split),
        P(split, None),
        P("seq", None),
        *([whole] * 7),
        P(split, None),
    )
    out_specs = (P(split, None), P("seq", None), P("seq", None), *([whole] * 7))
    return jax.shard_map(
        on_device, mesh=mesh, in_specs=in_specs, out_specs=out_specs, check_vma=False
    )
```

```python
import functools

import jax
import jax.numpy as jnp
from jax import lax
from jax.experimental import pallas as pl
from jax.experimental.pallas import tpu as pltpu
from jax.sharding import PartitionSpec as P

EPSILON = 1e-05
ROOT_HALF = 0.7071067811865476
PRECISE = lax.Precision.HIGHEST
F32, BF16, I32 = jnp.float32, jnp.bfloat16, jnp.int32
UTTS = 4
PAD = 16
ROWS = 1024
BLOCK = 128
WIDE = 256
MIB = 2**20

STAT_ROWS = 24
FIRST_ROW, LAST_ROW, EXTRA_ROW, FIRST_GRAD, LAST_GRAD = 16, 17, 18, 19, 20
SMALL_ROWS = 48
BITS_AT = 12


def owner_at(ends, position):
    return sum((position >= end).astype(I32) for end in ends)


def tile_of(ref, index, offset=0):
    return ref.at[pl.ds(pl.multiple_of(offset + index * ROWS, PAD), ROWS), :]


class Stream:
    def __init__(self, source, target, sems, source_offset=0, target_offset=0):
        self.ends = (source, source_offset, target, target_offset)
        self.sems = sems
        self.tiles = sems.shape[0]

    def tile(self, index):
        source, source_offset, target, target_offset = self.ends
        return pltpu.make_async_copy(
            tile_of(source, index, source_offset),
            tile_of(target, index, target_offset),
            self.sems.at[index],
        )

    def start(self):
        for index in range(self.tiles):
            self.tile(index).start()

    def finish(self):
        for index in range(self.tiles):
            self.tile(index).wait()


def edge_copies(source, target, sems):
    last = source.shape[0] - PAD
    return [
        pltpu.make_async_copy(
            source.at[pl.ds(at, PAD), :], target.at[pl.ds(at, PAD), :], sems.at[k]
        )
        for k, at in enumerate((0, last))
    ]


def rows_of(start, shape):
    return start + lax.broadcasted_iota(I32, shape, 0)


def fold_rows(values):
    return jnp.sum(values.reshape(values.shape[0] // 8, 8, values.shape[1]), axis=0)


def by_utterance(ends, start, count, uniform_body, mixed_body):
    low, high = owner_at(ends, start), owner_at(ends, start + count - 1)

    @pl.when(low == high)
    def _():
        uniform_body(low)

    @pl.when(low != high)
    def _():
        def step(u, carry):
            lower = jnp.int32(-1)
            upper = jnp.int32(2**30)
            for k in range(UTTS):
                lower = jnp.where(u == k + 1, ends[k], lower)
                upper = jnp.where(u == k, ends[k], upper)

            def mask(shape):
                rows = rows_of(start, shape)
                return (rows >= lower) & (rows < upper)

            mixed_body(u, mask)
            return carry

        lax.fori_loop(low, high + 1, step, 0)


class Blocks:
    def __init__(self, ends, base, channels):
        self.ends, self.base, self.channels = ends, base, channels

    def plain(self, start, body):
        for inside in range(0, ROWS, BLOCK):
            first = self.base + start + inside
            low = owner_at(self.ends, first)
            alone = (low == owner_at(self.ends, first + BLOCK - 1)).astype(F32)
            body(start + inside, low, alone)

    def mixed(self, start, body):
        def step(i, carry):
            at = pl.multiple_of(start + i * BLOCK, BLOCK)
            by_utterance(
                self.ends,
                self.base + at,
                BLOCK,
                lambda u: None,
                lambda u, mask: body(at, u, mask((BLOCK, self.channels))),
            )
            return carry

        low = owner_at(self.ends, self.base + start)

        @pl.when(low != owner_at(self.ends, self.base + start + ROWS - 1))
        def _():
            lax.fori_loop(0, ROWS // BLOCK, step, 0)


def row(ref, index):
    return ref[pl.ds(index, 1), :]


def logistic(values):
    return 0.5 * jnp.tanh(0.5 * values) + 0.5


def taps_of(padded_ref, ends, start, base):
    channels = padded_ref.shape[1]
    block = padded_ref[pl.ds(start, ROWS + 2 * PAD), :].astype(F32)
    positions = rows_of(base + start, (ROWS, channels))
    cut_left = positions == ends[0]
    cut_right = positions + 1 == ends[0]
    for end in ends[1:]:
        cut_left = cut_left | (positions == end)
        cut_right = cut_right | (positions + 1 == end)
    before = jnp.where(cut_left, 0.0, block[PAD - 1 : PAD - 1 + ROWS]).astype(BF16)
    after = jnp.where(cut_right, 0.0, block[PAD + 1 : PAD + 1 + ROWS]).astype(BF16)
    return before, padded_ref[pl.ds(start + PAD, ROWS), :], after


def convolved(taps, weight_ref):
    channels = weight_ref.shape[1]
    return sum(
        jnp.dot(tap, weight_ref[k * channels : (k + 1) * channels, :], preferred_element_type=F32)
        for k, tap in enumerate(taps)
    )


def convolved_back(taps, weight_ref):
    channels = weight_ref.shape[1]
    return sum(
        lax.dot_general(
            tap,
            weight_ref[k * channels : (k + 1) * channels, :],
            (((1,), (1,)), ((), ())),
            preferred_element_type=F32,
        )
        for k, tap in enumerate(taps)
    )


def for_blocks(first, count, size, body, unroll=1):
    def step(i, carry):
        body(pl.multiple_of(first + i * size, size))
        return carry

    lax.fori_loop(0, count // size, step, 0, unroll=unroll)


def for_tiles(count, body):
    def step(i, carry):
        body(i, pl.multiple_of(i * ROWS, ROWS))
        return carry

    lax.fori_loop(0, count // ROWS, step, 0)


def wait_next(streams, i, count):
    @pl.when(i + 1 < count // ROWS)
    def _():
        for stream in streams:
            stream.tile(i + 1).wait()


def sum_over_tm(own_ref, other_refs, first, count):
    one, two, three = other_refs
    part = pl.ds(first, count)
    return (own_ref[part, :] + two[part, :]) + (one[part, :] + three[part, :])


def finish_stats(acc_ref, stat_ref):
    for kind in range(2):
        for u in range(8):
            at = kind * 8 + u
            if u < UTTS:
                first = (kind * (UTTS + 1) + u) * 8
                stat_ref[at : at + 1, :] = jnp.sum(
                    acc_ref[first : first + 8, :], axis=0, keepdims=True
                )
            else:
                stat_ref[at : at + 1, :] = jnp.zeros_like(stat_ref[at : at + 1, :])
    stat_ref[16:24, :] = jnp.zeros_like(stat_ref[16:24, :])


ACC_ROWS = 2 * (UTTS + 1) * 8


def add_stats(acc_ref, u, first, second, weight=None):
    for kind, term in enumerate((first, second)):
        at = pl.ds(pl.multiple_of((kind * (UTTS + 1) + u) * 8, 8), 8)
        term = fold_rows(term)
        acc_ref[at, :] += term if weight is None else term * weight


def read_ends(info_ref):
    return [info_ref[k] for k in range(UTTS)]


def halo_owner(info_ref, ends, base, frames):
    before = jnp.where(base == 0, UTTS, owner_at(ends, base - 1))
    return before, owner_at(ends, base + frames)


def gradient_kernel(
    info_ref,
    cot_hbm,
    weight_ref,
    out_hbm,
    padded_hbm,
    bias_ref,
    cot_ref,
    padded_ref,
    out_ref,
    cot_sems,
    padded_sems,
    out_sems,
):
    frames, channels = cot_ref.shape
    ends = read_ends(info_ref)
    base = info_ref[8]
    cot_in = Stream(cot_hbm, cot_ref, cot_sems)
    padded_out = Stream(padded_ref, padded_hbm, padded_sems, PAD)
    outward = Stream(out_ref, out_hbm, out_sems)
    cot_in.start()
    padded_ref[0:PAD, :] = jnp.zeros((PAD, channels), BF16)
    padded_ref[PAD + frames :, :] = jnp.zeros((PAD, channels), BF16)
    bias_ref[...] = jnp.zeros_like(bias_ref)

    def scale(start):
        here = cot_ref[pl.ds(start, BLOCK), :].astype(F32) * ROOT_HALF
        here = jnp.where(rows_of(base + start, (BLOCK, channels)) < ends[UTTS - 1], here, 0.0)
        rounded = here.astype(BF16)
        padded_ref[pl.ds(start + PAD, BLOCK), :] = rounded
        bias_ref[0:8, :] += fold_rows(rounded.astype(F32))

    def scale_tile(i, start):
        cot_in.tile(i).wait()
        for_blocks(start, ROWS, BLOCK, scale)
        padded_out.tile(i).start()

    for_tiles(frames, scale_tile)

    def conv(i, start):
        before, here, after = taps_of(padded_ref, ends, start, base)
        total = convolved((after, here, before), weight_ref)
        out_ref[pl.ds(start, ROWS), :] = total.astype(BF16)
        outward.tile(i).start()

    for_tiles(frames, conv)
    bias_ref[8:9, :] = padded_ref[PAD : 2 * PAD, :].astype(F32)[0:1]
    bias_ref[9:10, :] = padded_ref[frames : frames + PAD, :].astype(F32)[PAD - 1 :]
    padded_out.finish()
    outward.finish()


def upsample_kernel(
    info_ref,
    offset_ref,
    rows_ref,
    align_hbm,
    bias_ref,
    out_ref,
    out_hbm,
    wide_hbm,
    stat_ref,
    buffer_ref,
    acc_ref,
    align_ref,
    wide_ref,
    align_sems,
    out_sems,
    wide_sems,
):
    frames, channels = out_ref.shape
    align_in = Stream(align_hbm, align_ref, align_sems)
    outward = Stream(out_ref, out_hbm, out_sems)
    wide_out = Stream(wide_ref, wide_hbm, wide_sems)
    align_in.start()
    window = align_ref.shape[1]
    tiles = offset_ref.shape[0]
    rows = frames // tiles
    groups, both = rows_ref.shape[:2]
    halo = window // 2
    piece = next(n for n in range(both // 2, both) if both - n == min(halo, n))
    own, extra = groups * piece, both - piece
    ends = read_ends(info_ref)
    slot_ends = [info_ref[UTTS + k] for k in range(UTTS)]
    base, slot_base = info_ref[8], info_ref[9]
    for s in range(groups):
        buffer_ref[halo + s * piece : halo + (s + 1) * piece, :] = rows_ref[s, 0:piece, :]
    for n in range(halo // extra):
        buffer_ref[n * extra : (n + 1) * extra, :] = rows_ref[
            groups - halo // extra + n, piece:both, :
        ]
        at = halo + own + n * extra
        buffer_ref[at : at + extra, :] = rows_ref[n, piece:both, :]
    buffer_ref[2 * halo + own :, :] = jnp.zeros_like(buffer_ref[2 * halo + own :, :])
    acc_ref[...] = jnp.zeros_like(acc_ref)

    def step(i):
        start = pl.multiple_of(i * rows, rows)
        shift = offset_ref[i] - slot_base
        aligned = pl.multiple_of((shift // PAD) * PAD, PAD)
        block = align_ref[pl.ds(start, rows), :].astype(F32)
        block = jnp.concatenate([block, jnp.zeros((rows, WIDE - window), F32)], axis=1)
        block = pltpu.roll(block, shift - aligned, 1)
        slots = slot_base + aligned + lax.broadcasted_iota(I32, (rows, WIDE), 1)
        slot_owner = owner_at(slot_ends, slots)
        frame_owner = owner_at(ends, rows_of(base + start, (rows, WIDE)))
        match = (slot_owner == frame_owner) & (frame_owner < UTTS)
        block = jnp.where(match, block, 0.0).astype(BF16)
        wide_ref[pl.ds(start, rows), :] = block
        out_ref[pl.ds(start, rows), :] = jnp.dot(
            block, buffer_ref[pl.ds(aligned, WIDE), :], preferred_element_type=F32
        )

    def blocks(i, start):
        align_in.tile(i).wait()
        each = ROWS // rows

        def four(k, carry):
            for n in range(4):
                step(i * each + k * 4 + n)
            return carry

        lax.fori_loop(0, each // 4, four, 0)
        outward.tile(i).start()
        wide_out.tile(i).start()
        for_blocks(
            start, ROWS, BLOCK, lambda at: value_sums(out_ref, acc_ref, ends, base, at)
        )

    for_tiles(frames, blocks)
    finish_stats(acc_ref, stat_ref)
    stat_ref[FIRST_ROW : FIRST_ROW + 1, :] = out_ref[0:1, :]
    stat_ref[LAST_ROW : LAST_ROW + 1, :] = out_ref[frames - 1 : frames, :]
    stat_ref[EXTRA_ROW : EXTRA_ROW + 1, :] = jnp.sum(bias_ref[0:8, :], axis=0, keepdims=True)
    stat_ref[FIRST_GRAD : FIRST_GRAD + 2, :] = bias_ref[8:10, :]
    outward.finish()
    wide_out.finish()


def value_sums(out_ref, acc_ref, ends, base, start):
    channels = out_ref.shape[1]

    def uniform(u):
        here = out_ref[pl.ds(start, BLOCK), :]
        add_stats(acc_ref, u, here, here * here)

    def mixed(u, mask):
        here = jnp.where(mask((BLOCK, channels)), out_ref[pl.ds(start, BLOCK), :], 0.0)
        add_stats(acc_ref, u, here, here * here)

    by_utterance(ends, base + start, BLOCK, uniform, mixed)


def write_coefficients(own_ref, other_refs, inverse_ref, params_ref, coef_ref):
    channels = inverse_ref.shape[1]
    inverse = inverse_ref[...]
    total = sum_over_tm(own_ref, other_refs, 0, 8)
    square = sum_over_tm(own_ref, other_refs, 8, 8)
    mean = total * inverse
    real = inverse > 0.0
    rstd = jnp.where(real, lax.rsqrt(square * inverse - mean * mean + EPSILON), 0.0)
    gain = jnp.where(real, 1.0 + params_ref[:, 0:channels], 0.0)
    shift = jnp.where(real, params_ref[:, channels : 2 * channels], 0.0)
    coef_ref[0:8, :] = rstd
    coef_ref[8:16, :] = mean * rstd
    coef_ref[16:24, :] = gain * rstd
    coef_ref[24:32, :] = 0.5 * gain
    coef_ref[32:40, :] = 0.5 * shift
    coef_ref[40:48, :] = 0.5 * gain * rstd
    coef_ref[48:56, :] = 0.5 * (shift - mean * gain * rstd)
    coef_ref[56:57, :] = row(other_refs[0], LAST_ROW)
    coef_ref[57:58, :] = row(other_refs[2], FIRST_ROW)


UNIT, HALF_OF_UNIT, HALF_OF_VALUE = (0, 8), (24, 32), (40, 48)


def unit_of(values, coef_ref, u):
    return values * row(coef_ref, u) - row(coef_ref, 8 + u)


def half_normed(values, coef_ref, u, rows):
    return values * row(coef_ref, rows[0] + u) + row(coef_ref, rows[1] + u)


def twice_logistic(half):
    return jnp.tanh(half) + 1.0


def activation(values, coef_ref, u):
    half = half_normed(values, coef_ref, u, HALF_OF_VALUE)
    return half * twice_logistic(half)


def edge_rows(padded_ref, before, after):
    channels = padded_ref.shape[1]
    padded_ref[0:PAD, :] = jnp.broadcast_to(before, (PAD, channels)).astype(BF16)
    last = padded_ref.shape[0] - PAD
    padded_ref[last:, :] = jnp.broadcast_to(after, (PAD, channels)).astype(BF16)


def first_conv_kernel(
    info_ref,
    values_ref,
    own_ref,
    one_ref,
    two_ref,
    three_ref,
    inverse_ref,
    params_ref,
    weight_ref,
    turned_ref,
    act_hbm,
    out_ref,
    out_hbm,
    unit_hbm,
    coef_ref,
    stat_ref,
    edge_ref,
    added_ref,
    acc_ref,
    act_ref,
    unit_ref,
    act_sems,
    edge_sems,
    out_sems,
    unit_sems,
):
    frames, channels = values_ref.shape
    tiles = frames // ROWS
    act_out = Stream(act_ref, act_hbm, act_sems, PAD, PAD)
    unit_out = Stream(unit_ref, unit_hbm, unit_sems)
    outward = Stream(out_ref, out_hbm, out_sems)
    ends = read_ends(info_ref)
    base = info_ref[8]
    blocks = Blocks(ends, base, channels)
    write_coefficients(own_ref, (one_ref, two_ref, three_ref), inverse_ref, params_ref, coef_ref)
    acc_ref[...] = jnp.zeros_like(acc_ref)
    owner_before, owner_after = halo_owner(info_ref, ends, base, frames)
    edge_rows(
        act_ref,
        activation(row(one_ref, LAST_ROW), coef_ref, owner_before),
        activation(row(three_ref, FIRST_ROW), coef_ref, owner_after),
    )
    edges = edge_copies(act_ref, act_hbm, edge_sems)
    for edge in edges:
        edge.start()

    def act_parts(at, u):
        unit = unit_of(values_ref[pl.ds(at, BLOCK), :], coef_ref, u)
        half = half_normed(unit, coef_ref, u, HALF_OF_UNIT)
        return unit, half * twice_logistic(half)

    def act_plain(at, u, alone):
        unit, act = act_parts(at, u)
        unit_ref[pl.ds(at, BLOCK), :] = unit.astype(BF16)
        act_ref[pl.ds(at + PAD, BLOCK), :] = act.astype(BF16)

    def act_mixed(at, u, keep):
        here, there = pl.ds(at, BLOCK), pl.ds(at + PAD, BLOCK)
        unit, act = act_parts(at, u)
        unit_ref[here, :] = jnp.where(keep, unit, unit_ref[here, :].astype(F32)).astype(BF16)
        act_ref[there, :] = jnp.where(keep, act, act_ref[there, :].astype(F32)).astype(BF16)

    def sums_plain(at, u, alone):
        here = out_ref[pl.ds(at, BLOCK), :]
        add_stats(acc_ref, u, here, here * here, alone)

    def sums_mixed(at, u, keep):
        here = jnp.where(keep, out_ref[pl.ds(at, BLOCK), :], 0.0)
        add_stats(acc_ref, u, here, here * here)

    for turn in range(-1, tiles + 1):
        if turn + 1 < tiles:
            blocks.plain((turn + 1) * ROWS, act_plain)
        if 0 <= turn < tiles:
            start = turn * ROWS
            out_ref[start : start + ROWS, :] = convolved(
                taps_of(act_ref, ends, start, base), weight_ref
            )
        if turn > 0:
            blocks.plain((turn - 1) * ROWS, sums_plain)
        if turn + 1 < tiles:
            blocks.mixed((turn + 1) * ROWS, act_mixed)
            act_out.tile(turn + 1).start()
            unit_out.tile(turn + 1).start()
        if 0 <= turn < tiles:
            outward.tile(turn).start()
        if turn > 0:
            blocks.mixed((turn - 1) * ROWS, sums_mixed)
    edge_ref[...] = jnp.zeros_like(edge_ref)
    added_ref[...] = jnp.zeros_like(added_ref)
    neighbours = (
        (one_ref, LAST_GRAD, owner_before, owner_at(ends, base), 2 * channels),
        (three_ref, FIRST_GRAD, owner_after, owner_at(ends, base + frames - 1), 0),
    )
    for k, (ref, at, theirs, ours, tap) in enumerate(neighbours):
        valid = (theirs == ours) & (ours < UTTS)
        edge_ref[k : k + 1, :] = jnp.where(valid, ref[at : at + 1, :], 0.0)
        rows = jnp.broadcast_to(edge_ref[k : k + 1, :], (PAD, channels)).astype(BF16)
        added_ref[k : k + 1, :] = jnp.dot(
            rows, turned_ref[tap : tap + channels, :], preferred_element_type=F32
        )[0:1]
    finish_stats(acc_ref, stat_ref)
    stat_ref[FIRST_ROW : FIRST_ROW + 1, :] = out_ref[0:1, :]
    stat_ref[LAST_ROW : LAST_ROW + 1, :] = out_ref[frames - 1 : frames, :]
    act_out.finish()
    unit_out.finish()
    outward.finish()
    for edge in edges:
        edge.wait()


def slope_and_sums(gradient, values, coef_ref, u, rows):
    half = half_normed(values, coef_ref, u, rows)
    gate = twice_logistic(half)
    act = half * gate
    inner = gradient * (gate * (half - 0.5 * act + 0.5))
    return act, inner, inner * values


def second_norm_kernel(
    info_ref,
    gradient_hbm,
    values_ref,
    own_ref,
    one_ref,
    two_ref,
    three_ref,
    inverse_ref,
    params_ref,
    added_ref,
    act_hbm,
    inner_ref,
    coef_ref,
    stat_ref,
    acc_ref,
    gradient_ref,
    act_ref,
    gradient_sems,
    act_sems,
    edge_sems,
):
    frames, channels = values_ref.shape
    gradient_in = Stream(gradient_hbm, gradient_ref, gradient_sems)
    outward = [
        Stream(act_ref, act_hbm, act_sems, PAD, PAD),
    ]
    gradient_in.start()
    ends = read_ends(info_ref)
    base = info_ref[8]
    write_coefficients(own_ref, (one_ref, two_ref, three_ref), inverse_ref, params_ref, coef_ref)
    acc_ref[...] = jnp.zeros_like(acc_ref)
    owner_before, owner_after = halo_owner(info_ref, ends, base, frames)
    edge_rows(
        act_ref,
        activation(row(one_ref, LAST_ROW), coef_ref, owner_before),
        activation(row(three_ref, FIRST_ROW), coef_ref, owner_after),
    )

    edges = edge_copies(act_ref, act_hbm, edge_sems)
    for edge in edges:
        edge.start()

    def step(start):
        here = pl.ds(start, BLOCK)
        there = pl.ds(start + PAD, BLOCK)

        def parts(u):
            return slope_and_sums(
                gradient_ref[here, :].astype(F32), values_ref[here, :], coef_ref, u, HALF_OF_VALUE
            )

        def uniform(u):
            act, inner, cross = parts(u)
            act_ref[there, :] = act.astype(BF16)
            inner_ref[here, :] = inner.astype(BF16)
            add_stats(acc_ref, u, inner, cross)

        def mixed(u, mask):
            keep = mask((BLOCK, channels))
            act, inner, cross = parts(u)
            act_ref[there, :] = jnp.where(keep, act, act_ref[there, :].astype(F32)).astype(BF16)
            old = inner_ref[here, :].astype(F32)
            inner_ref[here, :] = jnp.where(keep, inner, old).astype(BF16)
            add_stats(acc_ref, u, jnp.where(keep, inner, 0.0), jnp.where(keep, cross, 0.0))

        by_utterance(ends, base + start, BLOCK, uniform, mixed)

    def tile(i, start):
        gradient_in.tile(i).wait()
        for k, at in enumerate((0, frames - PAD)):

            @pl.when(i == at // ROWS)
            def _(k=k, at=at):
                edge = gradient_ref[at : at + PAD, :].astype(F32)
                inside = rows_of(0, (PAD, channels)) == k * (PAD - 1)
                edge = edge + jnp.where(inside, added_ref[k : k + 1, :], 0.0)
                gradient_ref[at : at + PAD, :] = edge.astype(BF16)

        for_blocks(start, ROWS, BLOCK, step)
        for stream in outward:
            stream.tile(i).start()

    for_tiles(frames, tile)
    finish_stats(acc_ref, stat_ref)
    stat_ref[FIRST_ROW : FIRST_ROW + 1, :] = inner_ref[0:PAD, :].astype(F32)[0:1]
    stat_ref[LAST_ROW : LAST_ROW + 1, :] = inner_ref[frames - PAD :, :].astype(F32)[PAD - 1 :]
    for stream in outward:
        stream.finish()
    for edge in edges:
        edge.wait()


def second_conv_kernel(
    info_ref,
    act_hbm,
    values_hbm,
    weight_ref,
    bias_ref,
    out_hbm,
    act_ref,
    values_ref,
    out_ref,
    act_sems,
    edge_sems,
    values_sems,
    out_sems,
):
    frames, channels = values_ref.shape
    ends = read_ends(info_ref)
    base = info_ref[8]
    bias = bias_ref[...].astype(F32)
    act_in = Stream(act_hbm, act_ref, act_sems, PAD, PAD)
    values_in = Stream(values_hbm, values_ref, values_sems)
    outward = Stream(out_ref, out_hbm, out_sems)
    edges = edge_copies(act_hbm, act_ref, edge_sems)
    for edge in edges:
        edge.start()
    act_in.start()
    values_in.start()
    for edge in edges:
        edge.wait()
    act_in.tile(0).wait()

    def step(i, start):
        here = pl.ds(start, ROWS)
        wait_next([act_in], i, frames)
        values_in.tile(i).wait()
        branch = convolved(taps_of(act_ref, ends, start, base), weight_ref) + bias
        valid = rows_of(base + start, (ROWS, channels)) < ends[UTTS - 1]
        total = jnp.where(valid, (values_ref[here, :] + branch) * ROOT_HALF, 0.0)
        out_ref[here, :] = total.astype(BF16)
        outward.tile(i).start()

    for_tiles(frames, step)
    outward.finish()


def weight_gradient_kernel(
    info_ref,
    act_hbm,
    gradient_hbm,
    edge_ref,
    keep_ref,
    give_ref,
    out_ref,
    act_ref,
    gradient_ref,
    act_sems,
    gradient_sems,
):
    frames = act_ref.shape[0] - 2 * PAD
    channels = act_ref.shape[1]
    ends = read_ends(info_ref)
    base = info_ref[8]
    act_in = Stream(act_hbm, act_ref, act_sems, PAD, PAD)
    gradient_in = Stream(gradient_hbm, gradient_ref, gradient_sems, 0, PAD)
    for index in range(frames // ROWS):
        gradient_in.tile(index).start()
        act_in.tile(index).start()
    out_ref[...] = jnp.zeros_like(out_ref)
    edge_rows(gradient_ref, edge_ref[0:1, :], edge_ref[1:2, :])
    gradient_in.tile(0).wait()

    def step(i, start):
        wait_next([gradient_in], i, frames)
        act_in.tile(i).wait()
        before, here, after = taps_of(gradient_ref, ends, start, base)
        act = act_ref[pl.ds(start + PAD, ROWS), :]
        for k, tap in enumerate((after, here, before)):
            out_ref[k * channels : (k + 1) * channels, :] += lax.dot_general(
                act, tap, (((0,), (0,)), ((), ())), preferred_element_type=F32
            )

    for_tiles(frames, step)
    write_halves(info_ref, 0, out_ref, keep_ref, give_ref)


def write_halves(info_ref, bit, total_ref, keep_ref, give_ref):
    half = keep_ref.shape[0]
    mine = info_ref[BITS_AT + bit]
    keep_ref[...] = total_ref[pl.ds(pl.multiple_of(mine * half, PAD), half), :]
    give_ref[...] = total_ref[pl.ds(pl.multiple_of((1 - mine) * half, PAD), half), :].astype(BF16)


def halves_kernel(bits, info_ref, *refs):
    count = len(bits)
    inputs, outputs, totals = refs[: 2 * count], refs[2 * count : 4 * count], refs[4 * count :]
    for k, bit in enumerate(bits):
        totals[k][...] = inputs[2 * k][...] + inputs[2 * k + 1][...].astype(F32)
        write_halves(info_ref, bit, totals[k], outputs[2 * k], outputs[2 * k + 1])


def join_kernel(bits, info_ref, *refs):
    count = len(bits)
    for k, bit in enumerate(bits):
        part_ref, other_ref, out_ref = refs[2 * k], refs[2 * k + 1], refs[2 * count + k]
        half = part_ref.shape[0]
        mine = info_ref[BITS_AT + bit]
        out_ref[pl.ds(pl.multiple_of(mine * half, PAD), half), :] = part_ref[...]
        out_ref[pl.ds(pl.multiple_of((1 - mine) * half, PAD), half), :] = other_ref[...]


def block_order(order):
    places = []
    for index in range(1 << (len(order) + 1)):
        source, joined = index & 1, 0
        for at, bit in enumerate(order):
            source = 2 * source + ((index >> bit) & 1)
            joined += ((index >> bit) & 1) << at
        places.append((index & 1, source, joined))
    return places


def final_kernel(
    orders,
    rows,
    info_ref,
    second_ref,
    second_other_ref,
    first_ref,
    first_other_ref,
    second_out_ref,
    first_out_ref,
    first_affine_ref,
    first_shift_ref,
    second_affine_ref,
    second_shift_ref,
    bias_ref,
):
    channels = second_ref.shape[1]
    mine = info_ref[BITS_AT]
    gathered = []
    pairs = (
        (second_ref, second_other_ref, second_out_ref, rows + SMALL_ROWS),
        (first_ref, first_other_ref, first_out_ref, rows),
    )
    for k, (part_ref, other_ref, out_ref, step) in enumerate(pairs):
        for core, source, joined in block_order(orders[k]):
            here = pl.ds(joined * step, step)
            block = jnp.where(
                mine == core, part_ref[here, :].astype(F32), other_ref[here, :].astype(F32)
            )
            out_ref[source * rows : (source + 1) * rows, :] = block[:rows]
            if k == 0:
                gathered.append(block[rows:])
    styles = jnp.concatenate([block[32:40, 0:128] for block in gathered], axis=0)
    for at, (affine_ref, shift_ref) in enumerate(
        ((first_affine_ref, first_shift_ref), (second_affine_ref, second_shift_ref))
    ):
        for side in range(2):
            first = 16 * at + 8 * side
            sums = jnp.concatenate([block[first : first + 8] for block in gathered], axis=0)
            lanes = slice(side * channels, (side + 1) * channels)
            affine_ref[:, lanes] = lax.dot_general(
                styles, sums, (((0,), (0,)), ((), ())), precision=PRECISE
            )
            shift_ref[:, lanes] = jnp.sum(sums, axis=0, keepdims=True)
    biases = jnp.concatenate([block[40:48] for block in gathered], axis=0)
    bias_ref[...] = jnp.sum(biases, axis=0, keepdims=True)


def back_coefficients(own_ref, other_refs, inverse_ref, coef_ref, back_ref, of_values):
    inverse = inverse_ref[...]
    rstd, mean_rstd, scale = coef_ref[0:8, :], coef_ref[8:16, :], coef_ref[16:24, :]
    total = sum_over_tm(own_ref, other_refs, 0, 8)
    cross = sum_over_tm(own_ref, other_refs, 8, 8)
    if of_values:
        cross = rstd * cross - mean_rstd * total
    back_ref[0:8, :] = total
    back_ref[8:16, :] = cross
    slant = scale * cross * inverse
    back_ref[16:24, :] = scale * total * inverse - (mean_rstd * slant if of_values else 0.0)
    back_ref[24:32, :] = rstd * slant if of_values else slant
    back_ref[32:40, :] = scale


def inward(inner, values, back_ref, u):
    return inner * row(back_ref, 32 + u) - row(back_ref, 16 + u) - values * row(back_ref, 24 + u)


def first_back_kernel(
    info_ref,
    inner_ref,
    middle_hbm,
    own_ref,
    one_ref,
    two_ref,
    three_ref,
    inverse_ref,
    coef_two_ref,
    coef_one_ref,
    unit_one_hbm,
    weight_ref,
    gradient_hbm,
    edge_ref,
    out_ref,
    back_ref,
    stat_ref,
    acc_ref,
    full_ref,
    middle_ref,
    unit_one_ref,
    gradient_ref,
    two_sems,
    one_sems,
    gradient_sems,
):
    frames, channels = unit_one_ref.shape
    early = [
        Stream(middle_hbm, middle_ref, two_sems),
    ]
    late = Stream(unit_one_hbm, unit_one_ref, one_sems)
    gradient_out = Stream(gradient_ref, gradient_hbm, gradient_sems, PAD)
    for index in range(frames // ROWS):
        for stream in (*early, late):
            stream.tile(index).start()
    ends = read_ends(info_ref)
    base = info_ref[8]
    back_coefficients(own_ref, (one_ref, two_ref, three_ref), inverse_ref, coef_two_ref, back_ref, True)
    acc_ref[...] = jnp.zeros_like(acc_ref)
    owner_before, owner_after = halo_owner(info_ref, ends, base, frames)
    edge_rows(
        gradient_ref,
        inward(
            row(one_ref, LAST_ROW),
            row(coef_two_ref, 56),
            back_ref,
            owner_before,
        ),
        inward(
            row(three_ref, FIRST_ROW),
            row(coef_two_ref, 57),
            back_ref,
            owner_after,
        ),
    )

    def back_step(start):
        here = pl.ds(start, BLOCK)
        there = pl.ds(start + PAD, BLOCK)

        def now(u):
            return inward(
                inner_ref[here, :].astype(F32), middle_ref[here, :], back_ref, u
            )

        def uniform(u):
            gradient_ref[there, :] = now(u).astype(BF16)

        def mixed(u, mask):
            old = gradient_ref[there, :].astype(F32)
            gradient_ref[there, :] = jnp.where(mask((BLOCK, channels)), now(u), old).astype(BF16)

        by_utterance(ends, base + start, BLOCK, uniform, mixed)

    edge_ref[0:8, :] = gradient_ref[0:PAD, :].astype(F32)[0:8]
    edge_ref[1:2, :] = gradient_ref[PAD + frames :, :].astype(F32)[0:1]

    def back_tile(i):
        for stream in early:
            stream.tile(i).wait()
        for_blocks(pl.multiple_of(i * ROWS, ROWS), ROWS, BLOCK, back_step)
        gradient_out.tile(i).start()

    back_tile(0)

    def slope_step(start, row_start):
        here = pl.ds(start, BLOCK)

        def parts(u):
            unit = unit_one_ref[here, :].astype(F32)
            _, inner, cross = slope_and_sums(
                full_ref[pl.ds(row_start, BLOCK), :], unit, coef_one_ref, u, HALF_OF_UNIT
            )
            return inner, cross

        def uniform(u):
            inner, cross = parts(u)
            out_ref[here, :] = inner.astype(BF16)
            add_stats(acc_ref, u, inner, cross)

        def mixed(u, mask):
            keep = mask((BLOCK, channels))
            inner, cross = parts(u)
            old = out_ref[here, :].astype(F32)
            out_ref[here, :] = jnp.where(keep, inner, old).astype(BF16)
            add_stats(acc_ref, u, jnp.where(keep, inner, 0.0), jnp.where(keep, cross, 0.0))

        by_utterance(ends, base + start, BLOCK, uniform, mixed)

    def conv(i, start):
        @pl.when(i + 1 < frames // ROWS)
        def _():
            back_tile(i + 1)

        late.tile(i).wait()
        before, here, after = taps_of(gradient_ref, ends, start, base)
        full_ref[...] = convolved_back((after, here, before), weight_ref)
        for_blocks(0, ROWS, BLOCK, lambda inside: slope_step(start + inside, inside))

    for_tiles(frames, conv)
    finish_stats(acc_ref, stat_ref)
    gradient_out.finish()


def buffer_gradient_kernel(
    info_ref,
    offset_ref,
    inner_ref,
    unit_hbm,
    cot_hbm,
    wide_hbm,
    own_ref,
    one_ref,
    two_ref,
    three_ref,
    inverse_ref,
    coef_ref,
    before_ref,
    out_ref,
    after_ref,
    back_ref,
    up_ref,
    total_ref,
    unit_ref,
    cot_ref,
    wide_ref,
    unit_sems,
    cot_sems,
    wide_sems,
):
    frames, channels = unit_ref.shape
    streams = [
        Stream(unit_hbm, unit_ref, unit_sems),
        Stream(cot_hbm, cot_ref, cot_sems),
        Stream(wide_hbm, wide_ref, wide_sems),
    ]
    for index in range(frames // ROWS):
        for stream in streams:
            stream.tile(index).start()
    tiles = offset_ref.shape[0]
    rows = frames // tiles
    halo, own = before_ref.shape[0], out_ref.shape[0]
    ends = read_ends(info_ref)
    base, slot_base = info_ref[8], info_ref[9]
    back_coefficients(
        own_ref, (one_ref, two_ref, three_ref), inverse_ref, coef_ref, back_ref, False
    )
    total_ref[...] = jnp.zeros_like(total_ref)
    span = rows + PAD

    def up_step(start):
        here = pl.ds(start, BLOCK)

        def upward(u):
            lead = cot_ref[here, :].astype(F32) * ROOT_HALF
            return lead + inward(
                inner_ref[here, :].astype(F32), unit_ref[here, :].astype(F32), back_ref, u
            )

        def uniform(u):
            up_ref[here, :] = upward(u).astype(BF16)

        def mixed(u, mask):
            old = up_ref[here, :].astype(F32)
            up_ref[here, :] = jnp.where(mask((BLOCK, channels)), upward(u), old).astype(BF16)

        by_utterance(ends, base + start, BLOCK, uniform, mixed)

    def step(i):
        start = pl.multiple_of(i * rows, rows)
        here = pl.ds(start, rows)
        shift = offset_ref[i] - slot_base
        aligned = pl.multiple_of((shift // PAD) * PAD, PAD)
        part = lax.dot_general(
            wide_ref[here, :], up_ref[here, :], (((0,), (0,)), ((), ())), preferred_element_type=F32
        )
        total_ref[pl.ds(aligned, span), :] += part[0:span]

    def blocks(i, start):
        for stream in streams:
            stream.tile(i).wait()
        for_blocks(start, ROWS, BLOCK, up_step)
        each = ROWS // rows

        def four(k, carry):
            for n in range(4):
                step(i * each + k * 4 + n)
            return carry

        lax.fori_loop(0, each // 4, four, 0)

    for_tiles(frames, blocks)
    before_ref[...] = total_ref[0:halo, :].astype(BF16)
    out_ref[...] = total_ref[halo : halo + own, :]
    after_ref[...] = total_ref[halo + own : 2 * halo + own, :].astype(BF16)


def scatter_kernel(places, copies, info_ref, order_ref, *refs):
    parts, out_ref, tmp_ref = refs[: len(places)], refs[-2], refs[-1]
    groups, piece, channels = parts[0].shape
    lanes = channels // 128
    me = info_ref[10]
    for old_ref in refs[len(places) : -2]:

        def copy(start, old_ref=old_ref):
            out_ref[pl.ds(start, ROWS), :] = old_ref[pl.ds(start, ROWS), :]

        for_blocks(0, out_ref.shape[0], ROWS, copy)
    for back, part_ref in zip(places, parts):
        source = lax.rem(me + copies - back, copies)

        def body(g, carry, part_ref=part_ref, source=source):
            for b in range(piece // 16):
                both = part_ref[g, b * 16 : b * 16 + 16, :].astype(F32)
                for h in range(2):
                    for q in range(lanes):
                        tmp_ref[pl.ds(((2 * b + h) * lanes + q) * 8, 8), :] = both[
                            8 * h : 8 * h + 8, q * 128 : (q + 1) * 128
                        ]
            first = (g * copies + source) * piece
            for r in range(piece):
                out_ref[pl.ds(order_ref[first + r], lanes, stride=8), :] = tmp_ref[
                    pl.ds((r // 8) * 8 * lanes + r % 8, lanes, stride=8), :
                ]
            return carry

        lax.fori_loop(0, groups, body, 0)


VM = pl.BlockSpec(memory_space=pltpu.VMEM)
SM = pl.BlockSpec(memory_space=pltpu.SMEM)


HB = pl.BlockSpec(memory_space=pltpu.HBM)


def call(kernel, inputs, outputs, scratch, flops, limit):
    return pl.pallas_call(
        kernel,
        in_specs=[spec for _, spec in inputs],
        out_specs=tuple(spec for _, _, spec in outputs),
        out_shape=tuple(
            pltpu.HBM(shape, dtype) if spec is HB else jax.ShapeDtypeStruct(shape, dtype)
            for shape, dtype, spec in outputs
        ),
        scratch_shapes=[
            pltpu.SemaphoreType.DMA((one,)) if isinstance(one, int) else pltpu.VMEM(*one)
            for one in scratch
        ],
        compiler_params=pltpu.CompilerParams(vmem_limit_bytes=limit * MIB),
        cost_estimate=pl.CostEstimate(flops=flops, bytes_accessed=flops // 200, transcendentals=0),
    )(
        *(
            pltpu.with_memory_space_constraint(array, pltpu.HBM) if spec is HB else array
            for array, spec in inputs
        )
    )


def scattered(old, parts, places, copies, info, order):
    piece, channels = parts[0].shape[1:]
    lanes = channels // 128
    kept = [] if old is None else [old]
    return pl.pallas_call(
        functools.partial(scatter_kernel, places, copies),
        in_specs=[SM, SM] + [VM] * (len(parts) + len(kept)),
        out_specs=VM,
        out_shape=(pltpu.VMEM if old is None else jax.ShapeDtypeStruct)(
            (order.shape[0] * lanes, 128), F32
        ),
        scratch_shapes=[pltpu.VMEM((piece * lanes, 128), F32)],
        input_output_aliases={2 + len(parts): 0} if kept else {},
        compiler_params=pltpu.CompilerParams(vmem_limit_bytes=22 * MIB),
        cost_estimate=pl.CostEstimate(flops=10**6, bytes_accessed=10**4, transcendentals=0),
    )(info, order, *parts, *kept)


def shifted(values, axis, step):
    devices = lax.axis_size(axis)
    return lax.ppermute(values, axis, [(i, (i + step) % devices) for i in range(devices)])


def others_over_tm(values):
    return [shifted(values, "tm", d) for d in (1, 2, 3)]


def from_neighbours(first_rows, last_rows):
    devices = lax.axis_size("tm")
    up = [(i, i + 1) for i in range(devices - 1)]
    down = [(i + 1, i) for i in range(devices - 1)]
    return lax.ppermute(last_rows, "tm", up), lax.ppermute(first_rows, "tm", down)


def swapped(values, bit):
    devices = lax.axis_size("seq")
    return lax.ppermute(values, "seq", [(i, i ^ (1 << bit)) for i in range(devices)])


def after(values, *others):
    return lax.optimization_barrier((values, others))[0]


def summed_over_tm(parts):
    copies, tm_index = lax.axis_size("tm"), lax.axis_index("tm")
    rows, channels = parts[0].shape
    pieces = jnp.stack(parts).reshape(len(parts), copies, rows // copies, channels)
    part = lax.dynamic_index_in_dim(pieces, tm_index, 1, False)
    sent = pieces.astype(BF16)
    for step in (1, 3, 2):
        give = lax.dynamic_index_in_dim(sent, (tm_index + step) % copies, 1, False)
        part = part + shifted(give, "tm", step).astype(F32)
    return part.astype(BF16)


def gathered_over_tm(part):
    copies, tm_index = lax.axis_size("tm"), lax.axis_index("tm")
    count, rows, channels = part.shape
    every = jnp.zeros((count, copies, rows, channels), BF16)
    every = lax.dynamic_update_index_in_dim(every, part, tm_index, 1)
    for step in (1, 3, 2):
        every = lax.dynamic_update_index_in_dim(
            every, shifted(part, "tm", step), (tm_index - step) % copies, 1
        )
    return every.reshape(count, copies * rows, channels)


def on_device(
    phonemes,
    send_order,
    phoneme_counts,
    frame_lengths,
    tile_offsets,
    alignment,
    style_vec,
    first_affine_weight,
    first_affine_bias,
    first_conv_weight,
    second_affine_weight,
    second_affine_bias,
    second_conv_weight,
    second_conv_bias,
    cotangent,
):
    frames, channels = cotangent.shape
    slot_count = phonemes.shape[0]
    groups = lax.axis_size("seq")
    copies = lax.axis_size("tm")
    seq_index, tm_index = lax.axis_index("seq"), lax.axis_index("tm")
    piece_rows = slot_count // groups // copies
    local_rows = slot_count // copies
    tiles = tile_offsets.shape[0]
    window = alignment.shape[1]
    halo = window // 2
    lengths = frame_lengths[0]
    conv_flops = 2 * frames * 3 * channels * channels

    info = jnp.concatenate(
        [
            jnp.cumsum(lengths),
            jnp.cumsum(phoneme_counts[0]),
            (tm_index * frames)[None],
            (tm_index * local_rows - halo)[None],
            tm_index[None],
            (seq_index < groups // 2)[None].astype(I32),
            (seq_index[None] >> jnp.arange(12, dtype=I32)) & 1,
        ]
    ).astype(I32)
    inverse = jnp.zeros((8, channels), F32).at[0:UTTS].set(
        jnp.broadcast_to(1.0 / lengths.astype(F32)[:, None], (UTTS, channels))
    )
    style_rows = jnp.zeros((8, style_vec.shape[1]), BF16).at[0:UTTS].set(style_vec)
    params_one = jnp.dot(style_rows, first_affine_weight, preferred_element_type=F32) + (
        first_affine_bias.astype(F32)
    )
    params_two = jnp.dot(style_rows, second_affine_weight, preferred_element_type=F32) + (
        second_affine_bias.astype(F32)
    )

    def turned(weight):
        return (
            weight.reshape(3, channels, channels).transpose(0, 2, 1).reshape(3 * channels, channels)
        )

    tiles_of = frames // ROWS
    full, padded = (frames, channels), (frames + 2 * PAD, channels)
    stats_shape, coef_shape = (STAT_ROWS, channels), (64, channels)
    small_acc = ((ACC_ROWS, channels), F32)

    order = send_order[0].reshape(groups, copies, piece_rows)
    extra = min(halo, piece_rows)
    from_first = seq_index < groups // 2
    mine = lax.dynamic_index_in_dim(order, tm_index, 1, False)
    following = lax.dynamic_index_in_dim(order, jnp.minimum(tm_index + 1, copies - 1), 1, False)
    leading = lax.dynamic_index_in_dim(order, jnp.maximum(tm_index - 1, 0), 1, False)
    beside = jnp.where(from_first, following[:, :extra], leading[:, piece_rows - extra :])
    mine = jnp.concatenate([mine, beside], axis=1)
    outgoing = jnp.take(phonemes, mine.reshape(-1), axis=0, mode="clip")
    received = lax.all_to_all(
        outgoing.reshape(groups, piece_rows + extra, channels), "seq", 0, 0, tiled=True
    )

    second_turned = turned(second_conv_weight)
    grad_act_two, grad_branch, bias_part = call(
        gradient_kernel,
        (
            (info, SM),
            (cotangent, HB),
            (second_turned, VM),
        ),
        ((full, BF16, HB), (full, BF16, HB), ((16, channels), F32, VM)),
        [(full, BF16), (padded, BF16), (full, BF16), tiles_of, tiles_of, tiles_of],
        conv_flops,
        32,
    )

    received, bias_part = lax.optimization_barrier((received, bias_part))
    upsampled, upsampled_far, wide, stat = call(
        upsample_kernel,
        (
            (info, SM),
            (tile_offsets, SM),
            (received, VM),
            (alignment, HB),
            (bias_part, VM),
        ),
        (
            (full, F32, VM),
            (full, F32, HB),
            ((frames, WIDE), BF16, HB),
            (stats_shape, F32, VM),
        ),
        [
            ((local_rows + WIDE, channels), BF16),
            small_acc,
            ((frames, window), BF16),
            ((frames, WIDE), BF16),
            tiles_of,
            tiles_of,
            tiles_of,
        ],
        2 * frames * WIDE * channels,
        20,
    )
    others = others_over_tm(stat)
    bias_total = (stat[EXTRA_ROW] + others[1][EXTRA_ROW]) + (
        others[0][EXTRA_ROW] + others[2][EXTRA_ROW]
    )

    act_one, middle, middle_far, unit_one, coef_one, stat_two, grad_edges, added = call(
        first_conv_kernel,
        (
            (info, SM),
            (upsampled, VM),
            *((one, VM) for one in (stat, *others)),
            (inverse, VM),
            (params_one, VM),
            (first_conv_weight, VM),
            (second_turned, VM),
        ),
        (
            (padded, BF16, HB),
            (full, F32, VM),
            (full, F32, HB),
            (full, BF16, HB),
            (coef_shape, F32, VM),
            (stats_shape, F32, VM),
            ((8, channels), F32, VM),
            ((8, channels), F32, VM),
        ),
        [small_acc, (padded, BF16), (full, BF16), tiles_of, 2, tiles_of, tiles_of],
        conv_flops,
        28,
    )
    others_two = others_over_tm(stat_two)

    act_two, inner_two, coef_two, stat_three = call(
        second_norm_kernel,
        (
            (info, SM),
            (grad_act_two, HB),
            (middle, VM),
            *((one, VM) for one in (stat_two, *others_two)),
            (inverse, VM),
            (params_two, VM),
            (added, VM),
        ),
        (
            (padded, BF16, HB),
            (full, BF16, VM),
            (coef_shape, F32, VM),
            (stats_shape, F32, VM),
        ),
        [
            small_acc,
            (full, BF16),
            (padded, BF16),
            tiles_of,
            tiles_of,
            2,
        ],
        2 * frames * channels * 100,
        28,
    )
    others_three = others_over_tm(stat_three)
    grad_middle, middle_edges, inner_one, back_two, stat_four = call(
        first_back_kernel,
        (
            (info, SM),
            (inner_two, VM),
            (middle_far, HB),
            *((one, VM) for one in (stat_three, *others_three)),
            (inverse, VM),
            (coef_two, VM),
            (coef_one, VM),
            (unit_one, HB),
            (first_conv_weight, VM),
        ),
        (
            (full, BF16, HB),
            ((8, channels), F32, VM),
            (full, BF16, VM),
            ((40, channels), F32, VM),
            (stats_shape, F32, VM),
        ),
        [
            small_acc,
            ((ROWS, channels), F32),
            (full, F32),
            (full, BF16),
            (padded, BF16),
            *([tiles_of] * 3),
        ],
        conv_flops,
        40,
    )
    others_four = others_over_tm(stat_four)
    grad_before, grad_own, grad_after, back_one = call(
        buffer_gradient_kernel,
        (
            (info, SM),
            (tile_offsets, SM),
            (inner_one, VM),
            (unit_one, HB),
            (cotangent, HB),
            (wide, HB),
            *((one, VM) for one in (stat_four, *others_four)),
            (inverse, VM),
            (coef_one, VM),
        ),
        (
            ((halo, channels), BF16, VM),
            ((local_rows, channels), F32, VM),
            ((halo, channels), BF16, VM),
            ((40, channels), F32, VM),
        ),
        [
            (full, BF16),
            ((local_rows + WIDE, channels), F32),
            *([(full, BF16)] * 2),
            ((frames, WIDE), BF16),
            *([tiles_of] * 3),
        ],
        2 * frames * WIDE * channels,
        36,
    )

    row_places = (send_order[0] >> 3) * (8 * (channels // 128)) + (send_order[0] & 7)
    from_before, from_after = from_neighbours(grad_before, grad_after)
    return_rows = jnp.concatenate(
        [grad_own[:halo] + from_before, grad_own[halo:-halo], grad_own[-halo:] + from_after]
    ).astype(BF16)
    returned = lax.all_to_all(
        return_rows.reshape(groups, piece_rows, channels), "seq", 0, 0, tiled=True
    )

    bits = [b for b in range(12) if (1 << b) < groups]
    orders = (bits[1:], bits[1:][::-1])
    second_keep, second_give = call(
        weight_gradient_kernel,
        ((info, SM), (after(act_two, back_one), HB), (grad_branch, HB), (grad_edges, VM)),
        (((3 * channels // 2, channels), F32, VM), ((3 * channels // 2, channels), BF16, VM)),
        [((3 * channels, channels), F32), (padded, BF16), (padded, BF16), tiles_of, tiles_of],
        10**6,
        24,
    )

    returned, second_keep, second_give = lax.optimization_barrier(
        (returned, second_keep, second_give)
    )
    rounds = [returned, shifted(returned, "tm", 1)]
    first_keep, first_give = call(
        weight_gradient_kernel,
        ((info, SM), (act_one, HB), (after(grad_middle, returned), HB), (middle_edges, VM)),
        (((3 * channels // 2, channels), F32, VM), ((3 * channels // 2, channels), BF16, VM)),
        [((3 * channels, channels), F32), (padded, BF16), (padded, BF16), tiles_of, tiles_of],
        10**6,
        24,
    )

    keeps, gives = [second_keep, first_keep], [second_give, first_give]
    gots = [swapped(give, bits[0]) for give in gives]
    for turn, pair in enumerate(zip(*orders)):
        count = keeps[0].shape[0] // 2
        out = call(
            functools.partial(halves_kernel, pair),
            ((info, SM), *((one, VM) for both in zip(keeps, gots) for one in both)),
            (((count, channels), F32, VM), ((count, channels), BF16, VM)) * 2,
            [((2 * count, channels), F32)] * 2,
            10**6,
            16,
        )
        keeps, gives = [out[0], out[2]], [out[1], out[3]]
        if turn == 0:
            rounds[1], keeps, gives = lax.optimization_barrier((rounds[1], keeps, gives))
            rounds.append(shifted(rounds[1], "tm", 1))
        gots = [swapped(give, bit) for give, bit in zip(gives, pair)]
    row_sums = [keep + got.astype(F32) for keep, got in zip(keeps, gots)]
    placed = scattered(None, rounds[:2], (0, 1), copies, info, row_places)
    rounds[2], row_sums, placed = lax.optimization_barrier((rounds[2], row_sums, placed))
    sums = gathered_over_tm(summed_over_tm(row_sums))
    rounds[2], sums = lax.optimization_barrier((rounds[2], sums))
    rounds.append(shifted(rounds[2], "tm", 1))

    act_two, _ = lax.optimization_barrier((act_two, sums))
    (frames_out,) = call(
        second_conv_kernel,
        (
            (info, SM),
            (act_two, HB),
            (upsampled_far, HB),
            (second_conv_weight, VM),
            (second_conv_bias[None], VM),
        ),
        ((full, BF16, HB),),
        [(padded, BF16), (full, F32), (full, BF16), tiles_of, 2, tiles_of, tiles_of],
        10**6,
        36,
    )


    params_grad = [
        jnp.concatenate([back[8 : 8 + UTTS], back[0:UTTS]], axis=1) for back in (back_one, back_two)
    ]
    style_grad = jnp.dot(
        params_grad[0], first_affine_weight.astype(F32).T, precision=PRECISE
    ) + jnp.dot(params_grad[1], second_affine_weight.astype(F32).T, precision=PRECISE)
    style_block = jnp.zeros((8, channels), BF16).at[:, : style_rows.shape[1]].set(style_rows)
    small = jnp.concatenate(
        [
            back_one[8:16].astype(BF16),
            back_one[0:8].astype(BF16),
            back_two[8:16].astype(BF16),
            back_two[0:8].astype(BF16),
            style_block,
            jnp.zeros((8, channels), BF16).at[0].set(bias_total.astype(BF16)),
        ]
    )
    rows = sums.shape[1]
    held = [jnp.concatenate([sums[0], small]), sums[1]]
    for pair in zip(*orders):
        others = [swapped(one, bit) for one, bit in zip(held, pair)]
        held = call(
            functools.partial(join_kernel, pair),
            ((info, SM), *((one, VM) for both in zip(held, others) for one in both)),
            tuple(((2 * one.shape[0], channels), BF16, VM) for one in held),
            [],
            10**6,
            16,
        )
    rounds[3], held, frames_out = lax.optimization_barrier((rounds[3], list(held), frames_out))
    others = [swapped(one, bits[0]) for one in held]
    (
        second_conv_grad,
        first_conv_grad,
        first_affine_grad,
        first_shift_grad,
        second_affine_grad,
        second_shift_grad,
        second_bias_grad,
    ) = call(
        functools.partial(final_kernel, orders, rows),
        (
            (info, SM),
            (held[0], VM),
            (others[0], VM),
            (held[1], VM),
            (others[1], VM),
        ),
        (
            ((3 * channels, channels), F32, VM),
            ((3 * channels, channels), F32, VM),
            *(
                (((style_vec.shape[1], 2 * channels), F32, VM), ((1, 2 * channels), F32, VM)) * 2
            ),
            ((1, channels), F32, VM),
        ),
        [],
        10**6,
        28,
    )
    placed = scattered(placed, rounds[2:], (2, 3), copies, info, row_places)
    lanes = channels // 128
    phonemes_grad = (
        placed.reshape(slot_count // 8, lanes, 8, 128)
        .transpose(0, 2, 1, 3)
        .reshape(slot_count, channels)
    )
    return (
        frames_out,
        phonemes_grad,
        style_grad,
        first_affine_grad,
        first_shift_grad[0],
        first_conv_grad,
        second_affine_grad,
        second_shift_grad[0],
        second_conv_grad,
        second_bias_grad[0],
    )


def solution(mesh):
    split, whole = ("seq", "tm"), P()
    in_specs = (
        P("seq", None),
        P("seq", None),
        P("seq", None),
        P("seq", None),
        P(split),
        P(split, None),
        P("seq", None),
        *([whole] * 7),
        P(split, None),
    )
    out_specs = (P(split, None), P("seq", None), P("seq", None), *([whole] * 7))
    return jax.shard_map(
        on_device, mesh=mesh, in_specs=in_specs, out_specs=out_specs, check_vma=False
    )
```
